128 devices in a mesh: ctx: 8 (over x, core), tp: 16 (over z, y).
Axes of the slice: x: 4, y: 4, z: 4, core: 2. Of those that a mesh axis runs over, the one named last changes fastest.
Arguments:
- tokens: bfloat16 [8192, 4096], P('ctx', 'tp')
- modality: int32 [8192], P('ctx'), may hold values from 0 to 2, as said below
- w_query: bfloat16 [3, 4096, 4096], P(None, None, 'tp')
- w_key: bfloat16 [3, 4096, 4096], P(None, None, 'tp'), may hold values from -0.09375 to 0.09375
- w_value: bfloat16 [3, 4096, 4096], P(None, None, 'tp'), may hold values from -0.09375 to 0.09375
- w_out: bfloat16 [3, 4096, 4096], P(None, 'tp'), may hold values from -0.5 to 0.5
Outputs:
- mixed: bfloat16 [8192, 4096], P('ctx', 'tp')
The draws below stay inside these ranges and needn't reach their ends.
Inputs may be any that keep to these rules, and one draw needn't show every extreme that they name: In each aligned block of 1024 tokens (one index of ctx) the tokens of each modality form one contiguous run of at most 512 tokens; in every draw some block has a modality with exactly 512 tokens.
All inputs are finite; a program needn't handle non-finite values.
Results may differ from the reference program's by a relative error of at most 0.013.
Values may be sent and summed in bfloat16 or wider, within the bound.
No kernel may reach another device: no remote copies, remote signals or barrier semaphores. Data moves between devices by JAX's collectives and lax.ppermute only.
A program may use at most 128 MiB of HBM per device.

```python
import math
import jax
import jax.numpy as jnp
from jax import lax

D = 4096
HEADS = 32
HD = 128
MODALITIES = 3
TOK_DEV = 1024
CAP = 512
TOKENS = 8192
N_TP = 16


def draw_tokens(key, part):
    key = jax.random.fold_in(key, 11)
    base_key, row_key, column_key = jax.random.split(key, 3)
    base = jax.random.normal(base_key, (TOKENS, D), jnp.float32)
    spread = math.log(10.0)
    row_scale = jnp.exp(jax.random.uniform(row_key, (TOKENS, 1), jnp.float32, 0.0, spread))
    column_scale = jnp.exp(jax.random.uniform(column_key, (1, D), jnp.float32, 0.0, spread))
    return (base * row_scale * column_scale / 4.0).astype(jnp.bfloat16)


def draw_modality(key, part):
    key = jax.random.fold_in(key, 12)
    first_key, pick_key, second_key, order_key = jax.random.split(key, 4)
    blocks = TOKENS // TOK_DEV
    first_count = jax.random.randint(first_key, (blocks,), 0, CAP + 1)
    chosen = jax.random.randint(pick_key, (), 0, blocks)
    first_count = jnp.where(jnp.arange(blocks) == chosen, CAP, first_count).astype(jnp.int32)
    lowest = jnp.maximum(0, TOK_DEV - CAP - first_count)
    highest = jnp.minimum(CAP, TOK_DEV - first_count)
    second_count = jax.random.randint(second_key, (blocks,), lowest, highest + 1).astype(jnp.int32)
    ranks = jax.random.randint(order_key, (blocks, MODALITIES), 0, 1 << 20) * 4 + jnp.arange(MODALITIES)
    order = jnp.argsort(ranks, axis=1).astype(jnp.int32)
    positions = jnp.arange(TOK_DEV, dtype=jnp.int32)[None, :]
    slot_index = (positions >= first_count[:, None]).astype(jnp.int32) + (positions >= (first_count + second_count)[:, None]).astype(jnp.int32)
    return jnp.take_along_axis(order, slot_index, axis=1).reshape(TOKENS).astype(jnp.int32)


def draw_w_query(key, part):
    key = jax.random.fold_in(key, 13)
    base_key, head_key, channel_key = jax.random.split(key, 3)
    base = jax.random.normal(base_key, (MODALITIES, D, D), jnp.float32) / math.sqrt(D)
    head_scale = jnp.exp(jax.random.uniform(head_key, (MODALITIES, 1, HEADS, 1), jnp.float32, math.log(0.7), math.log(3.0)))
    channel_scale = jnp.exp(jax.random.uniform(channel_key, (MODALITIES, 1, HEADS, HD), jnp.float32, math.log(0.6), math.log(1.6)))
    scales = (head_scale * channel_scale).reshape(MODALITIES, 1, D)
    return (base * scales).astype(jnp.bfloat16)


def raised(array, stream_key, source, target, shards_of, factor):
    owner, partner = [(jnp.arange(array.shape[position]) // (array.shape[position] // shards_of)).reshape([-1 if axis == position else 1 for axis in range(array.ndim)]) for position in (source, target)]
    chosen = jax.random.permutation(stream_key, shards_of)[partner]
    strong = (owner == chosen) | (owner == (partner + shards_of // 2) % shards_of)
    return jnp.where(strong, factor * array, array)


def steps_of(key, extent, pieces, low, high):
    factor_of, own = 1.0, jax.random.fold_in(key, 6)
    for axis_at, shards_of in pieces:
        draws = jnp.exp(jax.random.uniform(jax.random.fold_in(own, axis_at), (shards_of,), jnp.float32, low / len(pieces), high / len(pieces)))
        factor_of = factor_of * jnp.repeat(draws, extent[axis_at] // shards_of).reshape([-1 if axis == axis_at else 1 for axis in range(len(extent))])
    return factor_of


def gaussian(own_key, shape, width, most, shards=(), kind=jnp.bfloat16):
    drawn = width * jax.random.normal(own_key, shape, jnp.float32)
    if shards:
        drawn = drawn * steps_of(own_key, shape, shards, -0.22, 0.18)
    return jnp.clip(drawn, -most, most).astype(kind)


def gaussian_with(key, shape, scale, reach, pieces, heavy, kind=jnp.bfloat16):
    result = scale * jax.random.normal(key, shape, jnp.float32)
    if pieces:
        result = result * steps_of(key, shape, pieces, -0.22, 0.18)
    return jnp.clip(raised(result, jax.random.fold_in(key, 3), *heavy), -reach, reach).astype(kind)


def setup_inputs(seed: int = 0) -> dict:
    streams_of = jax.random.split(jax.random.key(seed), 7)
    tokens = draw_tokens(jax.random.fold_in(streams_of[6], 71), 0)
    modality = draw_modality(jax.random.fold_in(streams_of[6], 71), 0)
    w_query = draw_w_query(jax.random.fold_in(streams_of[6], 71), 0)
    w_key = gaussian(streams_of[3], (MODALITIES, D, D), D ** -0.5, 0.09375, ((2, 16),))
    w_value = gaussian(streams_of[4], (MODALITIES, D, D), D ** -0.5, 0.09375, ((2, 16),))
    w_out = gaussian_with(streams_of[5], (MODALITIES, D, D), (D // 16) ** -0.5, 0.5, ((1, 16),), (1, 2, 16, 2.0))
    return dict(tokens=tokens, modality=modality, w_query=w_query, w_key=w_key, w_value=w_value, w_out=w_out)


def modal_product(inputs, stacked, modality):
    row_count = inputs.shape[0]
    positions = jnp.arange(row_count, dtype=jnp.int32)
    results = [jnp.zeros((row_count, weight.shape[2]), jnp.float32) for weight in stacked]
    for modal_index in range(MODALITIES):
        member = modality == modal_index
        first_row = jnp.min(jnp.where(member, positions, row_count))
        begin_row = jnp.clip(first_row, 0, row_count - CAP).astype(jnp.int32)
        window = lax.dynamic_slice_in_dim(inputs, begin_row, CAP, 0)
        keep_rows = lax.dynamic_slice_in_dim(member, begin_row, CAP, 0)[:, None]
        for weight_index in range(len(stacked)):
            product = jnp.dot(window, stacked[weight_index][modal_index], preferred_element_type=jnp.float32)
            former = lax.dynamic_slice_in_dim(results[weight_index], begin_row, CAP, 0)
            results[weight_index] = lax.dynamic_update_slice_in_dim(results[weight_index], jnp.where(keep_rows, product, former), begin_row, 0)
    return results

def reference(tokens, modality, w_query, w_key, w_value, w_out):
    blocks = TOKENS // TOK_DEV
    widened = tokens.astype(jnp.float32)
    normed = (widened * lax.rsqrt(lax.optimization_barrier(jnp.mean(widened * widened, axis=-1, keepdims=True)) + 1e-05)).astype(jnp.bfloat16)
    modal_blocks = modality.reshape(blocks, TOK_DEV)

    def project(paired):
        block_rows, modal_rows = paired
        parts = modal_product(block_rows, [w_query, w_key, w_value], modal_rows)
        return tuple((single.astype(jnp.bfloat16) for single in parts))
    queries, key_rows, value_rows = lax.map(project, (normed.reshape(blocks, TOK_DEV, D), modal_blocks))
    queries = queries.reshape(TOKENS, HEADS, HD)
    keys_all = key_rows.reshape(TOKENS, HEADS, HD)
    values_all = value_rows.reshape(TOKENS, HEADS, HD)
    score_scale = 1.0 / math.sqrt(HD)
    span_rows = 512 if TOKENS % 512 == 0 else TOKENS
    key_positions = jnp.arange(TOKENS, dtype=jnp.int32)

    def attend(offset):
        query_part = lax.dynamic_slice_in_dim(queries, offset, span_rows, 0)
        scores = jnp.einsum('qhd,khd->hqk', query_part, keys_all, preferred_element_type=jnp.float32) * score_scale
        query_pos = offset + jnp.arange(span_rows, dtype=jnp.int32)
        allowed = key_positions[None, :] <= query_pos[:, None]
        scores = jnp.where(allowed[None], scores, -1e+30)
        row_top = lax.optimization_barrier(jnp.max(scores, axis=-1))
        weights = jnp.where(allowed[None], jnp.exp(scores - row_top[..., None]), 0.0)
        row_total = lax.optimization_barrier(jnp.sum(weights, axis=-1))
        mixture = jnp.einsum('hqk,khd->qhd', weights.astype(jnp.bfloat16), values_all, preferred_element_type=jnp.float32) / jnp.transpose(row_total)[:, :, None]
        return mixture.reshape(span_rows, D).astype(jnp.bfloat16)
    starts = jnp.arange(TOKENS // span_rows, dtype=jnp.int32) * span_rows
    attended = lax.map(attend, starts).reshape(TOKENS, D)
    group_width = D // N_TP

    def output_block(paired):
        block_rows, modal_rows = paired
        summed = jnp.zeros((TOK_DEV, D), jnp.float32)
        for group in range(N_TP):
            rows_part = block_rows[:, group * group_width:(group + 1) * group_width]
            weight_part = w_out[:, group * group_width:(group + 1) * group_width, :]
            partial_term = modal_product(rows_part, [weight_part], modal_rows)[0].astype(jnp.bfloat16)
            summed = summed + lax.optimization_barrier(partial_term).astype(jnp.float32)
        return summed
    branch = lax.map(output_block, (attended.reshape(blocks, TOK_DEV, D), modal_blocks)).reshape(TOKENS, D)
    return (widened + branch).astype(jnp.bfloat16)
```

```python
import functools
import math

import jax
import jax.numpy as jnp
import numpy as np
from jax import lax
from jax.experimental import pallas as pl
from jax.experimental.pallas import tpu as pltpu
from jax.sharding import PartitionSpec as P

HD = 128
MODALITIES = 3
EPS = 1e-05
ROW_TILE = 256
Q_TILE = 512
K_TILE = 512
AXES = ("ctx", "tp")
BF = jnp.bfloat16
F32 = jnp.float32
OFFSETS = np.array([0, 3, 1, 2])
VMEM_BYTES = 48 * 1024 * 1024


def plane_perm(first, step):
    pairs = []
    for ctx in range(8):
        for z in range(4):
            for y in range(4):
                along_y = (ctx % 2 == 0) == first
                to_z = z if along_y else (z + step) % 4
                to_y = (y + step) % 4 if along_y else y
                pairs.append((ctx * 16 + z * 4 + y, ctx * 16 + to_z * 4 + to_y))
    return pairs


def move(array, first, step):
    return lax.ppermute(array, AXES, plane_perm(first, step))


def move_x(array, step):
    pairs = [(x * 2 + c, ((x + step) % 4) * 2 + c) for x in range(4) for c in range(2)]
    return lax.ppermute(array, "ctx", pairs)


def swap_core(array):
    return lax.ppermute(array, "ctx", [(i, i ^ 1) for i in range(8)])


def shard_table(first_offsets, second_offsets):
    core = lax.axis_index("ctx") % 2
    tp = lax.axis_index("tp")
    z, y = tp // 4, tp % 4
    first_offsets = jnp.asarray(first_offsets, jnp.int32)
    second_offsets = jnp.asarray(second_offsets, jnp.int32)
    first = (jnp.where(core == 0, y, z) + first_offsets) % 4
    second = (jnp.where(core == 0, z, y) + second_offsets) % 4
    return jnp.where(core == 0, second * 4 + first, first * 4 + second).astype(jnp.int32)


def segment_scalars(modality):
    rows = modality.shape[0]
    kinds = jnp.arange(MODALITIES, dtype=jnp.int32)[:, None]
    member = modality[None, :] == kinds
    positions = jnp.arange(rows, dtype=jnp.int32)[None, :]
    begin = jnp.min(jnp.where(member, positions, rows), axis=1)
    end = jnp.max(jnp.where(member, positions + 1, 0), axis=1)
    end = jnp.maximum(end, begin)
    core = lax.axis_index("ctx") % 2
    return jnp.concatenate([begin, end, core[None]]).astype(jnp.int32)


def for_tiles(seg_ref, body):
    for kind in range(MODALITIES):
        begin = seg_ref[kind]
        end = seg_ref[MODALITIES + kind]

        def step(tile, carry, kind=kind, begin=begin, end=end):
            row = pl.multiple_of(tile * ROW_TILE, ROW_TILE)
            positions = row + lax.broadcasted_iota(jnp.int32, (ROW_TILE, 1), 0)
            body(kind, row, (positions >= begin) & (positions < end))
            return carry

        lax.fori_loop(begin // ROW_TILE, (end + ROW_TILE - 1) // ROW_TILE, step, 0)


def project(pieces, scale, weights, table, seg, before=None, last=False):
    counts = [piece.shape[0] for piece in pieces]
    starts = [sum(counts[:i]) for i in range(len(counts))]
    steps = sum(counts)
    rows, width = pieces[0].shape[1:]
    out_width = 3 * width
    has_before = before is not None

    def kernel(table_ref, seg_ref, *refs):
        piece_refs = refs[: len(pieces)]
        refs = refs[len(pieces) :]
        scale_ref, *refs = refs
        weight_refs = refs[:3]
        refs = refs[3:]
        if has_before:
            before_ref, *refs = refs
        if last:
            query_ref, kv_ref, query_send_ref, kv_send_ref, total, normed = refs
        else:
            total, normed = refs
        step = pl.program_id(0)

        @pl.when(step == 0)
        def _():
            total[...] = before_ref[...] if has_before else jnp.zeros_like(total)

        for piece_ref, start, count in zip(piece_refs, starts, counts):

            @pl.when((step >= start) & (step < start + count))
            def _(piece_ref=piece_ref):
                normed[...] = (piece_ref[0].astype(F32) * scale_ref[...]).astype(BF)

        def tile(kind, row, keep):
            at = pl.ds(row, ROW_TILE)
            left = jnp.where(keep, normed[at, :], jnp.zeros((), BF))
            for i in range(3):
                total[at, i * width : (i + 1) * width] += jnp.dot(
                    left, weight_refs[i][kind, 0], preferred_element_type=F32
                )

        for_tiles(seg_ref, tile)

        if last:

            @pl.when(step == steps - 1)
            def _():
                query_scale = math.log2(math.e) / math.sqrt(HD)
                core = seg_ref[2 * MODALITIES]
                for mine in range(2):

                    @pl.when(core == mine)
                    def _(mine=mine):
                        for head, q_out, kv_out in (
                            (mine, query_ref, kv_ref),
                            (1 - mine, query_send_ref, kv_send_ref),
                        ):
                            at = head * HD
                            q_out[...] = (total[:, at : at + HD] * query_scale).astype(BF)
                            kv_out[:, :HD] = total[:, width + at : width + at + HD].astype(BF)
                            kv_out[:, HD:] = total[
                                :, 2 * width + at : 2 * width + at + HD
                            ].astype(BF)

    def piece_spec(start, count):
        return pl.BlockSpec(
            (1, rows, width), lambda k, t, s: (jnp.clip(k - start, 0, count - 1), 0, 0)
        )

    whole = lambda shape: pl.BlockSpec(shape, lambda k, t, s: (0,) * len(shape))
    in_specs = [piece_spec(start, count) for start, count in zip(starts, counts)]
    in_specs.append(whole((rows, 1)))
    weight_views = [w.reshape(MODALITIES, 16, width, width) for w in weights]
    in_specs += [
        pl.BlockSpec((MODALITIES, 1, width, width), lambda k, t, s: (0, t[k], 0, 0))
    ] * 3
    operands = [*pieces, scale, *weight_views]
    if has_before:
        in_specs.append(whole((rows, out_width)))
        operands.append(before)
    scratch = [pltpu.VMEM((rows, width), BF)]
    if last:
        shapes = [(rows, HD), (rows, 2 * HD)] * 2
        out_shape = tuple(jax.ShapeDtypeStruct(shape, BF) for shape in shapes)
        out_specs = tuple(whole(shape) for shape in shapes)
        scratch = [pltpu.VMEM((rows, out_width), F32)] + scratch
    else:
        out_shape = jax.ShapeDtypeStruct((rows, out_width), F32)
        out_specs = whole((rows, out_width))
    return pl.pallas_call(
        kernel,
        grid_spec=pltpu.PrefetchScalarGridSpec(
            num_scalar_prefetch=2,
            grid=(steps,),
            in_specs=in_specs,
            out_specs=out_specs,
            scratch_shapes=scratch,
        ),
        out_shape=out_shape,
        compiler_params=pltpu.CompilerParams(vmem_limit_bytes=VMEM_BYTES),
        cost_estimate=pl.CostEstimate(
            flops=2 * steps * rows * 3 * width * width * 3 // 2,
            bytes_accessed=steps * (rows * width * 2 + 9 * width * width * 2),
            transcendentals=0,
        ),
    )(table, seg, *operands)


def fold(query, key, value, keep, state):
    top, total, summed = state
    scores = lax.dot_general(
        query, key, (((1,), (1,)), ((), ())), preferred_element_type=F32
    )
    if keep is not None:
        scores = jnp.where(keep, scores, -1e30)
    new_top = jnp.maximum(top, jnp.max(scores, axis=-1, keepdims=True))
    factor = jnp.exp2(top - new_top)
    weights = jnp.exp2(scores - new_top)
    total = total * factor + jnp.sum(weights, axis=-1, keepdims=True)
    summed = summed * factor + jnp.dot(
        weights.astype(BF), value, preferred_element_type=F32
    )
    return new_top, total, summed


def store_state(state, state_ref):
    top, total, summed = state
    state_ref[0, :, :HD] = summed
    lanes = lax.broadcasted_iota(jnp.int32, (summed.shape[0], HD), 1)
    state_ref[0, :, HD:] = jnp.where(lanes < HD // 2, top, total)


def load_state(state_ref):
    return (
        state_ref[0, :, HD : HD + 1],
        state_ref[0, :, HD + HD // 2 : HD + HD // 2 + 1],
        state_ref[0, :, :HD],
    )


def attend_own(query, kv, core):
    _, rows, _ = query.shape
    per_block = rows // Q_TILE

    def kernel(core_ref, query_ref, kv_ref, state_ref):
        place = pl.program_id(0)
        q = query_ref[0]

        def part(tile):
            block = (tile // per_block) ^ core_ref[0]
            at = pl.ds(pl.multiple_of((tile % per_block) * K_TILE, K_TILE), K_TILE)
            return kv_ref[block, at, :HD], kv_ref[block, at, HD:]

        state = (
            jnp.full((Q_TILE, 1), -1e30, F32),
            jnp.zeros((Q_TILE, 1), F32),
            jnp.zeros((Q_TILE, HD), F32),
        )
        causal = lax.broadcasted_iota(
            jnp.int32, (Q_TILE, K_TILE), 1
        ) <= lax.broadcasted_iota(jnp.int32, (Q_TILE, K_TILE), 0)
        state = fold(q, *part(place), causal, state)
        state = lax.fori_loop(
            0, place, lambda tile, state: fold(q, *part(tile), None, state), state
        )
        store_state(state, state_ref)

    at_tile = lambda i, core: ((i // per_block) ^ core[0], i % per_block, 0)
    return pl.pallas_call(
        kernel,
        grid_spec=pltpu.PrefetchScalarGridSpec(
            num_scalar_prefetch=1,
            grid=(2 * per_block,),
            in_specs=[
                pl.BlockSpec((1, Q_TILE, HD), at_tile),
                pl.BlockSpec((2, rows, 2 * HD), lambda i, core: (0, 0, 0)),
            ],
            out_specs=pl.BlockSpec((1, Q_TILE, 2 * HD), at_tile),
        ),
        out_shape=jax.ShapeDtypeStruct((2, rows, 2 * HD), F32),
        compiler_params=pltpu.CompilerParams(vmem_limit_bytes=VMEM_BYTES),
        cost_estimate=pl.CostEstimate(
            flops=10 * Q_TILE * K_TILE * HD * 4, bytes_accessed=4 << 20, transcendentals=10 * Q_TILE * K_TILE
        ),
    )(core, query, kv)


def attend_other(query, state, sources, use, last=False):
    blocks, rows, _ = query.shape
    per_block = rows // Q_TILE

    def kernel(use_ref, query_ref, before_ref, *refs):
        source_refs = refs[: len(sources)]
        out_ref, after = refs[len(sources) :]
        q = query_ref[0]
        after[...] = before_ref[...]
        for i, source_ref in enumerate(source_refs):

            @pl.when(use_ref[i] != 0)
            def _(source_ref=source_ref):
                state = load_state(after)
                for block in range(source_ref.shape[0]):
                    for tile in range(source_ref.shape[1] // K_TILE):
                        at = pl.ds(tile * K_TILE, K_TILE)
                        state = fold(
                            q, source_ref[block, at, :HD], source_ref[block, at, HD:], None, state
                        )
                store_state(state, after)

        if last:
            _, total, summed = load_state(after)
            out_ref[0] = (summed / total).astype(BF)
        else:
            out_ref[...] = after[...]

    at_tile = lambda i, use: (i // per_block, i % per_block, 0)
    out_width = HD if last else 2 * HD
    keys = sum(source.shape[0] * source.shape[1] for source in sources)
    return pl.pallas_call(
        kernel,
        grid_spec=pltpu.PrefetchScalarGridSpec(
            num_scalar_prefetch=1,
            grid=(blocks * per_block,),
            in_specs=[
                pl.BlockSpec((1, Q_TILE, HD), at_tile),
                pl.BlockSpec((1, Q_TILE, 2 * HD), at_tile),
            ]
            + [pl.BlockSpec(source.shape, lambda i, use: (0, 0, 0)) for source in sources],
            out_specs=pl.BlockSpec((1, Q_TILE, out_width), at_tile),
            scratch_shapes=[pltpu.VMEM((1, Q_TILE, 2 * HD), F32)],
        ),
        out_shape=jax.ShapeDtypeStruct((blocks, rows, out_width), BF if last else F32),
        compiler_params=pltpu.CompilerParams(vmem_limit_bytes=VMEM_BYTES),
        cost_estimate=pl.CostEstimate(
            flops=blocks * rows * keys * HD * 4,
            bytes_accessed=6 << 20,
            transcendentals=blocks * rows * keys,
        ),
    )(use, query, state, *sources)


def output_part(own, other, w_out, table, seg, adds=(), split=False):
    steps = table.shape[0]
    rows = own.shape[0]
    width = 2 * HD

    def kernel(table_ref, seg_ref, own_ref, other_ref, weight_ref, *refs):
        add_refs = refs[: len(adds)]
        *out_refs, attended, total = refs[len(adds) :]
        step = pl.program_id(0)

        @pl.when(step == 0)
        def _():
            core = seg_ref[2 * MODALITIES]

            @pl.when(core == 0)
            def _():
                attended[:, :HD] = own_ref[...]
                attended[:, HD:] = other_ref[...]

            @pl.when(core == 1)
            def _():
                attended[:, :HD] = other_ref[...]
                attended[:, HD:] = own_ref[...]

        total[...] = jnp.zeros_like(total)

        def tile(kind, row, keep):
            at = pl.ds(row, ROW_TILE)
            left = jnp.where(keep, attended[at, :], jnp.zeros((), BF))
            total[at, :] += jnp.dot(left, weight_ref[kind], preferred_element_type=F32)

        for_tiles(seg_ref, tile)
        for (array, start), add_ref in zip(adds, add_refs):

            @pl.when((step >= start) & (step < start + array.shape[0]))
            def _(add_ref=add_ref):
                total[...] += add_ref[0].astype(F32)

        if split:
            for i, out_ref in enumerate(out_refs):

                @pl.when(step == i)
                def _(out_ref=out_ref):
                    out_ref[...] = total[...].astype(BF)

        else:
            out_refs[0][0] = total[...].astype(BF)

    def add_spec(array, start):
        return pl.BlockSpec(
            (1, rows, width), lambda k, t, s: (jnp.clip(k - start, 0, array.shape[0] - 1), 0, 0)
        )

    if split:
        out_shape = (jax.ShapeDtypeStruct((rows, width), BF),) * steps
        out_specs = (pl.BlockSpec((rows, width), lambda k, t, s: (0, 0)),) * steps
    else:
        out_shape = jax.ShapeDtypeStruct((steps, rows, width), BF)
        out_specs = pl.BlockSpec((1, rows, width), lambda k, t, s: (k, 0, 0))
    return pl.pallas_call(
        kernel,
        grid_spec=pltpu.PrefetchScalarGridSpec(
            num_scalar_prefetch=2,
            grid=(steps,),
            in_specs=[
                pl.BlockSpec((rows, HD), lambda k, t, s: (0, 0)),
                pl.BlockSpec((rows, HD), lambda k, t, s: (0, 0)),
                pl.BlockSpec((MODALITIES, width, width), lambda k, t, s: (0, 0, t[k])),
            ]
            + [add_spec(array, start) for array, start in adds],
            out_specs=out_specs,
            scratch_shapes=[pltpu.VMEM((rows, width), BF), pltpu.VMEM((rows, width), F32)],
        ),
        out_shape=out_shape,
        compiler_params=pltpu.CompilerParams(vmem_limit_bytes=VMEM_BYTES),
        cost_estimate=pl.CostEstimate(
            flops=3 * steps * rows * width * width,
            bytes_accessed=steps * (3 * width * width + rows * width) * 2,
            transcendentals=0,
        ),
    )(table, seg, own, other, w_out, *[array for array, _ in adds])


def local(tokens, modality, w_query, w_key, w_value, w_out):
    seg = segment_scalars(modality)
    core = seg[2 * MODALITIES :]

    near = [tokens, move(tokens, True, 1), move(tokens, True, -1), move(tokens, True, 2)]
    group = jnp.stack(near)
    squares = jnp.sum(jnp.square(group.astype(F32)), axis=(0, 2))
    mean = (
        squares + move(squares, False, 1) + move(squares, False, -1) + move(squares, False, 2)
    ) / 4096.0
    scale = lax.rsqrt(mean + EPS)[:, None]
    from_before = move(group, False, 1)
    from_after = move(group, False, -1)
    far_low = move(from_before[:2], False, 1)
    far_high = move(from_after[2:], False, -1)
    weights = (w_query, w_key, w_value)
    table = shard_table(np.tile(OFFSETS, 4), np.repeat(OFFSETS, 4))
    partial = project([group, from_before, from_after], scale, weights, table[:12], seg)
    query, kv, query_send, kv_send = project(
        [far_low, far_high], scale, weights, table[12:], seg, before=partial, last=True
    )

    kv = jnp.stack([kv, swap_core(kv_send)])
    query = jnp.stack([query, swap_core(query_send)])
    kv_before = move_x(kv, 1)
    kv_after = move_x(kv, -1)
    kv_far_low = move_x(kv_before[:1], 1)
    kv_far_high = move_x(kv_after[1:], -1)
    chip = lax.axis_index("ctx") // 2
    state = attend_own(query, kv, core)
    near_use = jnp.stack([chip >= 1, chip == 3]).astype(jnp.int32)
    state = attend_other(query, state, [kv_before, kv_after], near_use)
    far_use = jnp.stack([chip >= 2, chip >= 2]).astype(jnp.int32)
    attended = attend_other(query, state, [kv_far_low, kv_far_high], far_use, last=True)
    own = attended[0]
    other = swap_core(attended[1])

    part = functools.partial(output_part, own, other, w_out)
    seconds = np.arange(4)
    groups = [shard_table(np.full(4, offset), seconds) for offset in range(4)]
    low = move(part(groups[2][:2], seg), True, 1)
    high = move(part(groups[2][2:], seg), True, -1)
    from_before = move(part(groups[1], seg, adds=[(low, 0)]), True, 1)
    from_after = move(part(groups[3], seg, adds=[(high, 2)]), True, -1)
    here, plus, two, minus = part(
        groups[0], seg, adds=[(from_before, 0), (from_after, 0)], split=True
    )
    branch = (
        here.astype(F32)
        + move(plus, False, 1).astype(F32)
        + move(two, False, 2).astype(F32)
        + move(minus, False, -1).astype(F32)
    )
    return (tokens.astype(F32) + branch).astype(BF)


def solution(mesh):
    in_specs = (
        P("ctx", "tp"),
        P("ctx"),
        P(None, None, "tp"),
        P(None, None, "tp"),
        P(None, None, "tp"),
        P(None, "tp", None),
    )
    return jax.shard_map(
        local, mesh=mesh, in_specs=in_specs, out_specs=P("ctx", "tp"), check_vma=False
    )
```

```python
import functools
import math

import jax
import jax.numpy as jnp
import numpy as np
from jax import lax
from jax.experimental import pallas as pl
from jax.experimental.pallas import tpu as pltpu
from jax.sharding import PartitionSpec as P

HD = 128
MODALITIES = 3
EPS = 1e-05
WINDOW = 528
ALIGN = 16
Q_TILE = 512
K_TILE = 1024
STATE_ROWS = HD + 16
AXES = ("ctx", "tp")
BF = jnp.bfloat16
F32 = jnp.float32
OFFSETS = np.array([0, 3, 1, 2])
VMEM_BYTES = 48 * 1024 * 1024


def plane_perm(first, step):
    pairs = []
    for ctx in range(8):
        for z in range(4):
            for y in range(4):
                along_y = (ctx % 2 == 0) == first
                to_z = z if along_y else (z + step) % 4
                to_y = (y + step) % 4 if along_y else y
                pairs.append((ctx * 16 + z * 4 + y, ctx * 16 + to_z * 4 + to_y))
    return pairs


def move(array, first, step):
    return lax.ppermute(array, AXES, plane_perm(first, step))


def move_x(array, step):
    pairs = [(x * 2 + c, ((x + step) % 4) * 2 + c) for x in range(4) for c in range(2)]
    return lax.ppermute(array, "ctx", pairs)


def swap_core(array):
    return lax.ppermute(array, "ctx", [(i, i ^ 1) for i in range(8)])


def shard_table(first_offsets, second_offsets):
    core = lax.axis_index("ctx") % 2
    tp = lax.axis_index("tp")
    z, y = tp // 4, tp % 4
    first_offsets = jnp.asarray(first_offsets, jnp.int32)
    second_offsets = jnp.asarray(second_offsets, jnp.int32)
    first = (jnp.where(core == 0, y, z) + first_offsets) % 4
    second = (jnp.where(core == 0, z, y) + second_offsets) % 4
    return jnp.where(core == 0, second * 4 + first, first * 4 + second).astype(jnp.int32)


def segment_scalars(modality):
    rows = modality.shape[0]
    kinds = jnp.arange(MODALITIES, dtype=jnp.int32)[:, None]
    member = modality[None, :] == kinds
    positions = jnp.arange(rows, dtype=jnp.int32)[None, :]
    begin = jnp.min(jnp.where(member, positions, rows), axis=1)
    end = jnp.max(jnp.where(member, positions + 1, 0), axis=1)
    end = jnp.maximum(end, begin)
    core = lax.axis_index("ctx") % 2
    return jnp.concatenate([begin, end, core[None]]).astype(jnp.int32)


def for_runs(seg_ref, rows, body):
    for kind in range(MODALITIES):
        begin = seg_ref[kind]
        end = seg_ref[MODALITIES + kind]

        @pl.when(end > begin)
        def _(kind=kind, begin=begin, end=end):
            first = jnp.minimum(begin // ALIGN * ALIGN, rows - WINDOW)
            first = pl.multiple_of(first, ALIGN)
            positions = first + lax.broadcasted_iota(jnp.int32, (WINDOW, 1), 0)
            body(kind, pl.ds(first, WINDOW), (positions >= begin) & (positions < end))


def constant_spec(shape):
    return pl.BlockSpec(shape, lambda k, *scalars: (0,) * len(shape))


def project(pieces, scale, weights, table, seg, before=None, last=False):
    steps = len(pieces)
    shards, rows, width = pieces[0].shape
    out_width = 3 * width
    has_before = before is not None

    def kernel(table_ref, seg_ref, *refs):
        piece_refs = refs[:steps]
        scale_ref, *refs = refs[steps:]
        weight_refs = [refs[i * shards : (i + 1) * shards] for i in range(3)]
        refs = refs[3 * shards :]
        if has_before:
            before_ref, *refs = refs
        if last:
            query_ref, kv_ref, query_send_ref, kv_send_ref, total, normed = refs
        else:
            total, normed = refs
        step = pl.program_id(0)

        @pl.when(step == 0)
        def _():
            total[...] = before_ref[...] if has_before else jnp.zeros_like(total)

        for i, piece_ref in enumerate(piece_refs):

            @pl.when(step == i)
            def _(piece_ref=piece_ref):
                for j in range(shards):
                    normed[:, j * width : (j + 1) * width] = (
                        piece_ref[j].astype(F32) * scale_ref[...]
                    ).astype(BF)

        def run(kind, at, keep):
            left = jnp.where(keep, normed[at, :], jnp.zeros((), BF))
            for i in range(3):
                right = jnp.concatenate([ref[kind, 0] for ref in weight_refs[i]], axis=0)
                total[at, i * width : (i + 1) * width] += jnp.dot(
                    left, right, preferred_element_type=F32
                )

        for_runs(seg_ref, rows, run)

        if last:

            @pl.when(step == steps - 1)
            def _():
                query_scale = math.log2(math.e) / math.sqrt(HD)
                core = seg_ref[2 * MODALITIES]
                for mine in range(2):

                    @pl.when(core == mine)
                    def _(mine=mine):
                        for head, q_out, kv_out in (
                            (mine, query_ref, kv_ref),
                            (1 - mine, query_send_ref, kv_send_ref),
                        ):
                            at = head * HD
                            q_out[...] = (total[:, at : at + HD] * query_scale).astype(BF)
                            kv_out[:, :HD] = total[:, width + at : width + at + HD].astype(BF)
                            at += 2 * width
                            for row in range(0, rows, HD):
                                block = total[row : row + HD, at : at + HD]
                                kv_out[row : row + HD, HD:] = block.T.astype(BF)

    in_specs = [constant_spec(piece.shape) for piece in pieces]
    in_specs.append(constant_spec((rows, 1)))
    operands = [*pieces, scale]
    for weight in weights:
        view = weight.reshape(MODALITIES, 16, width, width)
        for j in range(shards):
            in_specs.append(
                pl.BlockSpec(
                    (MODALITIES, 1, width, width),
                    lambda k, t, s, j=j: (0, t[k * shards + j], 0, 0),
                )
            )
            operands.append(view)
    if has_before:
        in_specs.append(constant_spec((rows, out_width)))
        operands.append(before)
    scratch = [pltpu.VMEM((rows, shards * width), BF)]
    if last:
        shapes = [(rows, HD), (rows, 2 * HD)] * 2
        out_shape = tuple(jax.ShapeDtypeStruct(shape, BF) for shape in shapes)
        out_specs = tuple(constant_spec(shape) for shape in shapes)
        scratch = [pltpu.VMEM((rows, out_width), F32)] + scratch
    else:
        out_shape = jax.ShapeDtypeStruct((rows, out_width), F32)
        out_specs = constant_spec((rows, out_width))
    return pl.pallas_call(
        kernel,
        grid_spec=pltpu.PrefetchScalarGridSpec(
            num_scalar_prefetch=2,
            grid=(steps,),
            in_specs=in_specs,
            out_specs=out_specs,
            scratch_shapes=scratch,
        ),
        out_shape=out_shape,
        compiler_params=pltpu.CompilerParams(vmem_limit_bytes=VMEM_BYTES),
        cost_estimate=pl.CostEstimate(
            flops=2 * steps * shards * 3 * WINDOW * width * out_width,
            bytes_accessed=steps * shards * (rows * width * 2 + 9 * width * width * 2),
            transcendentals=0,
        ),
    )(table, seg, *operands)


def score(query, key, keep=None):
    scores = lax.dot_general(key, query, (((1,), (1,)), ((), ())), preferred_element_type=F32)
    return scores if keep is None else jnp.where(keep, scores, -1e30)


def fold(state, scores, value_t):
    top, total, summed = state
    new_top = jnp.maximum(top, jnp.max(scores, axis=0, keepdims=True))
    factor = jnp.exp2(top - new_top)
    weights = jnp.exp2(scores - new_top)
    total = total * factor + jnp.sum(weights, axis=0, keepdims=True)
    summed = summed * factor + jnp.dot(value_t, weights.astype(BF), preferred_element_type=F32)
    return new_top, total, summed


def empty_state():
    return (
        jnp.full((1, Q_TILE), -1e30, F32),
        jnp.zeros((1, Q_TILE), F32),
        jnp.zeros((HD, Q_TILE), F32),
    )


def store_state(state, state_ref):
    top, total, summed = state
    state_ref[0, :HD, :] = summed
    state_ref[0, HD : HD + 8, :] = jnp.broadcast_to(top, (8, Q_TILE))
    state_ref[0, HD + 8 :, :] = jnp.broadcast_to(total, (8, Q_TILE))


def load_state(state_ref):
    return (
        state_ref[0, HD : HD + 1, :],
        state_ref[0, HD + 8 : HD + 9, :],
        state_ref[0, :HD, :],
    )


def read_keys(ref, first, count):
    key = ref[pl.ds(first, count), :HD]
    blocks = [ref[pl.ds(first + i, HD), HD:] for i in range(0, count, HD)]
    return key, jnp.concatenate(blocks, axis=1)


def attend_own(query, query_other, kv, kv_other, core):
    rows = query.shape[0]
    per_block = rows // Q_TILE
    tiles = 2 * per_block

    def kernel(core_ref, query_ref, query_other_ref, kv_ref, kv_other_ref, state_ref, keys, both):
        place = pl.program_id(0)

        @pl.when(place == 0)
        def _():
            for mine in range(2):

                @pl.when(core_ref[0] == mine)
                def _(mine=mine):
                    at, other = mine * rows, (1 - mine) * rows
                    keys[at : at + rows, :] = kv_ref[...]
                    keys[other : other + rows, :] = kv_other_ref[...]
                    both[at : at + rows, :] = query_ref[...]
                    both[other : other + rows, :] = query_other_ref[...]

        at = pl.multiple_of(place * Q_TILE, Q_TILE)
        q = both[pl.ds(at, Q_TILE), :]
        causal = lax.broadcasted_iota(
            jnp.int32, (Q_TILE, Q_TILE), 0
        ) <= lax.broadcasted_iota(jnp.int32, (Q_TILE, Q_TILE), 1)
        key, value_t = read_keys(keys, at, Q_TILE)
        state = fold(empty_state(), score(q, key, causal), value_t)

        def earlier(tile, state):
            key, value_t = read_keys(keys, pl.multiple_of(tile * Q_TILE, Q_TILE), Q_TILE)
            return fold(state, score(q, key), value_t)

        store_state(lax.fori_loop(0, place, earlier, state), state_ref)

    whole = constant_spec((rows, HD))
    whole_kv = constant_spec((rows, 2 * HD))
    return pl.pallas_call(
        kernel,
        grid_spec=pltpu.PrefetchScalarGridSpec(
            num_scalar_prefetch=1,
            grid=(tiles,),
            in_specs=[whole, whole, whole_kv, whole_kv],
            out_specs=pl.BlockSpec(
                (1, STATE_ROWS, Q_TILE),
                lambda i, core: ((i + core[0] * per_block) % tiles, 0, 0),
            ),
            scratch_shapes=[
                pltpu.VMEM((2 * rows, 2 * HD), BF),
                pltpu.VMEM((2 * rows, HD), BF),
            ],
        ),
        out_shape=jax.ShapeDtypeStruct((tiles, STATE_ROWS, Q_TILE), F32),
        compiler_params=pltpu.CompilerParams(vmem_limit_bytes=VMEM_BYTES),
        cost_estimate=pl.CostEstimate(
            flops=10 * Q_TILE * Q_TILE * HD * 4,
            bytes_accessed=4 << 20,
            transcendentals=10 * Q_TILE * Q_TILE,
        ),
    )(core, query, query_other, kv, kv_other)


def attend_other(query, query_other, state, sources, use, last=False):
    rows = query.shape[0]
    per_block = rows // Q_TILE
    tiles = 2 * per_block
    count = len(sources)

    def kernel(use_ref, query_ref, query_other_ref, before_ref, *refs):
        source_refs = refs[:count]
        *out_refs, after, q_ref = refs[count:]
        tile = pl.program_id(0)

        @pl.when(tile < per_block)
        def _():
            q_ref[...] = query_ref[...]

        @pl.when(tile >= per_block)
        def _():
            q_ref[...] = query_other_ref[...]

        q = q_ref[...]
        after[...] = before_ref[...]

        def fold_in(refs):
            parts = [(ref, at) for ref in refs for at in range(0, rows, K_TILE)]
            state = load_state(after)
            scores = None
            for i, (ref, at) in enumerate(parts):
                key, value_t = read_keys(ref, at, K_TILE)
                if scores is None:
                    scores = score(q, key)
                later = None
                if i + 1 < len(parts):
                    next_ref, next_at = parts[i + 1]
                    later = score(q, next_ref[next_at : next_at + K_TILE, :HD])
                state = fold(state, scores, value_t)
                scores = later
            store_state(state, after)

        all_used = use_ref[0]
        for i in range(1, count):
            all_used = all_used & use_ref[i]

        @pl.when(all_used != 0)
        def _():
            fold_in(source_refs)

        for i, source_ref in enumerate(source_refs):

            @pl.when((all_used == 0) & (use_ref[i] != 0))
            def _(source_ref=source_ref):
                fold_in([source_ref])

        if last:
            _, total, summed = load_state(after)
            attended = (summed / total).T.astype(BF)
            for part, out_ref in enumerate(out_refs):

                @pl.when(tile // per_block == part)
                def _(out_ref=out_ref):
                    at = pl.multiple_of(tile % per_block * Q_TILE, Q_TILE)
                    out_ref[pl.ds(at, Q_TILE), :] = attended

        else:
            out_refs[0][...] = after[...]

    state_spec = pl.BlockSpec((1, STATE_ROWS, Q_TILE), lambda i, use: (i, 0, 0))
    if last:
        out_shape = (jax.ShapeDtypeStruct((rows, HD), BF),) * 2
        out_specs = (constant_spec((rows, HD)),) * 2
    else:
        out_shape = jax.ShapeDtypeStruct((tiles, STATE_ROWS, Q_TILE), F32)
        out_specs = state_spec
    return pl.pallas_call(
        kernel,
        grid_spec=pltpu.PrefetchScalarGridSpec(
            num_scalar_prefetch=1,
            grid=(tiles,),
            in_specs=[
                pl.BlockSpec((Q_TILE, HD), lambda i, use: (jnp.minimum(i, per_block - 1), 0)),
                pl.BlockSpec((Q_TILE, HD), lambda i, use: (jnp.maximum(i - per_block, 0), 0)),
                state_spec,
            ]
            + [constant_spec(source.shape) for source in sources],
            out_specs=out_specs,
            scratch_shapes=[
                pltpu.VMEM((1, STATE_ROWS, Q_TILE), F32),
                pltpu.VMEM((Q_TILE, HD), BF),
            ],
        ),
        out_shape=out_shape,
        compiler_params=pltpu.CompilerParams(vmem_limit_bytes=VMEM_BYTES),
        cost_estimate=pl.CostEstimate(
            flops=2 * rows * count * rows * HD * 4,
            bytes_accessed=6 << 20,
            transcendentals=2 * rows * count * rows,
        ),
    )(use, query, query_other, state, *sources)


def output_part(own, other, w_out, table, seg, adds=(), split=False):
    steps = table.shape[0] // 2
    rows = own.shape[0]
    width = 2 * HD

    def kernel(table_ref, seg_ref, own_ref, other_ref, *refs):
        weight_refs = refs[:2]
        add_refs = refs[2 : 2 + len(adds)]
        *out_refs, attended, total = refs[2 + len(adds) :]
        step = pl.program_id(0)

        @pl.when(step == 0)
        def _():
            core = seg_ref[2 * MODALITIES]

            @pl.when(core == 0)
            def _():
                attended[:, :HD] = own_ref[...]
                attended[:, HD:] = other_ref[...]

            @pl.when(core == 1)
            def _():
                attended[:, :HD] = other_ref[...]
                attended[:, HD:] = own_ref[...]

        total[...] = jnp.zeros_like(total)

        def run(kind, at, keep):
            left = jnp.where(keep, attended[at, :], jnp.zeros((), BF))
            for i in range(2):
                total[at, i * width : (i + 1) * width] += jnp.dot(
                    left, weight_refs[i][kind], preferred_element_type=F32
                )

        for_runs(seg_ref, rows, run)
        for (_, at), add_ref in zip(adds, add_refs):

            @pl.when(step == at)
            def _(add_ref=add_ref):
                for i in range(2):
                    total[:, i * width : (i + 1) * width] += add_ref[i].astype(F32)

        for at in range(steps):

            @pl.when(step == at)
            def _(at=at):
                for i in range(2):
                    result = total[:, i * width : (i + 1) * width].astype(BF)
                    if split:
                        out_refs[2 * at + i][...] = result
                    else:
                        out_refs[at][i] = result

    shape = (rows, width) if split else (2, rows, width)
    outs = 2 * steps if split else steps
    return pl.pallas_call(
        kernel,
        grid_spec=pltpu.PrefetchScalarGridSpec(
            num_scalar_prefetch=2,
            grid=(steps,),
            in_specs=[constant_spec((rows, HD))] * 2
            + [
                pl.BlockSpec(
                    (MODALITIES, width, width), lambda k, t, s, i=i: (0, 0, t[2 * k + i])
                )
                for i in range(2)
            ]
            + [constant_spec(array.shape) for array, _ in adds],
            out_specs=(constant_spec(shape),) * outs,
            scratch_shapes=[pltpu.VMEM((rows, width), BF), pltpu.VMEM((rows, 2 * width), F32)],
        ),
        out_shape=(jax.ShapeDtypeStruct(shape, BF),) * outs,
        compiler_params=pltpu.CompilerParams(vmem_limit_bytes=VMEM_BYTES),
        cost_estimate=pl.CostEstimate(
            flops=2 * 3 * WINDOW * steps * 2 * width * width,
            bytes_accessed=steps * 2 * (3 * width * width + rows * width) * 2,
            transcendentals=0,
        ),
    )(table, seg, own, other, w_out, w_out, *[array for array, _ in adds])


def local(tokens, modality, w_query, w_key, w_value, w_out):
    seg = segment_scalars(modality)
    core = seg[2 * MODALITIES :]
    weights = (w_query, w_key, w_value)

    low = jnp.stack([tokens, move(tokens, True, 1)])
    high = jnp.stack([move(tokens, True, -1), move(tokens, True, 2)])
    squares = sum(jnp.sum(jnp.square(half.astype(F32)), axis=(0, 2)) for half in (low, high))
    total = squares + move(squares, False, 1) + move(squares, False, -1) + move(squares, False, 2)
    scale = lax.rsqrt(total / 4096.0 + EPS)[:, None]
    before_low = move(low, False, 1)
    after_high = move(high, False, -1)
    before_high = move(high, False, 1)
    after_low = move(low, False, -1)
    before_low, after_high, scale = lax.optimization_barrier((before_low, after_high, scale))
    far_low = move(before_low, False, 1)
    far_high = move(after_high, False, -1)
    table = shard_table(np.tile(OFFSETS, 4), np.repeat(OFFSETS, 4))
    partial = project([low, high], scale, weights, table[:4], seg)
    partial = project(
        [before_low, before_high, after_low, after_high],
        scale, weights, table[4:12], seg, before=partial,
    )
    query, kv, query_send, kv_send = project(
        [far_low, far_high], scale, weights, table[12:], seg, before=partial, last=True
    )

    kv_other = swap_core(kv_send)
    query_other = swap_core(query_send)
    kv_before = move_x(kv, 1)
    kv_other_after = move_x(kv_other, -1)
    kv_other_before = move_x(kv_other, 1)
    kv_after = move_x(kv, -1)
    kv_far = move_x(kv_before, 1)
    kv_other_far = move_x(kv_other_after, -1)
    chip = lax.axis_index("ctx") // 2
    near_use = jnp.stack([chip >= 1, chip == 3]).astype(jnp.int32)
    far_use = jnp.stack([chip >= 2, chip >= 2]).astype(jnp.int32)
    queries = (query, query_other)
    state = attend_own(*queries, kv, kv_other, core)
    state = attend_other(*queries, state, [kv_before, kv_other_after], near_use)
    state = attend_other(*queries, state, [kv_other_before, kv_after], near_use)
    own, own_send = attend_other(*queries, state, [kv_far, kv_other_far], far_use, last=True)
    other = swap_core(own_send)

    part = functools.partial(output_part, own, other, w_out)
    plus, two, minus = (shard_table(np.full(4, offset), np.arange(4)) for offset in (1, 2, 3))
    here = shard_table(np.zeros(4), np.arange(4))
    two_low, two_high = part(two, seg)
    two_low = move(two_low, True, 1)
    two_high = move(two_high, True, -1)
    plus_high, minus_low = part(jnp.concatenate([plus[2:], minus[:2]]), seg)
    plus_high = move(plus_high, True, 1)
    minus_low = move(minus_low, True, -1)
    (plus_low,) = part(plus[:2], seg, adds=[(two_low, 0)])
    plus_low = move(plus_low, True, 1)
    (minus_high,) = part(minus[2:], seg, adds=[(two_high, 0)])
    minus_high = move(minus_high, True, -1)
    mine, plus, two, minus = part(
        here, seg, adds=[(plus_low, 0), (minus_low, 0), (plus_high, 1), (minus_high, 1)], split=True
    )
    branch = (
        mine.astype(F32)
        + move(plus, False, 1).astype(F32)
        + move(two, False, 2).astype(F32)
        + move(minus, False, -1).astype(F32)
    )
    return (tokens.astype(F32) + branch).astype(BF)


def solution(mesh):
    in_specs = (
        P("ctx", "tp"),
        P("ctx"),
        P(None, None, "tp"),
        P(None, None, "tp"),
        P(None, None, "tp"),
        P(None, "tp", None),
    )
    return jax.shard_map(
        local, mesh=mesh, in_specs=in_specs, out_specs=P("ctx", "tp"), check_vma=False
    )
```

```python
import functools
import math

import jax
import jax.numpy as jnp
import numpy as np
from jax import lax
from jax.experimental import pallas as pl
from jax.experimental.pallas import tpu as pltpu
from jax.sharding import PartitionSpec as P

HD = 128
MODALITIES = 3
EPS = 1e-05
WINDOW = 528
ALIGN = 16
Q_TILE = 512
K_TILE = 1024
STATE_ROWS = HD + 16
AXES = ("ctx", "tp")
BF = jnp.bfloat16
F32 = jnp.float32
OFFSETS = np.array([0, 3, 1, 2])
VMEM_BYTES = 28 * 1024 * 1024


def plane_perm(first, step):
    pairs = []
    for ctx in range(8):
        for z in range(4):
            for y in range(4):
                along_y = (ctx % 2 == 0) == first
                to_z = z if along_y else (z + step) % 4
                to_y = (y + step) % 4 if along_y else y
                pairs.append((ctx * 16 + z * 4 + y, ctx * 16 + to_z * 4 + to_y))
    return pairs


def move(array, first, step):
    return lax.ppermute(array, AXES, plane_perm(first, step))


def move_x(array, step):
    pairs = [(x * 2 + c, ((x + step) % 4) * 2 + c) for x in range(4) for c in range(2)]
    return lax.ppermute(array, "ctx", pairs)


def swap_core(array):
    return lax.ppermute(array, "ctx", [(i, i ^ 1) for i in range(8)])


def shard_table(first_offsets, second_offsets):
    core = lax.axis_index("ctx") % 2
    tp = lax.axis_index("tp")
    z, y = tp // 4, tp % 4
    first_offsets = jnp.asarray(first_offsets, jnp.int32)
    second_offsets = jnp.asarray(second_offsets, jnp.int32)
    first = (jnp.where(core == 0, y, z) + first_offsets) % 4
    second = (jnp.where(core == 0, z, y) + second_offsets) % 4
    return jnp.where(core == 0, second * 4 + first, first * 4 + second).astype(jnp.int32)


def segment_scalars(modality):
    rows = modality.shape[0]
    kinds = jnp.arange(MODALITIES, dtype=jnp.int32)[:, None]
    member = modality[None, :] == kinds
    positions = jnp.arange(rows, dtype=jnp.int32)[None, :]
    begin = jnp.min(jnp.where(member, positions, rows), axis=1)
    end = jnp.max(jnp.where(member, positions + 1, 0), axis=1)
    end = jnp.maximum(end, begin)
    core = lax.axis_index("ctx") % 2
    return jnp.concatenate([begin, end, core[None]]).astype(jnp.int32)


def for_runs(seg_ref, rows, body):
    for kind in range(MODALITIES):
        begin = seg_ref[kind]
        end = seg_ref[MODALITIES + kind]
        first = jnp.minimum(begin // ALIGN * ALIGN, rows - WINDOW)
        first = pl.multiple_of(first, ALIGN)
        positions = first + lax.broadcasted_iota(jnp.int32, (WINDOW, 1), 0)
        body(kind, pl.ds(first, WINDOW), (positions >= begin) & (positions < end))


def constant_spec(shape):
    return pl.BlockSpec(shape, lambda k, *scalars: (0,) * len(shape))


def project(pieces, scale, weights, table, seg, before=None, last=False):
    count = len(pieces)
    shards, rows, width = pieces[0].shape
    depth = count * shards
    has_before = before is not None

    def kernel(table_ref, seg_ref, scale_ref, *refs):
        piece_refs = refs[:count]
        weight_refs = refs[count : count + 3]
        refs = refs[count + 3 :]
        if has_before:
            before_ref, *refs = refs
        if last:
            query_ref, kv_ref, query_send_ref, kv_send_ref, *refs = refs
        else:
            out_ref, *refs = refs
        held, left, right, total, piece_sem, weight_sem, total_sem = refs

        piece_copies = [
            pltpu.make_async_copy(piece_refs[i], held.at[i], piece_sem.at[i]) for i in range(count)
        ]
        weight_copies = []
        total_copies = []
        for i in range(3):
            for j in range(depth):
                first = pl.multiple_of(table_ref[j] * width, width)
                weight_copies.append(
                    pltpu.make_async_copy(
                        weight_refs[i].at[:, pl.ds(first, width), :],
                        right.at[i, :, pl.ds(j * width, width), :],
                        weight_sem.at[i, j],
                    )
                )
            if has_before:
                total_copies.append(
                    pltpu.make_async_copy(before_ref.at[i], total.at[i], total_sem.at[i])
                )
        for copy in piece_copies:
            copy.start()
        for i in range(3):
            for copy in weight_copies[i * depth : (i + 1) * depth]:
                copy.start()
            if has_before:
                total_copies[i].start()
        for i in range(count):
            piece_copies[i].wait()

        def norm(kind, at, keep):
            row_scale = jnp.where(keep, scale_ref[at, :], 0.0)
            for j in range(depth):
                piece = held[j // shards, j % shards, at, :].astype(F32)
                left[kind, :, j * width : (j + 1) * width] = (piece * row_scale).astype(BF)

        for_runs(seg_ref, rows, norm)
        out_copies = []
        for i in range(3):
            if has_before:
                total_copies[i].wait()
            else:
                total[i] = jnp.zeros((rows, width), F32)
            for copy in weight_copies[i * depth : (i + 1) * depth]:
                copy.wait()

            def run(kind, at, keep, i=i):
                total[i, at, :] += jnp.dot(left[kind], right[i, kind], preferred_element_type=F32)

            for_runs(seg_ref, rows, run)
            if not last:
                out_copies.append(
                    pltpu.make_async_copy(total.at[i], out_ref.at[i], total_sem.at[3 + i])
                )
                out_copies[i].start()
        for copy in out_copies:
            copy.wait()

        if last:
            query_scale = math.log2(math.e) / math.sqrt(HD)
            core = seg_ref[2 * MODALITIES]
            for mine in range(2):

                @pl.when(core == mine)
                def _(mine=mine):
                    for head, q_out, kv_out in (
                        (mine, query_ref, kv_ref),
                        (1 - mine, query_send_ref, kv_send_ref),
                    ):
                        at = slice(head * HD, (head + 1) * HD)
                        kv_out[:, :HD] = total[0, :, at].astype(BF)
                        for row in range(0, rows, HD):
                            kv_out[row : row + HD, HD:] = total[1, row : row + HD, at].T.astype(BF)
                        q_out[...] = (total[2, :, at] * query_scale).astype(BF)

    in_specs = [pl.BlockSpec(memory_space=pltpu.SMEM)] * 2
    in_specs.append(pl.BlockSpec(memory_space=pltpu.VMEM))
    operands = [table, seg, scale, *pieces, *weights]
    if has_before:
        operands.append(before)
    in_specs += [pl.BlockSpec(memory_space=pl.ANY)] * (len(operands) - 3)
    if last:
        shapes = [(rows, HD), (rows, 2 * HD)] * 2
        out_shape = tuple(jax.ShapeDtypeStruct(shape, BF) for shape in shapes)
        out_specs = (pl.BlockSpec(memory_space=pltpu.VMEM),) * 4
    else:
        out_shape = jax.ShapeDtypeStruct((3, rows, width), F32)
        out_specs = pl.BlockSpec(memory_space=pl.ANY)
    return pl.pallas_call(
        kernel,
        in_specs=in_specs,
        out_specs=out_specs,
        scratch_shapes=[
            pltpu.VMEM((count, shards, rows, width), BF),
            pltpu.VMEM((MODALITIES, WINDOW, depth * width), BF),
            pltpu.VMEM((3, MODALITIES, depth * width, width), BF),
            pltpu.VMEM((3, rows, width), F32),
            pltpu.SemaphoreType.DMA((count,)),
            pltpu.SemaphoreType.DMA((3, depth)),
            pltpu.SemaphoreType.DMA((6,)),
        ],
        out_shape=out_shape,
        compiler_params=pltpu.CompilerParams(vmem_limit_bytes=VMEM_BYTES),
        cost_estimate=pl.CostEstimate(
            flops=2 * depth * 3 * WINDOW * width * 3 * width,
            bytes_accessed=depth * (rows * width * 2 + 9 * width * width * 2),
            transcendentals=0,
        ),
    )(*operands)


def score(query, key, keep=None):
    scores = lax.dot_general(key, query, (((1,), (1,)), ((), ())), preferred_element_type=F32)
    return scores if keep is None else jnp.where(keep, scores, -1e30)


def fold(state, scores, value_t):
    top, total, summed = state
    new_top = jnp.maximum(top, jnp.max(scores, axis=0, keepdims=True))
    factor = jnp.exp2(top - new_top)
    weights = jnp.exp2(scores - new_top)
    total = total * factor + jnp.sum(weights, axis=0, keepdims=True)
    summed = summed * factor + jnp.dot(value_t, weights.astype(BF), preferred_element_type=F32)
    return new_top, total, summed


def empty_state():
    return (
        jnp.full((1, Q_TILE), -1e30, F32),
        jnp.zeros((1, Q_TILE), F32),
        jnp.zeros((HD, Q_TILE), F32),
    )


def store_state(state, state_ref):
    top, total, summed = state
    state_ref[0, :HD, :] = summed
    state_ref[0, HD : HD + 8, :] = jnp.broadcast_to(top, (8, Q_TILE))
    state_ref[0, HD + 8 :, :] = jnp.broadcast_to(total, (8, Q_TILE))


def load_state(state_ref):
    return (
        state_ref[0, HD : HD + 1, :],
        state_ref[0, HD + 8 : HD + 9, :],
        state_ref[0, :HD, :],
    )


def read_keys(ref, first, count):
    key = ref[pl.ds(first, count), :HD]
    blocks = [ref[pl.ds(first + i, HD), HD:] for i in range(0, count, HD)]
    return key, jnp.concatenate(blocks, axis=1)


def attend_own(query, query_other, kv, kv_other, core):
    rows = query.shape[0]
    per_block = rows // Q_TILE
    tiles = 2 * per_block

    def kernel(core_ref, query_ref, query_other_ref, kv_ref, kv_other_ref, state_ref, keys, both):
        place = pl.program_id(0)

        @pl.when(place == 0)
        def _():
            for mine in range(2):

                @pl.when(core_ref[0] == mine)
                def _(mine=mine):
                    at, other = mine * rows, (1 - mine) * rows
                    keys[at : at + rows, :] = kv_ref[...]
                    keys[other : other + rows, :] = kv_other_ref[...]
                    both[at : at + rows, :] = query_ref[...]
                    both[other : other + rows, :] = query_other_ref[...]

        at = pl.multiple_of(place * Q_TILE, Q_TILE)
        q = both[pl.ds(at, Q_TILE), :]
        causal = lax.broadcasted_iota(
            jnp.int32, (Q_TILE, Q_TILE), 0
        ) <= lax.broadcasted_iota(jnp.int32, (Q_TILE, Q_TILE), 1)
        key, value_t = read_keys(keys, at, Q_TILE)
        state = fold(empty_state(), score(q, key, causal), value_t)

        def earlier(tile, state):
            key, value_t = read_keys(keys, pl.multiple_of(tile * Q_TILE, Q_TILE), Q_TILE)
            return fold(state, score(q, key), value_t)

        store_state(lax.fori_loop(0, place, earlier, state), state_ref)

    whole = constant_spec((rows, HD))
    whole_kv = constant_spec((rows, 2 * HD))
    return pl.pallas_call(
        kernel,
        grid_spec=pltpu.PrefetchScalarGridSpec(
            num_scalar_prefetch=1,
            grid=(tiles,),
            in_specs=[whole, whole, whole_kv, whole_kv],
            out_specs=pl.BlockSpec(
                (1, STATE_ROWS, Q_TILE),
                lambda i, core: ((i + core[0] * per_block) % tiles, 0, 0),
            ),
            scratch_shapes=[
                pltpu.VMEM((2 * rows, 2 * HD), BF),
                pltpu.VMEM((2 * rows, HD), BF),
            ],
        ),
        out_shape=jax.ShapeDtypeStruct((tiles, STATE_ROWS, Q_TILE), F32),
        compiler_params=pltpu.CompilerParams(vmem_limit_bytes=VMEM_BYTES),
        cost_estimate=pl.CostEstimate(
            flops=10 * Q_TILE * Q_TILE * HD * 4,
            bytes_accessed=4 << 20,
            transcendentals=10 * Q_TILE * Q_TILE,
        ),
    )(core, query, query_other, kv, kv_other)


def attend_other(query, query_other, state, sources, use, last=False):
    rows = query.shape[0]
    per_block = rows // Q_TILE
    tiles = 2 * per_block
    count = len(sources)

    def kernel(use_ref, query_ref, query_other_ref, before_ref, *refs):
        source_refs = refs[:count]
        *out_refs, after, q_ref = refs[count:]
        tile = pl.program_id(0)

        @pl.when(tile < per_block)
        def _():
            q_ref[...] = query_ref[...]

        @pl.when(tile >= per_block)
        def _():
            q_ref[...] = query_other_ref[...]

        q = q_ref[...]
        after[...] = before_ref[...]

        def fold_in(refs):
            parts = [(ref, at) for ref in refs for at in range(0, rows, K_TILE)]
            state = load_state(after)
            scores = None
            for i, (ref, at) in enumerate(parts):
                key, value_t = read_keys(ref, at, K_TILE)
                if scores is None:
                    scores = score(q, key)
                later = None
                if i + 1 < len(parts):
                    next_ref, next_at = parts[i + 1]
                    later = score(q, next_ref[next_at : next_at + K_TILE, :HD])
                state = fold(state, scores, value_t)
                scores = later
            store_state(state, after)

        all_used = use_ref[0]
        for i in range(1, count):
            all_used = all_used & use_ref[i]

        @pl.when(all_used != 0)
        def _():
            fold_in(source_refs)

        for i, source_ref in enumerate(source_refs):

            @pl.when((all_used == 0) & (use_ref[i] != 0))
            def _(source_ref=source_ref):
                fold_in([source_ref])

        if last:
            _, total, summed = load_state(after)
            attended = (summed / total).T.astype(BF)
            for part, out_ref in enumerate(out_refs):

                @pl.when(tile // per_block == part)
                def _(out_ref=out_ref):
                    at = pl.multiple_of(tile % per_block * Q_TILE, Q_TILE)
                    out_ref[pl.ds(at, Q_TILE), :] = attended

        else:
            out_refs[0][...] = after[...]

    state_spec = pl.BlockSpec((1, STATE_ROWS, Q_TILE), lambda i, use: (i, 0, 0))
    if last:
        out_shape = (jax.ShapeDtypeStruct((rows, HD), BF),) * 2
        out_specs = (constant_spec((rows, HD)),) * 2
    else:
        out_shape = jax.ShapeDtypeStruct((tiles, STATE_ROWS, Q_TILE), F32)
        out_specs = state_spec
    return pl.pallas_call(
        kernel,
        grid_spec=pltpu.PrefetchScalarGridSpec(
            num_scalar_prefetch=1,
            grid=(tiles,),
            in_specs=[
                pl.BlockSpec((Q_TILE, HD), lambda i, use: (jnp.minimum(i, per_block - 1), 0)),
                pl.BlockSpec((Q_TILE, HD), lambda i, use: (jnp.maximum(i - per_block, 0), 0)),
                state_spec,
            ]
            + [constant_spec(source.shape) for source in sources],
            out_specs=out_specs,
            scratch_shapes=[
                pltpu.VMEM((1, STATE_ROWS, Q_TILE), F32),
                pltpu.VMEM((Q_TILE, HD), BF),
            ],
        ),
        out_shape=out_shape,
        compiler_params=pltpu.CompilerParams(vmem_limit_bytes=VMEM_BYTES),
        cost_estimate=pl.CostEstimate(
            flops=2 * rows * count * rows * HD * 4,
            bytes_accessed=6 << 20,
            transcendentals=2 * rows * count * rows,
        ),
    )(use, query, query_other, state, *sources)


def output_part(own, other, w_out, table, seg, sizes):
    steps = table.shape[0] // 2
    rows = own.shape[0]
    width = 2 * HD
    first_of = [sum(max(size, 1) for size in sizes[:i]) for i in range(len(sizes))]

    def kernel(table_ref, seg_ref, own_ref, other_ref, *refs):
        weight_refs = refs[:2]
        *out_refs, attended, left, total = refs[2:]
        step = pl.program_id(0)

        @pl.when(step == 0)
        def _():
            core = seg_ref[2 * MODALITIES]

            @pl.when(core == 0)
            def _():
                attended[:, :HD] = own_ref[...]
                attended[:, HD:] = other_ref[...]

            @pl.when(core == 1)
            def _():
                attended[:, :HD] = other_ref[...]
                attended[:, HD:] = own_ref[...]

            def mask(kind, at, keep):
                left[kind] = jnp.where(keep, attended[at, :], jnp.zeros((), BF))

            for_runs(seg_ref, rows, mask)

        total[...] = jnp.zeros_like(total)

        def run(kind, at, keep):
            right = jnp.concatenate([ref[kind] for ref in weight_refs], axis=1)
            total[at, :] += jnp.dot(left[kind], right, preferred_element_type=F32)

        for_runs(seg_ref, rows, run)
        for size, first, out_ref in zip(sizes, first_of, out_refs):

            @pl.when(step == first // 2)
            def _(size=size, first=first, out_ref=out_ref):
                for i in range(max(size, 1)):
                    at = (first + i) % 2 * width
                    result = total[:, at : at + width].astype(BF)
                    if size:
                        out_ref[i] = result
                    else:
                        out_ref[...] = result

    shapes = [(size, rows, width) if size else (rows, width) for size in sizes]
    return pl.pallas_call(
        kernel,
        grid_spec=pltpu.PrefetchScalarGridSpec(
            num_scalar_prefetch=2,
            grid=(steps,),
            in_specs=[constant_spec((rows, HD))] * 2
            + [
                pl.BlockSpec(
                    (MODALITIES, width, width), lambda k, t, s, i=i: (0, 0, t[2 * k + i])
                )
                for i in range(2)
            ],
            out_specs=tuple(constant_spec(shape) for shape in shapes),
            scratch_shapes=[
                pltpu.VMEM((rows, width), BF),
                pltpu.VMEM((MODALITIES, WINDOW, width), BF),
                pltpu.VMEM((rows, 2 * width), F32),
            ],
        ),
        out_shape=tuple(jax.ShapeDtypeStruct(shape, BF) for shape in shapes),
        compiler_params=pltpu.CompilerParams(vmem_limit_bytes=VMEM_BYTES),
        cost_estimate=pl.CostEstimate(
            flops=2 * 3 * WINDOW * steps * 2 * width * width,
            bytes_accessed=steps * 2 * (3 * width * width + rows * width) * 2,
            transcendentals=0,
        ),
    )(table, seg, own, other, w_out, w_out)


def add(*arrays):
    return sum(array.astype(F32) for array in arrays).astype(BF)


def local(tokens, modality, w_query, w_key, w_value, w_out):
    seg = segment_scalars(modality)
    core = seg[2 * MODALITIES :]
    weights = (w_key, w_value, w_query)

    low = jnp.stack([tokens, move(tokens, True, 1)])
    high = jnp.stack([move(tokens, True, -1), move(tokens, True, 2)])
    squares = sum(jnp.sum(jnp.square(half.astype(F32)), axis=(0, 2)) for half in (low, high))
    low, high, squares = lax.optimization_barrier((low, high, squares))
    total = squares + move(squares, False, 1) + move(squares, False, -1) + move(squares, False, 2)
    scale = lax.rsqrt(total / 4096.0 + EPS)[:, None]
    before_low = move(low, False, 1)
    after_high = move(high, False, -1)
    before_high = move(high, False, 1)
    after_low = move(low, False, -1)
    far_low = move(before_low, False, 1)
    far_high = move(after_high, False, -1)
    table = shard_table(np.tile(OFFSETS, 4), np.repeat(OFFSETS, 4))
    early = jnp.concatenate([table[:6], table[10:12]])
    partial = project([low, high, before_low, after_high], scale, weights, early, seg)
    partial = project([before_high, after_low], scale, weights, table[6:10], seg, before=partial)
    query, kv, query_send, kv_send = project(
        [far_low, far_high], scale, weights, table[12:], seg, before=partial, last=True
    )

    kv_other = swap_core(kv_send)
    query_other = swap_core(query_send)
    kv_before = move_x(kv, 1)
    kv_other_after = move_x(kv_other, -1)
    kv_other_before = move_x(kv_other, 1)
    kv_after = move_x(kv, -1)
    kv_far = move_x(kv_before, 1)
    kv_other_far = move_x(kv_other_after, -1)
    chip = lax.axis_index("ctx") // 2
    near_use = jnp.stack([chip >= 1, chip == 3]).astype(jnp.int32)
    far_use = jnp.stack([chip >= 2, chip >= 2]).astype(jnp.int32)
    queries = (query, query_other)
    state = attend_own(*queries, kv, kv_other, core)
    state = attend_other(*queries, state, [kv_before, kv_other_after], near_use)
    state = attend_other(*queries, state, [kv_other_before, kv_after], near_use)
    own, own_send = attend_other(*queries, state, [kv_far, kv_other_far], far_use, last=True)
    other = swap_core(own_send)

    part = functools.partial(output_part, own, other, w_out)
    here, plus, two, minus = (shard_table(np.full(4, offset), np.arange(4)) for offset in range(4))
    two_low, two_high = part(two, seg, (2, 2))
    plus_high, minus_low = part(jnp.concatenate([plus[2:], minus[:2]]), seg, (2, 2))
    two_low = move(two_low, True, 1)
    two_high = move(two_high, True, -1)
    plus_high = move(plus_high, True, 1)
    minus_low = move(minus_low, True, -1)
    plus_low, minus_high, *here = part(
        jnp.concatenate([plus[:2], minus[2:], here]), seg, (2, 2, 0, 0, 0, 0)
    )
    plus_low = move(add(plus_low, two_low), True, 1)
    minus_high = move(add(minus_high, two_high), True, -1)
    mine, plus, two, minus = (
        add(here[i], (plus_low, plus_high)[i // 2][i % 2], (minus_low, minus_high)[i // 2][i % 2])
        for i in range(4)
    )
    return add(
        tokens, mine, move(plus, False, 1), move(two, False, 2), move(minus, False, -1)
    )


def solution(mesh):
    in_specs = (
        P("ctx", "tp"),
        P("ctx"),
        P(None, None, "tp"),
        P(None, None, "tp"),
        P(None, None, "tp"),
        P(None, "tp", None),
    )
    return jax.shard_map(
        local, mesh=mesh, in_specs=in_specs, out_specs=P("ctx", "tp"), check_vma=False
    )
```

```python
import functools
import math

import jax
import jax.numpy as jnp
import numpy as np
from jax import lax
from jax.experimental import pallas as pl
from jax.experimental.pallas import tpu as pltpu
from jax.sharding import PartitionSpec as P

HD = 128
MODALITIES = 3
EPS = 1e-05
WINDOW = 528
ALIGN = 16
Q_TILE = 512
K_TILE = 1024
STATE_ROWS = HD + 16
AXES = ("ctx", "tp")
BF = jnp.bfloat16
F32 = jnp.float32
OFFSETS = np.array([0, 3, 1, 2])
VMEM_BYTES = 56 * 1024 * 1024
FEATURES = 4096
HEADROOM = 2.0**-13


def plane_perm(first, step):
    pairs = []
    for ctx in range(8):
        for z in range(4):
            for y in range(4):
                along_y = (ctx % 2 == 0) == first
                to_z = z if along_y else (z + step) % 4
                to_y = (y + step) % 4 if along_y else y
                pairs.append((ctx * 16 + z * 4 + y, ctx * 16 + to_z * 4 + to_y))
    return pairs


def move(array, first, step):
    return lax.ppermute(array, AXES, plane_perm(first, step))


def move_x(array, step):
    pairs = [(x * 2 + c, ((x + step) % 4) * 2 + c) for x in range(4) for c in range(2)]
    return lax.ppermute(array, "ctx", pairs)


def swap_core(array):
    return lax.ppermute(array, "ctx", [(i, i ^ 1) for i in range(8)])


def shard_table(first_offsets, second_offsets):
    core = lax.axis_index("ctx") % 2
    tp = lax.axis_index("tp")
    z, y = tp // 4, tp % 4
    first_offsets = jnp.asarray(first_offsets, jnp.int32)
    second_offsets = jnp.asarray(second_offsets, jnp.int32)
    first = (jnp.where(core == 0, y, z) + first_offsets) % 4
    second = (jnp.where(core == 0, z, y) + second_offsets) % 4
    return jnp.where(core == 0, second * 4 + first, first * 4 + second).astype(jnp.int32)


def segment_scalars(modality):
    rows = modality.shape[0]
    kinds = jnp.arange(MODALITIES, dtype=jnp.int32)[:, None]
    member = modality[None, :] == kinds
    positions = jnp.arange(rows, dtype=jnp.int32)[None, :]
    begin = jnp.min(jnp.where(member, positions, rows), axis=1)
    end = jnp.max(jnp.where(member, positions + 1, 0), axis=1)
    end = jnp.maximum(end, begin)
    core = lax.axis_index("ctx") % 2
    return jnp.concatenate([begin, end, core[None]]).astype(jnp.int32)


def for_runs(seg_ref, rows, body):
    for kind in range(MODALITIES):
        begin = seg_ref[kind]
        end = seg_ref[MODALITIES + kind]
        first = jnp.minimum(begin // ALIGN * ALIGN, rows - WINDOW)
        first = pl.multiple_of(first, ALIGN)
        positions = first + lax.broadcasted_iota(jnp.int32, (WINDOW, 1), 0)
        body(kind, pl.ds(first, WINDOW), (positions >= begin) & (positions < end))


def constant_spec(shape):
    return pl.BlockSpec(shape, lambda k, *scalars: (0,) * len(shape))


def project(pieces, weights, table, seg, before=None, last=False):
    count = len(pieces)
    shards, rows, width = pieces[0].shape
    depth = count * shards
    has_before = before is not None

    def kernel(table_ref, seg_ref, *refs):
        piece_refs = refs[:count]
        weight_refs = refs[count : count + 3]
        refs = refs[count + 3 :]
        if has_before:
            squares_before_ref, before_ref, *refs = refs
        if last:
            query_ref, kv_ref, query_send_ref, kv_send_ref, *refs = refs
        else:
            squares_ref, out_ref, *refs = refs
        held, left, right, total, scale, piece_sem, weight_sem, total_sem = refs

        piece_copies = [
            pltpu.make_async_copy(piece_refs[i], held.at[i], piece_sem.at[i]) for i in range(count)
        ]
        weight_copies = []
        total_copies = []
        for i in range(3):
            for j in range(depth):
                first = pl.multiple_of(table_ref[j] * width, width)
                weight_copies.append(
                    pltpu.make_async_copy(
                        weight_refs[i].at[:, pl.ds(first, width), :],
                        right.at[i, :, pl.ds(j * width, width), :],
                        weight_sem.at[i, j],
                    )
                )
            if has_before:
                total_copies.append(
                    pltpu.make_async_copy(before_ref.at[i], total.at[i], total_sem.at[i])
                )
        for copy in piece_copies:
            copy.start()
        for i in range(3):
            if has_before:
                total_copies[i].start()
            for copy in weight_copies[i * depth : (i + 1) * depth]:
                copy.start()

        squares = squares_before_ref[...] if has_before else jnp.zeros((rows, 1), F32)
        if has_before:
            scale_before = lax.rsqrt(squares / FEATURES + EPS)
        by_lane = jnp.zeros((rows, HD), F32)
        for i in range(count):
            piece_copies[i].wait()
            for j in range(shards):
                for at in range(0, width, HD):
                    by_lane += jnp.square(held[i, j, :, at : at + HD].astype(F32))
        squares += jnp.sum(by_lane, axis=1, keepdims=True)
        scale_now = lax.rsqrt(squares / FEATURES + EPS)
        scale[...] = scale_now * HEADROOM
        if not last:
            squares_ref[...] = squares
        if has_before:
            shrink = jnp.where(scale_before > 0.0, scale_now / scale_before, 0.0)

        def norm(kind, at, keep):
            row_scale = jnp.where(keep, scale[at, :], 0.0)
            for j in range(depth):
                piece = held[j // shards, j % shards, at, :].astype(F32)
                left[kind, :, j * width : (j + 1) * width] = (piece * row_scale).astype(BF)

        for_runs(seg_ref, rows, norm)

        out_copies = []
        for i in range(3):
            if has_before:
                total_copies[i].wait()
                total[i] = total[i] * shrink
            else:
                total[i] = jnp.zeros((rows, width), F32)
            for copy in weight_copies[i * depth : (i + 1) * depth]:
                copy.wait()

            def run(kind, at, keep, i=i):
                total[i, at, :] += jnp.dot(left[kind], right[i, kind], preferred_element_type=F32)

            for_runs(seg_ref, rows, run)
            if not last:
                out_copies.append(
                    pltpu.make_async_copy(total.at[i], out_ref.at[i], total_sem.at[3 + i])
                )
                out_copies[i].start()
        for copy in out_copies:
            copy.wait()

        if last:
            query_scale = math.log2(math.e) / math.sqrt(HD) / HEADROOM
            core = seg_ref[2 * MODALITIES]
            for mine in range(2):

                @pl.when(core == mine)
                def _(mine=mine):
                    for head, q_out, kv_out in (
                        (mine, query_ref, kv_ref),
                        (1 - mine, query_send_ref, kv_send_ref),
                    ):
                        at = slice(head * HD, (head + 1) * HD)
                        kv_out[:, :HD] = (total[0, :, at] / HEADROOM).astype(BF)
                        for row in range(0, rows, HD):
                            block = total[1, row : row + HD, at] / HEADROOM
                            kv_out[row : row + HD, HD:] = block.T.astype(BF)
                        q_out[...] = (total[2, :, at] * query_scale).astype(BF)

    vmem = pl.BlockSpec(memory_space=pltpu.VMEM)
    operands = [table, seg, *pieces, *weights]
    in_specs = [pl.BlockSpec(memory_space=pltpu.SMEM)] * 2
    in_specs += [pl.BlockSpec(memory_space=pl.ANY)] * count
    in_specs += [pl.BlockSpec(memory_space=pltpu.HBM)] * 3
    if has_before:
        operands += before
        in_specs += [vmem, pl.BlockSpec(memory_space=pl.ANY)]
    if last:
        shapes = [(rows, HD), (rows, 2 * HD)] * 2
        out_shape = tuple(jax.ShapeDtypeStruct(shape, BF) for shape in shapes)
        out_specs = (vmem,) * 4
    else:
        out_shape = (
            jax.ShapeDtypeStruct((rows, 1), F32),
            jax.ShapeDtypeStruct((3, rows, width), F32),
        )
        out_specs = (vmem, pl.BlockSpec(memory_space=pl.ANY))
    return pl.pallas_call(
        kernel,
        in_specs=in_specs,
        out_specs=out_specs,
        scratch_shapes=[
            pltpu.VMEM((count, shards, rows, width), BF),
            pltpu.VMEM((MODALITIES, WINDOW, depth * width), BF),
            pltpu.VMEM((3, MODALITIES, depth * width, width), BF),
            pltpu.VMEM((3, rows, width), F32),
            pltpu.VMEM((rows, 1), F32),
            pltpu.SemaphoreType.DMA((count,)),
            pltpu.SemaphoreType.DMA((3, depth)),
            pltpu.SemaphoreType.DMA((6,)),
        ],
        out_shape=out_shape,
        compiler_params=pltpu.CompilerParams(vmem_limit_bytes=VMEM_BYTES),
        cost_estimate=pl.CostEstimate(
            flops=2 * depth * 3 * WINDOW * width * 3 * width,
            bytes_accessed=depth * (rows * width * 2 + 9 * width * width * 2),
            transcendentals=0,
        ),
    )(*operands)


def score(query, key, keep=None):
    scores = lax.dot_general(key, query, (((1,), (1,)), ((), ())), preferred_element_type=F32)
    return scores if keep is None else jnp.where(keep, scores, -1e30)


def fold(state, scores, value_t):
    top, total, summed = state
    new_top = jnp.maximum(top, jnp.max(scores, axis=0, keepdims=True))
    factor = jnp.exp2(top - new_top)
    weights = jnp.exp2(scores - new_top)
    total = total * factor + jnp.sum(weights, axis=0, keepdims=True)
    summed = summed * factor + jnp.dot(value_t, weights.astype(BF), preferred_element_type=F32)
    return new_top, total, summed


def empty_state():
    return (
        jnp.full((1, Q_TILE), -1e30, F32),
        jnp.zeros((1, Q_TILE), F32),
        jnp.zeros((HD, Q_TILE), F32),
    )


def store_state(state, state_ref):
    top, total, summed = state
    state_ref[0, :HD, :] = summed
    state_ref[0, HD : HD + 8, :] = jnp.broadcast_to(top, (8, Q_TILE))
    state_ref[0, HD + 8 :, :] = jnp.broadcast_to(total, (8, Q_TILE))


def load_state(state_ref):
    return (
        state_ref[0, HD : HD + 1, :],
        state_ref[0, HD + 8 : HD + 9, :],
        state_ref[0, :HD, :],
    )


def read_keys(ref, first, count):
    key = ref[pl.ds(first, count), :HD]
    blocks = [ref[pl.ds(first + i, HD), HD:] for i in range(0, count, HD)]
    return key, jnp.concatenate(blocks, axis=1)


def attend_own(query, query_other, kv, kv_other, core):
    rows = query.shape[0]
    per_block = rows // Q_TILE
    tiles = 2 * per_block

    def kernel(core_ref, query_ref, query_other_ref, kv_ref, kv_other_ref, state_ref, keys, both):
        place = pl.program_id(0)

        @pl.when(place == 0)
        def _():
            for mine in range(2):

                @pl.when(core_ref[0] == mine)
                def _(mine=mine):
                    at, other = mine * rows, (1 - mine) * rows
                    keys[at : at + rows, :] = kv_ref[...]
                    keys[other : other + rows, :] = kv_other_ref[...]
                    both[at : at + rows, :] = query_ref[...]
                    both[other : other + rows, :] = query_other_ref[...]

        at = pl.multiple_of(place * Q_TILE, Q_TILE)
        q = both[pl.ds(at, Q_TILE), :]
        causal = lax.broadcasted_iota(
            jnp.int32, (Q_TILE, Q_TILE), 0
        ) <= lax.broadcasted_iota(jnp.int32, (Q_TILE, Q_TILE), 1)
        key, value_t = read_keys(keys, at, Q_TILE)
        state = fold(empty_state(), score(q, key, causal), value_t)

        def earlier(tile, state):
            key, value_t = read_keys(keys, pl.multiple_of(tile * Q_TILE, Q_TILE), Q_TILE)
            return fold(state, score(q, key), value_t)

        store_state(lax.fori_loop(0, place, earlier, state), state_ref)

    whole = constant_spec((rows, HD))
    whole_kv = constant_spec((rows, 2 * HD))
    return pl.pallas_call(
        kernel,
        grid_spec=pltpu.PrefetchScalarGridSpec(
            num_scalar_prefetch=1,
            grid=(tiles,),
            in_specs=[whole, whole, whole_kv, whole_kv],
            out_specs=pl.BlockSpec(
                (1, STATE_ROWS, Q_TILE),
                lambda i, core: ((i + core[0] * per_block) % tiles, 0, 0),
            ),
            scratch_shapes=[
                pltpu.VMEM((2 * rows, 2 * HD), BF),
                pltpu.VMEM((2 * rows, HD), BF),
            ],
        ),
        out_shape=jax.ShapeDtypeStruct((tiles, STATE_ROWS, Q_TILE), F32),
        compiler_params=pltpu.CompilerParams(vmem_limit_bytes=VMEM_BYTES),
        cost_estimate=pl.CostEstimate(
            flops=10 * Q_TILE * Q_TILE * HD * 4,
            bytes_accessed=4 << 20,
            transcendentals=10 * Q_TILE * Q_TILE,
        ),
    )(core, query, query_other, kv, kv_other)


def attend_other(query, query_other, state, sources, use, last=False):
    rows = query.shape[0]
    per_block = rows // Q_TILE
    tiles = 2 * per_block
    count = len(sources)

    def kernel(use_ref, query_ref, query_other_ref, before_ref, *refs):
        source_refs = refs[:count]
        *out_refs, after, q_ref = refs[count:]
        tile = pl.program_id(0)

        @pl.when(tile < per_block)
        def _():
            q_ref[...] = query_ref[...]

        @pl.when(tile >= per_block)
        def _():
            q_ref[...] = query_other_ref[...]

        q = q_ref[...]
        after[...] = before_ref[...]

        def fold_in(refs):
            parts = [(ref, at) for ref in refs for at in range(0, rows, K_TILE)]
            state = load_state(after)
            scores = None
            for i, (ref, at) in enumerate(parts):
                key, value_t = read_keys(ref, at, K_TILE)
                if scores is None:
                    scores = score(q, key)
                later = None
                if i + 1 < len(parts):
                    next_ref, next_at = parts[i + 1]
                    later = score(q, next_ref[next_at : next_at + K_TILE, :HD])
                state = fold(state, scores, value_t)
                scores = later
            store_state(state, after)

        all_used = use_ref[0]
        for i in range(1, count):
            all_used = all_used & use_ref[i]

        @pl.when(all_used != 0)
        def _():
            fold_in(source_refs)

        for i, source_ref in enumerate(source_refs):

            @pl.when((all_used == 0) & (use_ref[i] != 0))
            def _(source_ref=source_ref):
                fold_in([source_ref])

        if last:
            _, total, summed = load_state(after)
            attended = (summed / total).T.astype(BF)
            for part, out_ref in enumerate(out_refs):

                @pl.when(tile // per_block == part)
                def _(out_ref=out_ref):
                    at = pl.multiple_of(tile % per_block * Q_TILE, Q_TILE)
                    out_ref[pl.ds(at, Q_TILE), :] = attended

        else:
            out_refs[0][...] = after[...]

    state_spec = pl.BlockSpec((1, STATE_ROWS, Q_TILE), lambda i, use: (i, 0, 0))
    if last:
        out_shape = (jax.ShapeDtypeStruct((rows, HD), BF),) * 2
        out_specs = (constant_spec((rows, HD)),) * 2
    else:
        out_shape = jax.ShapeDtypeStruct((tiles, STATE_ROWS, Q_TILE), F32)
        out_specs = state_spec
    return pl.pallas_call(
        kernel,
        grid_spec=pltpu.PrefetchScalarGridSpec(
            num_scalar_prefetch=1,
            grid=(tiles,),
            in_specs=[
                pl.BlockSpec((Q_TILE, HD), lambda i, use: (jnp.minimum(i, per_block - 1), 0)),
                pl.BlockSpec((Q_TILE, HD), lambda i, use: (jnp.maximum(i - per_block, 0), 0)),
                state_spec,
            ]
            + [constant_spec(source.shape) for source in sources],
            out_specs=out_specs,
            scratch_shapes=[
                pltpu.VMEM((1, STATE_ROWS, Q_TILE), F32),
                pltpu.VMEM((Q_TILE, HD), BF),
            ],
        ),
        out_shape=out_shape,
        compiler_params=pltpu.CompilerParams(vmem_limit_bytes=VMEM_BYTES),
        cost_estimate=pl.CostEstimate(
            flops=2 * rows * count * rows * HD * 4,
            bytes_accessed=6 << 20,
            transcendentals=2 * rows * count * rows,
        ),
    )(use, query, query_other, state, *sources)


def output_part(own, other, w_out, table, seg, sizes):
    steps = table.shape[0] // 2
    rows = own.shape[0]
    width = 2 * HD
    first_of = [sum(max(size, 1) for size in sizes[:i]) for i in range(len(sizes))]

    def kernel(table_ref, seg_ref, own_ref, other_ref, *refs):
        weight_refs = refs[:2]
        *out_refs, attended, left, total = refs[2:]
        step = pl.program_id(0)

        @pl.when(step == 0)
        def _():
            core = seg_ref[2 * MODALITIES]

            @pl.when(core == 0)
            def _():
                attended[:, :HD] = own_ref[...]
                attended[:, HD:] = other_ref[...]

            @pl.when(core == 1)
            def _():
                attended[:, :HD] = other_ref[...]
                attended[:, HD:] = own_ref[...]

            def mask(kind, at, keep):
                left[kind] = jnp.where(keep, attended[at, :], jnp.zeros((), BF))

            for_runs(seg_ref, rows, mask)

        total[...] = jnp.zeros_like(total)

        def run(kind, at, keep):
            right = jnp.concatenate([ref[kind] for ref in weight_refs], axis=1)
            total[at, :] += jnp.dot(left[kind], right, preferred_element_type=F32)

        for_runs(seg_ref, rows, run)
        for size, first, out_ref in zip(sizes, first_of, out_refs):

            @pl.when(step == first // 2)
            def _(size=size, first=first, out_ref=out_ref):
                for i in range(max(size, 1)):
                    at = (first + i) % 2 * width
                    result = total[:, at : at + width].astype(BF)
                    if size:
                        out_ref[i] = result
                    else:
                        out_ref[...] = result

    shapes = [(size, rows, width) if size else (rows, width) for size in sizes]
    return pl.pallas_call(
        kernel,
        grid_spec=pltpu.PrefetchScalarGridSpec(
            num_scalar_prefetch=2,
            grid=(steps,),
            in_specs=[constant_spec((rows, HD))] * 2
            + [
                pl.BlockSpec(
                    (MODALITIES, width, width), lambda k, t, s, i=i: (0, 0, t[2 * k + i])
                )
                for i in range(2)
            ],
            out_specs=tuple(constant_spec(shape) for shape in shapes),
            scratch_shapes=[
                pltpu.VMEM((rows, width), BF),
                pltpu.VMEM((MODALITIES, WINDOW, width), BF),
                pltpu.VMEM((rows, 2 * width), F32),
            ],
        ),
        out_shape=tuple(jax.ShapeDtypeStruct(shape, BF) for shape in shapes),
        compiler_params=pltpu.CompilerParams(vmem_limit_bytes=VMEM_BYTES),
        cost_estimate=pl.CostEstimate(
            flops=2 * 3 * WINDOW * steps * 2 * width * width,
            bytes_accessed=steps * 2 * (3 * width * width + rows * width) * 2,
            transcendentals=0,
        ),
    )(table, seg, own, other, w_out, w_out)


def add(*arrays):
    return sum(array.astype(F32) for array in arrays).astype(BF)


def local(tokens, modality, w_query, w_key, w_value, w_out):
    seg = segment_scalars(modality)
    core = seg[2 * MODALITIES :]
    weights = (w_key, w_value, w_query)

    low = jnp.stack([tokens, move(tokens, True, 1)])
    high = jnp.stack([move(tokens, True, -1), move(tokens, True, 2)])
    before_low = move(low, False, 1)
    after_high = move(high, False, -1)
    before_high = move(high, False, 1)
    after_low = move(low, False, -1)
    table = shard_table(np.tile(OFFSETS, 4), np.repeat(OFFSETS, 4))
    partial = project([low, high], weights, table[:4], seg)
    before_low, after_high, partial = lax.optimization_barrier((before_low, after_high, partial))
    far_low = move(before_low, False, 1)
    far_high = move(after_high, False, -1)
    first = jnp.concatenate([table[4:6], table[10:12]])
    partial = project([before_low, after_high], weights, first, seg, before=partial)
    partial = project([before_high, after_low], weights, table[6:10], seg, before=partial)
    query, kv, query_send, kv_send = project(
        [far_low, far_high], weights, table[12:], seg, before=partial, last=True
    )

    kv_other = swap_core(kv_send)
    query_other = swap_core(query_send)
    kv_before = move_x(kv, 1)
    kv_other_after = move_x(kv_other, -1)
    kv_other_before = move_x(kv_other, 1)
    kv_after = move_x(kv, -1)
    kv_far = move_x(kv_before, 1)
    kv_other_far = move_x(kv_other_after, -1)
    chip = lax.axis_index("ctx") // 2
    near_use = jnp.stack([chip >= 1, chip == 3]).astype(jnp.int32)
    far_use = jnp.stack([chip >= 2, chip >= 2]).astype(jnp.int32)
    queries = (query, query_other)
    state = attend_own(*queries, kv, kv_other, core)
    state = attend_other(*queries, state, [kv_before, kv_other_after], near_use)
    state = attend_other(*queries, state, [kv_other_before, kv_after], near_use)
    own, own_send = attend_other(*queries, state, [kv_far, kv_other_far], far_use, last=True)
    other = swap_core(own_send)

    part = functools.partial(output_part, own, other, w_out)
    here, plus, two, minus = (shard_table(np.full(4, offset), np.arange(4)) for offset in range(4))
    two_low, two_high = part(two, seg, (2, 2))
    plus_high, minus_low = part(jnp.concatenate([plus[2:], minus[:2]]), seg, (2, 2))
    two_low = move(two_low, True, 1)
    two_high = move(two_high, True, -1)
    plus_high = move(plus_high, True, 1)
    minus_low = move(minus_low, True, -1)
    plus_low, minus_high, *here = part(
        jnp.concatenate([plus[:2], minus[2:], here]), seg, (2, 2, 0, 0, 0, 0)
    )
    plus_low = move(add(plus_low, two_low), True, 1)
    minus_high = move(add(minus_high, two_high), True, -1)
    mine, plus, two, minus = (
        add(here[i], (plus_low, plus_high)[i // 2][i % 2], (minus_low, minus_high)[i // 2][i % 2])
        for i in range(4)
    )
    return add(
        tokens, mine, move(plus, False, 1), move(two, False, 2), move(minus, False, -1)
    )


def solution(mesh):
    in_specs = (
        P("ctx", "tp"),
        P("ctx"),
        P(None, None, "tp"),
        P(None, None, "tp"),
        P(None, None, "tp"),
        P(None, "tp", None),
    )
    return jax.shard_map(
        local, mesh=mesh, in_specs=in_specs, out_specs=P("ctx", "tp"), check_vma=False
    )
```

```python
import functools
import math

import jax
import jax.numpy as jnp
import numpy as np
from jax import lax
from jax.experimental import pallas as pl
from jax.experimental.pallas import tpu as pltpu
from jax.sharding import PartitionSpec as P

HD = 128
MODALITIES = 3
EPS = 1e-05
WINDOW = 528
ALIGN = 16
Q_TILE = 512
K_TILE = 1024
STATE_ROWS = HD + 16
AXES = ("ctx", "tp")
BF = jnp.bfloat16
F32 = jnp.float32
OFFSETS = np.array([0, 3, 1, 2])
VMEM_PROJECT = 56 * 1024 * 1024
VMEM_BYTES = 24 * 1024 * 1024
FEATURES = 4096
HEADROOM = 2.0**-13


def plane_perm(first, step):
    pairs = []
    for ctx in range(8):
        for z in range(4):
            for y in range(4):
                along_y = (ctx % 2 == 0) == first
                to_z = z if along_y else (z + step) % 4
                to_y = (y + step) % 4 if along_y else y
                pairs.append((ctx * 16 + z * 4 + y, ctx * 16 + to_z * 4 + to_y))
    return pairs


def move(array, first, step):
    return lax.ppermute(array, AXES, plane_perm(first, step))


def move_x(array, step):
    pairs = [(x * 2 + c, ((x + step) % 4) * 2 + c) for x in range(4) for c in range(2)]
    return lax.ppermute(array, "ctx", pairs)


def swap_core(array):
    return lax.ppermute(array, "ctx", [(i, i ^ 1) for i in range(8)])


def shard_table(first_offsets, second_offsets):
    core = lax.axis_index("ctx") % 2
    tp = lax.axis_index("tp")
    z, y = tp // 4, tp % 4
    first_offsets = jnp.asarray(first_offsets, jnp.int32)
    second_offsets = jnp.asarray(second_offsets, jnp.int32)
    first = (jnp.where(core == 0, y, z) + first_offsets) % 4
    second = (jnp.where(core == 0, z, y) + second_offsets) % 4
    return jnp.where(core == 0, second * 4 + first, first * 4 + second).astype(jnp.int32)


def segment_scalars(modality):
    rows = modality.shape[0]
    kinds = jnp.arange(MODALITIES, dtype=jnp.int32)[:, None]
    member = modality[None, :] == kinds
    positions = jnp.arange(rows, dtype=jnp.int32)[None, :]
    begin = jnp.min(jnp.where(member, positions, rows), axis=1)
    end = jnp.max(jnp.where(member, positions + 1, 0), axis=1)
    end = jnp.maximum(end, begin)
    core = lax.axis_index("ctx") % 2
    return jnp.concatenate([begin, end, core[None]]).astype(jnp.int32)


def for_runs(seg_ref, rows, body):
    for kind in range(MODALITIES):
        begin = seg_ref[kind]
        end = seg_ref[MODALITIES + kind]
        first = jnp.minimum(begin // ALIGN * ALIGN, rows - WINDOW)
        first = pl.multiple_of(first, ALIGN)
        positions = first + lax.broadcasted_iota(jnp.int32, (WINDOW, 1), 0)
        body(kind, pl.ds(first, WINDOW), (positions >= begin) & (positions < end))


def constant_spec(shape):
    return pl.BlockSpec(shape, lambda k, *scalars: (0,) * len(shape))


def project(pieces, weights, table, seg, before=None, last=False):
    count = len(pieces)
    shards, rows, width = pieces[0].shape
    depth = count * shards
    has_before = before is not None

    def kernel(table_ref, seg_ref, *refs):
        piece_refs = refs[:count]
        weight_refs = refs[count : count + 3]
        refs = refs[count + 3 :]
        if has_before:
            squares_before_ref, before_ref, *refs = refs
        if last:
            query_ref, kv_ref, query_send_ref, kv_send_ref, *refs = refs
        else:
            squares_ref, out_ref, *refs = refs
        held, normed, left, right, total, piece_sem, weight_sem, total_sem = refs

        piece_copies = [
            pltpu.make_async_copy(piece_refs[i], held.at[i], piece_sem.at[i]) for i in range(count)
        ]
        weight_copies = []
        for j in range(depth):
            first = pl.multiple_of(table_ref[j] * width, width)
            for i in range(3):
                weight_copies.append(
                    pltpu.make_async_copy(
                        weight_refs[i].at[:, pl.ds(first, width), :],
                        right.at[:, pl.ds(j * width, width), pl.ds(i * width, width)],
                        weight_sem.at[i, j],
                    )
                )
        for copy in piece_copies:
            copy.start()
        if has_before:
            total_copy = pltpu.make_async_copy(before_ref, total, total_sem.at[0])
            total_copy.start()
        for copy in weight_copies:
            copy.start()
        for copy in piece_copies:
            copy.wait()
        if has_before:
            total_copy.wait()
        else:
            total[...] = jnp.zeros_like(total)

        for row in range(0, rows, HD):
            at = slice(row, row + HD)
            by_lane = jnp.zeros((HD, HD), F32)
            for i in range(count):
                for j in range(shards):
                    for column in range(0, width, HD):
                        by_lane += jnp.square(held[i, j, at, column : column + HD].astype(F32))
            squares = jnp.sum(by_lane, axis=1, keepdims=True)
            if has_before:
                squares_before = squares_before_ref[at, :]
                scale_before = lax.rsqrt(squares_before / FEATURES + EPS)
                squares += squares_before
            scale = lax.rsqrt(squares / FEATURES + EPS)
            if has_before:
                total[at, :] *= jnp.where(scale_before > 0.0, scale / scale_before, 0.0)
            if not last:
                squares_ref[at, :] = squares
            for j in range(depth):
                piece = held[j // shards, j % shards, at, :].astype(F32)
                normed[at, j * width : (j + 1) * width] = (piece * (scale * HEADROOM)).astype(BF)

        def mask(kind, at, keep):
            left[kind] = normed[at, :] * keep.astype(BF)

        for_runs(seg_ref, rows, mask)
        for copy in weight_copies:
            copy.wait()

        def run(kind, at, keep):
            total[at, :] += jnp.dot(left[kind], right[kind], preferred_element_type=F32)

        for_runs(seg_ref, rows, run)
        if not last:
            total_copy = pltpu.make_async_copy(total, out_ref, total_sem.at[1])
            total_copy.start()
            total_copy.wait()

        if last:
            query_scale = math.log2(math.e) / math.sqrt(HD) / HEADROOM
            core = seg_ref[2 * MODALITIES]
            for mine in range(2):

                @pl.when(core == mine)
                def _(mine=mine):
                    for head, q_out, kv_out in (
                        (mine, query_ref, kv_ref),
                        (1 - mine, query_send_ref, kv_send_ref),
                    ):
                        at = head * HD
                        kv_out[:, :HD] = (total[:, at : at + HD] / HEADROOM).astype(BF)
                        at += width
                        for row in range(0, rows, HD):
                            block = total[row : row + HD, at : at + HD] / HEADROOM
                            kv_out[row : row + HD, HD:] = block.T.astype(BF)
                        at += width
                        q_out[...] = (total[:, at : at + HD] * query_scale).astype(BF)

    vmem = pl.BlockSpec(memory_space=pltpu.VMEM)
    operands = [table, seg, *pieces, *weights]
    in_specs = [pl.BlockSpec(memory_space=pltpu.SMEM)] * 2
    in_specs += [pl.BlockSpec(memory_space=pl.ANY)] * count
    in_specs += [pl.BlockSpec(memory_space=pl.ANY)] * 3
    if has_before:
        operands += before
        in_specs += [vmem, pl.BlockSpec(memory_space=pl.ANY)]
    if last:
        shapes = [(rows, HD), (rows, 2 * HD)] * 2
        out_shape = tuple(jax.ShapeDtypeStruct(shape, BF) for shape in shapes)
        out_specs = (vmem,) * 4
    else:
        out_shape = (
            jax.ShapeDtypeStruct((rows, 1), F32),
            jax.ShapeDtypeStruct((rows, 3 * width), F32),
        )
        out_specs = (vmem, pl.BlockSpec(memory_space=pl.ANY))
    return pl.pallas_call(
        kernel,
        in_specs=in_specs,
        out_specs=out_specs,
        scratch_shapes=[
            pltpu.VMEM((count, shards, rows, width), BF),
            pltpu.VMEM((rows, depth * width), BF),
            pltpu.VMEM((MODALITIES, WINDOW, depth * width), BF),
            pltpu.VMEM((MODALITIES, depth * width, 3 * width), BF),
            pltpu.VMEM((rows, 3 * width), F32),
            pltpu.SemaphoreType.DMA((count,)),
            pltpu.SemaphoreType.DMA((3, depth)),
            pltpu.SemaphoreType.DMA((2,)),
        ],
        out_shape=out_shape,
        compiler_params=pltpu.CompilerParams(vmem_limit_bytes=VMEM_PROJECT),
        cost_estimate=pl.CostEstimate(
            flops=2 * depth * 3 * WINDOW * width * 3 * width,
            bytes_accessed=depth * (rows * width * 2 + 9 * width * width * 2),
            transcendentals=0,
        ),
    )(*operands)


def score(query, key, keep=None):
    scores = lax.dot_general(key, query, (((1,), (1,)), ((), ())), preferred_element_type=F32)
    return scores if keep is None else jnp.where(keep, scores, -1e30)


def fold(state, scores, value_t):
    top, total, summed = state
    new_top = jnp.maximum(top, jnp.max(scores, axis=0, keepdims=True))
    factor = jnp.exp2(top - new_top)
    weights = jnp.exp2(scores - new_top)
    total = total * factor + jnp.sum(weights, axis=0, keepdims=True)
    summed = summed * factor + jnp.dot(value_t, weights.astype(BF), preferred_element_type=F32)
    return new_top, total, summed


def empty_state():
    return (
        jnp.full((1, Q_TILE), -1e30, F32),
        jnp.zeros((1, Q_TILE), F32),
        jnp.zeros((HD, Q_TILE), F32),
    )


def store_state(state, state_ref):
    top, total, summed = state
    state_ref[0, :HD, :] = summed
    state_ref[0, HD : HD + 8, :] = jnp.broadcast_to(top, (8, Q_TILE))
    state_ref[0, HD + 8 :, :] = jnp.broadcast_to(total, (8, Q_TILE))


def load_state(state_ref):
    return (
        state_ref[0, HD : HD + 1, :],
        state_ref[0, HD + 8 : HD + 9, :],
        state_ref[0, :HD, :],
    )


def read_keys(ref, first, count):
    key = ref[pl.ds(first, count), :HD]
    blocks = [ref[pl.ds(first + i, HD), HD:] for i in range(0, count, HD)]
    return key, jnp.concatenate(blocks, axis=1)


def attend_own(query, query_other, kv, kv_other, core):
    rows = query.shape[0]
    per_block = rows // Q_TILE
    tiles = 2 * per_block

    def kernel(core_ref, query_ref, query_other_ref, kv_ref, kv_other_ref, state_ref, keys, both):
        place = pl.program_id(0)

        @pl.when(place == 0)
        def _():
            for mine in range(2):

                @pl.when(core_ref[0] == mine)
                def _(mine=mine):
                    at, other = mine * rows, (1 - mine) * rows
                    keys[at : at + rows, :] = kv_ref[...]
                    keys[other : other + rows, :] = kv_other_ref[...]
                    both[at : at + rows, :] = query_ref[...]
                    both[other : other + rows, :] = query_other_ref[...]

        at = pl.multiple_of(place * Q_TILE, Q_TILE)
        q = both[pl.ds(at, Q_TILE), :]
        causal = lax.broadcasted_iota(
            jnp.int32, (Q_TILE, Q_TILE), 0
        ) <= lax.broadcasted_iota(jnp.int32, (Q_TILE, Q_TILE), 1)
        key, value_t = read_keys(keys, at, Q_TILE)
        state = fold(empty_state(), score(q, key, causal), value_t)

        def earlier(tile, state):
            key, value_t = read_keys(keys, pl.multiple_of(tile * Q_TILE, Q_TILE), Q_TILE)
            return fold(state, score(q, key), value_t)

        store_state(lax.fori_loop(0, place, earlier, state), state_ref)

    whole = constant_spec((rows, HD))
    whole_kv = constant_spec((rows, 2 * HD))
    return pl.pallas_call(
        kernel,
        grid_spec=pltpu.PrefetchScalarGridSpec(
            num_scalar_prefetch=1,
            grid=(tiles,),
            in_specs=[whole, whole, whole_kv, whole_kv],
            out_specs=pl.BlockSpec(
                (1, STATE_ROWS, Q_TILE),
                lambda i, core: ((i + core[0] * per_block) % tiles, 0, 0),
            ),
            scratch_shapes=[
                pltpu.VMEM((2 * rows, 2 * HD), BF),
                pltpu.VMEM((2 * rows, HD), BF),
            ],
        ),
        out_shape=jax.ShapeDtypeStruct((tiles, STATE_ROWS, Q_TILE), F32),
        compiler_params=pltpu.CompilerParams(vmem_limit_bytes=VMEM_BYTES),
        cost_estimate=pl.CostEstimate(
            flops=10 * Q_TILE * Q_TILE * HD * 4,
            bytes_accessed=4 << 20,
            transcendentals=10 * Q_TILE * Q_TILE,
        ),
    )(core, query, query_other, kv, kv_other)


def attend_other(query, query_other, state, sources, use, last=False):
    rows = query.shape[0]
    per_block = rows // Q_TILE
    tiles = 2 * per_block
    count = len(sources)

    def kernel(use_ref, query_ref, query_other_ref, before_ref, *refs):
        source_refs = refs[:count]
        *out_refs, after, q_ref = refs[count:]
        tile = pl.program_id(0)

        @pl.when(tile < per_block)
        def _():
            q_ref[...] = query_ref[...]

        @pl.when(tile >= per_block)
        def _():
            q_ref[...] = query_other_ref[...]

        q = q_ref[...]
        after[...] = before_ref[...]

        def fold_in(refs):
            parts = [(ref, at) for ref in refs for at in range(0, rows, K_TILE)]
            state = load_state(after)
            scores = None
            for i, (ref, at) in enumerate(parts):
                key, value_t = read_keys(ref, at, K_TILE)
                if scores is None:
                    scores = score(q, key)
                later = None
                if i + 1 < len(parts):
                    next_ref, next_at = parts[i + 1]
                    later = score(q, next_ref[next_at : next_at + K_TILE, :HD])
                state = fold(state, scores, value_t)
                scores = later
            store_state(state, after)

        all_used = use_ref[0]
        for i in range(1, count):
            all_used = all_used & use_ref[i]

        @pl.when(all_used != 0)
        def _():
            fold_in(source_refs)

        for i, source_ref in enumerate(source_refs):

            @pl.when((all_used == 0) & (use_ref[i] != 0))
            def _(source_ref=source_ref):
                fold_in([source_ref])

        if last:
            _, total, summed = load_state(after)
            attended = (summed / total).T.astype(BF)
            for part, out_ref in enumerate(out_refs):

                @pl.when(tile // per_block == part)
                def _(out_ref=out_ref):
                    at = pl.multiple_of(tile % per_block * Q_TILE, Q_TILE)
                    out_ref[pl.ds(at, Q_TILE), :] = attended

        else:
            out_refs[0][...] = after[...]

    state_spec = pl.BlockSpec((1, STATE_ROWS, Q_TILE), lambda i, use: (i, 0, 0))
    if last:
        out_shape = (jax.ShapeDtypeStruct((rows, HD), BF),) * 2
        out_specs = (constant_spec((rows, HD)),) * 2
    else:
        out_shape = jax.ShapeDtypeStruct((tiles, STATE_ROWS, Q_TILE), F32)
        out_specs = state_spec
    return pl.pallas_call(
        kernel,
        grid_spec=pltpu.PrefetchScalarGridSpec(
            num_scalar_prefetch=1,
            grid=(tiles,),
            in_specs=[
                pl.BlockSpec((Q_TILE, HD), lambda i, use: (jnp.minimum(i, per_block - 1), 0)),
                pl.BlockSpec((Q_TILE, HD), lambda i, use: (jnp.maximum(i - per_block, 0), 0)),
                state_spec,
            ]
            + [constant_spec(source.shape) for source in sources],
            out_specs=out_specs,
            scratch_shapes=[
                pltpu.VMEM((1, STATE_ROWS, Q_TILE), F32),
                pltpu.VMEM((Q_TILE, HD), BF),
            ],
        ),
        out_shape=out_shape,
        compiler_params=pltpu.CompilerParams(vmem_limit_bytes=VMEM_BYTES),
        cost_estimate=pl.CostEstimate(
            flops=2 * rows * count * rows * HD * 4,
            bytes_accessed=6 << 20,
            transcendentals=2 * rows * count * rows,
        ),
    )(use, query, query_other, state, *sources)


def output_part(own, other, w_out, table, seg, sizes):
    blocks = table.shape[0]
    rows = own.shape[0]
    width = 2 * HD

    def kernel(table_ref, seg_ref, own_ref, other_ref, weight_ref, *refs):
        *out_refs, attended, left, right, total, result, weight_sem, out_sem = refs
        weight_copies = []
        for i in range(blocks):
            first = pl.multiple_of(table_ref[i] * width, width)
            weight_copies.append(
                pltpu.make_async_copy(
                    weight_ref.at[:, :, pl.ds(first, width)],
                    right.at[i // 2, :, :, pl.ds(i % 2 * width, width)],
                    weight_sem.at[i],
                )
            )
            weight_copies[i].start()
        core = seg_ref[2 * MODALITIES]
        for mine in range(2):

            @pl.when(core == mine)
            def _(mine=mine):
                attended[:, mine * HD : (mine + 1) * HD] = own_ref[...]
                attended[:, (1 - mine) * HD : (2 - mine) * HD] = other_ref[...]

        def mask(kind, at, keep):
            left[kind] = attended[at, :] * keep.astype(BF)

        for_runs(seg_ref, rows, mask)
        out_copies = []
        for pair in range(blocks // 2):
            weight_copies[2 * pair].wait()
            weight_copies[2 * pair + 1].wait()
            total[...] = jnp.zeros_like(total)

            def run(kind, at, keep, pair=pair):
                total[at, :] += jnp.dot(left[kind], right[pair, kind], preferred_element_type=F32)

            for_runs(seg_ref, rows, run)
            for i in range(2):
                result[2 * pair + i] = total[:, i * width : (i + 1) * width].astype(BF)
            done = 0
            for size, out_ref in zip(sizes, out_refs):
                if done // 2 == pair:
                    source = result.at[pl.ds(done, 2)] if size else result.at[done]
                    out_copies.append(
                        pltpu.make_async_copy(source, out_ref, out_sem.at[len(out_copies)])
                    )
                    out_copies[-1].start()
                done += max(size, 1)
        for copy in out_copies:
            copy.wait()

    vmem = pl.BlockSpec(memory_space=pltpu.VMEM)
    shapes = [(size, rows, width) if size else (rows, width) for size in sizes]
    return pl.pallas_call(
        kernel,
        in_specs=[pl.BlockSpec(memory_space=pltpu.SMEM)] * 2
        + [vmem, vmem, pl.BlockSpec(memory_space=pl.ANY)],
        out_specs=(pl.BlockSpec(memory_space=pl.ANY),) * len(shapes),
        scratch_shapes=[
            pltpu.VMEM((rows, width), BF),
            pltpu.VMEM((MODALITIES, WINDOW, width), BF),
            pltpu.VMEM((blocks // 2, MODALITIES, width, 2 * width), BF),
            pltpu.VMEM((rows, 2 * width), F32),
            pltpu.VMEM((blocks, rows, width), BF),
            pltpu.SemaphoreType.DMA((blocks,)),
            pltpu.SemaphoreType.DMA((len(shapes),)),
        ],
        out_shape=tuple(jax.ShapeDtypeStruct(shape, BF) for shape in shapes),
        compiler_params=pltpu.CompilerParams(vmem_limit_bytes=VMEM_BYTES),
        cost_estimate=pl.CostEstimate(
            flops=2 * 3 * WINDOW * blocks * width * width,
            bytes_accessed=blocks * (3 * width * width + rows * width) * 2,
            transcendentals=0,
        ),
    )(table, seg, own, other, w_out)


def add(*arrays):
    return sum(array.astype(F32) for array in arrays).astype(BF)


def local(tokens, modality, w_query, w_key, w_value, w_out):
    seg = segment_scalars(modality)
    core = seg[2 * MODALITIES :]
    weights = (w_key, w_value, w_query)

    low = jnp.stack([tokens, move(tokens, True, 1)])
    high = jnp.stack([move(tokens, True, -1), move(tokens, True, 2)])
    before_low = move(low, False, 1)
    after_high = move(high, False, -1)
    before_high = move(high, False, 1)
    after_low = move(low, False, -1)
    table = shard_table(np.tile(OFFSETS, 4), np.repeat(OFFSETS, 4))
    partial = project([low, high], weights, table[:4], seg)
    before_low, after_high, partial = lax.optimization_barrier((before_low, after_high, partial))
    far_low = move(before_low, False, 1)
    far_high = move(after_high, False, -1)
    first = jnp.concatenate([table[4:6], table[10:12]])
    partial = project([before_low, after_high], weights, first, seg, before=partial)
    partial = project([before_high, after_low], weights, table[6:10], seg, before=partial)
    query, kv, query_send, kv_send = project(
        [far_low, far_high], weights, table[12:], seg, before=partial, last=True
    )

    kv_other = swap_core(kv_send)
    query_other = swap_core(query_send)
    kv_before = move_x(kv, 1)
    kv_other_after = move_x(kv_other, -1)
    kv_other_before = move_x(kv_other, 1)
    kv_after = move_x(kv, -1)
    chip = lax.axis_index("ctx") // 2
    near_use = jnp.stack([chip >= 1, chip == 3]).astype(jnp.int32)
    far_use = jnp.stack([chip >= 2, chip >= 2]).astype(jnp.int32)
    queries = (query, query_other)
    state = attend_own(*queries, kv, kv_other, core)
    kv_before, kv_other_after, state = lax.optimization_barrier((kv_before, kv_other_after, state))
    kv_far = move_x(kv_before, 1)
    kv_other_far = move_x(kv_other_after, -1)
    state = attend_other(*queries, state, [kv_before, kv_other_after], near_use)
    state = attend_other(*queries, state, [kv_other_before, kv_after], near_use)
    own, own_send = attend_other(*queries, state, [kv_far, kv_other_far], far_use, last=True)
    other = swap_core(own_send)

    part = functools.partial(output_part, own, other, w_out)
    here, plus, two, minus = (shard_table(np.full(4, offset), np.arange(4)) for offset in range(4))
    two_low, two_high = part(two, seg, (2, 2))
    plus_high, minus_low = part(jnp.concatenate([plus[2:], minus[:2]]), seg, (2, 2))
    two_low = move(two_low, True, 1)
    two_high = move(two_high, True, -1)
    plus_high = move(plus_high, True, 1)
    minus_low = move(minus_low, True, -1)
    plus_low, minus_high, *here = part(
        jnp.concatenate([plus[:2], minus[2:], here]), seg, (2, 2, 0, 0, 0, 0)
    )
    plus_low = move(add(plus_low, two_low), True, 1)
    minus_high = move(add(minus_high, two_high), True, -1)
    mine, plus, two, minus = (
        add(here[i], (plus_low, plus_high)[i // 2][i % 2], (minus_low, minus_high)[i // 2][i % 2])
        for i in range(4)
    )
    return add(
        tokens, mine, move(plus, False, 1), move(two, False, 2), move(minus, False, -1)
    )


def solution(mesh):
    in_specs = (
        P("ctx", "tp"),
        P("ctx"),
        P(None, None, "tp"),
        P(None, None, "tp"),
        P(None, None, "tp"),
        P(None, "tp", None),
    )
    return jax.shard_map(
        local, mesh=mesh, in_specs=in_specs, out_specs=P("ctx", "tp"), check_vma=False
    )
```

```python
import functools
import math

import jax
import jax.numpy as jnp
import numpy as np
from jax import lax
from jax.experimental import pallas as pl
from jax.experimental.pallas import tpu as pltpu
from jax.sharding import PartitionSpec as P

HD = 128
MODALITIES = 3
EPS = 1e-05
WINDOW = 528
ALIGN = 16
Q_TILE = 512
K_TILE = 1024
STATE_ROWS = HD + 16
AXES = ("ctx", "tp")
BF = jnp.bfloat16
F32 = jnp.float32
OFFSETS = np.array([0, 3, 1, 2])
VMEM_PROJECT = 47 * 1024 * 1024
VMEM_BYTES = 24 * 1024 * 1024
FEATURES = 4096
SPAN = 128
HEADROOM = 2.0**-13


def plane_perm(first, step):
    pairs = []
    for ctx in range(8):
        for z in range(4):
            for y in range(4):
                along_y = (ctx % 2 == 0) == first
                to_z = z if along_y else (z + step) % 4
                to_y = (y + step) % 4 if along_y else y
                pairs.append((ctx * 16 + z * 4 + y, ctx * 16 + to_z * 4 + to_y))
    return pairs


def move(array, first, step):
    return lax.ppermute(array, AXES, plane_perm(first, step))


def move_x(array, step):
    pairs = [(x * 2 + c, ((x + step) % 4) * 2 + c) for x in range(4) for c in range(2)]
    return lax.ppermute(array, "ctx", pairs)


def swap_core(array):
    return lax.ppermute(array, "ctx", [(i, i ^ 1) for i in range(8)])


def shard_table(first_offsets, second_offsets):
    core = lax.axis_index("ctx") % 2
    tp = lax.axis_index("tp")
    z, y = tp // 4, tp % 4
    first_offsets = jnp.asarray(first_offsets, jnp.int32)
    second_offsets = jnp.asarray(second_offsets, jnp.int32)
    first = (jnp.where(core == 0, y, z) + first_offsets) % 4
    second = (jnp.where(core == 0, z, y) + second_offsets) % 4
    return jnp.where(core == 0, second * 4 + first, first * 4 + second).astype(jnp.int32)


def segment_scalars(modality):
    rows = modality.shape[0]
    kinds = jnp.arange(MODALITIES, dtype=jnp.int32)[:, None]
    member = modality[None, :] == kinds
    positions = jnp.arange(rows, dtype=jnp.int32)[None, :]
    begin = jnp.min(jnp.where(member, positions, rows), axis=1)
    end = jnp.max(jnp.where(member, positions + 1, 0), axis=1)
    end = jnp.maximum(end, begin)
    core = lax.axis_index("ctx") % 2
    return jnp.concatenate([begin, end, core[None]]).astype(jnp.int32)


def for_runs(seg_ref, rows, body):
    for kind in range(MODALITIES):
        begin = seg_ref[kind]
        end = seg_ref[MODALITIES + kind]
        first = jnp.minimum(begin // ALIGN * ALIGN, rows - WINDOW)
        first = pl.multiple_of(first, ALIGN)
        positions = first + lax.broadcasted_iota(jnp.int32, (WINDOW, 1), 0)
        body(kind, pl.ds(first, WINDOW), (positions >= begin) & (positions < end))


def constant_spec(shape):
    return pl.BlockSpec(shape, lambda k, *scalars: (0,) * len(shape))


def project(pieces, weights, table, seg, before=None, last=False):
    count = len(pieces)
    shards, rows, width = pieces[0].shape
    depth = count * shards
    has_before = before is not None

    def kernel(table_ref, seg_ref, *refs):
        piece_refs = refs[:count]
        weight_refs = refs[count : count + 3]
        refs = refs[count + 3 :]
        if has_before:
            squares_before_ref, before_ref, *refs = refs
        if last:
            query_ref, kv_ref, query_send_ref, kv_send_ref, *refs = refs
        else:
            squares_ref, out_ref, *refs = refs
        held, normed, left, right, total, piece_sem, weight_sem, total_sem = refs

        spans = [pl.ds(row, SPAN) for row in range(0, rows, SPAN)]
        piece_copies = [
            pltpu.make_async_copy(
                piece_refs[i].at[:, span, :], held.at[i, :, span, :], piece_sem.at[k, i]
            )
            for k, span in enumerate(spans)
            for i in range(count)
        ]
        before_copies = []
        if has_before:
            before_copies = [
                pltpu.make_async_copy(
                    before_ref.at[span, :], total.at[span, :], total_sem.at[0, k]
                )
                for k, span in enumerate(spans)
            ]
        weight_copies = []
        for j in range(depth):
            first = pl.multiple_of(table_ref[j] * width, width)
            for i in range(3):
                weight_copies.append(
                    pltpu.make_async_copy(
                        weight_refs[i].at[:, pl.ds(first, width), :],
                        right.at[:, pl.ds(j * width, width), pl.ds(i * width, width)],
                        weight_sem.at[i, j],
                    )
                )
        for copy in piece_copies + before_copies + weight_copies:
            copy.start()
        if not has_before:
            total[...] = jnp.zeros_like(total)

        for row in range(0, rows, HD):
            at = slice(row, row + HD)
            if row % SPAN == 0:
                k = row // SPAN
                for copy in piece_copies[k * count : (k + 1) * count] + before_copies[k : k + 1]:
                    copy.wait()
            by_lane = jnp.zeros((HD, HD), F32)
            for i in range(count):
                for j in range(shards):
                    for column in range(0, width, HD):
                        by_lane += jnp.square(held[i, j, at, column : column + HD].astype(F32))
            squares = jnp.sum(by_lane, axis=1, keepdims=True)
            if has_before:
                squares_before = squares_before_ref[at, :]
                scale_before = lax.rsqrt(squares_before / FEATURES + EPS)
                squares += squares_before
            scale = lax.rsqrt(squares / FEATURES + EPS)
            if has_before:
                total[at, :] *= jnp.where(scale_before > 0.0, scale / scale_before, 0.0)
            if not last:
                squares_ref[at, :] = squares
            for j in range(depth):
                piece = held[j // shards, j % shards, at, :].astype(F32)
                normed[at, j * width : (j + 1) * width] = (piece * (scale * HEADROOM)).astype(BF)

        def mask(kind, at, keep):
            left[kind] = normed[at, :] * keep.astype(BF)

        for_runs(seg_ref, rows, mask)
        for copy in weight_copies:
            copy.wait()

        def run(kind, at, keep):
            total[at, :] += jnp.dot(left[kind], right[kind], preferred_element_type=F32)

        for_runs(seg_ref, rows, run)
        if not last:
            out_copies = [
                pltpu.make_async_copy(total.at[span, :], out_ref.at[span, :], total_sem.at[1, k])
                for k, span in enumerate(spans)
            ]
            for copy in out_copies:
                copy.start()
            for copy in out_copies:
                copy.wait()

        if last:
            query_scale = math.log2(math.e) / math.sqrt(HD) / HEADROOM
            core = seg_ref[2 * MODALITIES]
            for mine in range(2):

                @pl.when(core == mine)
                def _(mine=mine):
                    for head, q_out, kv_out in (
                        (mine, query_ref, kv_ref),
                        (1 - mine, query_send_ref, kv_send_ref),
                    ):
                        at = head * HD
                        kv_out[:, :HD] = (total[:, at : at + HD] / HEADROOM).astype(BF)
                        at += width
                        for row in range(0, rows, HD):
                            block = total[row : row + HD, at : at + HD] / HEADROOM
                            kv_out[row : row + HD, HD:] = block.T.astype(BF)
                        at += width
                        q_out[...] = (total[:, at : at + HD] * query_scale).astype(BF)

    vmem = pl.BlockSpec(memory_space=pltpu.VMEM)
    operands = [table, seg, *pieces, *weights]
    in_specs = [pl.BlockSpec(memory_space=pltpu.SMEM)] * 2
    in_specs += [pl.BlockSpec(memory_space=pl.ANY)] * count
    in_specs += [pl.BlockSpec(memory_space=pl.ANY)] * 3
    if has_before:
        operands += before
        in_specs += [vmem, pl.BlockSpec(memory_space=pl.ANY)]
    if last:
        shapes = [(rows, HD), (rows, 2 * HD)] * 2
        out_shape = tuple(jax.ShapeDtypeStruct(shape, BF) for shape in shapes)
        out_specs = (vmem,) * 4
    else:
        out_shape = (
            jax.ShapeDtypeStruct((rows, 1), F32),
            jax.ShapeDtypeStruct((rows, 3 * width), F32),
        )
        out_specs = (vmem, pl.BlockSpec(memory_space=pl.ANY))
    return pl.pallas_call(
        kernel,
        in_specs=in_specs,
        out_specs=out_specs,
        scratch_shapes=[
            pltpu.VMEM((count, shards, rows, width), BF),
            pltpu.VMEM((rows, depth * width), BF),
            pltpu.VMEM((MODALITIES, WINDOW, depth * width), BF),
            pltpu.VMEM((MODALITIES, depth * width, 3 * width), BF),
            pltpu.VMEM((rows, 3 * width), F32),
            pltpu.SemaphoreType.DMA((rows // SPAN, count)),
            pltpu.SemaphoreType.DMA((3, depth)),
            pltpu.SemaphoreType.DMA((2, rows // SPAN)),
        ],
        out_shape=out_shape,
        compiler_params=pltpu.CompilerParams(vmem_limit_bytes=VMEM_PROJECT),
        cost_estimate=pl.CostEstimate(
            flops=2 * depth * 3 * WINDOW * width * 3 * width,
            bytes_accessed=depth * (rows * width * 2 + 9 * width * width * 2),
            transcendentals=0,
        ),
    )(*operands)


def score(query, key, keep=None):
    scores = lax.dot_general(key, query, (((1,), (1,)), ((), ())), preferred_element_type=F32)
    return scores if keep is None else jnp.where(keep, scores, -1e30)


def fold(state, scores, value_t):
    top, total, summed = state
    new_top = jnp.maximum(top, jnp.max(scores, axis=0, keepdims=True))
    factor = jnp.exp2(top - new_top)
    weights = jnp.exp2(scores - new_top)
    total = total * factor + jnp.sum(weights, axis=0, keepdims=True)
    summed = summed * factor + jnp.dot(value_t, weights.astype(BF), preferred_element_type=F32)
    return new_top, total, summed


def empty_state():
    return (
        jnp.full((1, Q_TILE), -1e30, F32),
        jnp.zeros((1, Q_TILE), F32),
        jnp.zeros((HD, Q_TILE), F32),
    )


def store_state(state, state_ref):
    top, total, summed = state
    state_ref[0, :HD, :] = summed
    state_ref[0, HD : HD + 8, :] = jnp.broadcast_to(top, (8, Q_TILE))
    state_ref[0, HD + 8 :, :] = jnp.broadcast_to(total, (8, Q_TILE))


def load_state(state_ref):
    return (
        state_ref[0, HD : HD + 1, :],
        state_ref[0, HD + 8 : HD + 9, :],
        state_ref[0, :HD, :],
    )


def read_keys(ref, first, count):
    key = ref[pl.ds(first, count), :HD]
    blocks = [ref[pl.ds(first + i, HD), HD:] for i in range(0, count, HD)]
    return key, jnp.concatenate(blocks, axis=1)


def attend_own(query, query_other, kv, kv_other, core):
    rows = query.shape[0]
    per_block = rows // Q_TILE
    tiles = 2 * per_block

    def kernel(core_ref, query_ref, query_other_ref, kv_ref, kv_other_ref, state_ref, keys, both):
        place = pl.program_id(0)

        @pl.when(place == 0)
        def _():
            for mine in range(2):

                @pl.when(core_ref[0] == mine)
                def _(mine=mine):
                    at, other = mine * rows, (1 - mine) * rows
                    keys[at : at + rows, :] = kv_ref[...]
                    keys[other : other + rows, :] = kv_other_ref[...]
                    both[at : at + rows, :] = query_ref[...]
                    both[other : other + rows, :] = query_other_ref[...]

        at = pl.multiple_of(place * Q_TILE, Q_TILE)
        q = both[pl.ds(at, Q_TILE), :]
        causal = lax.broadcasted_iota(
            jnp.int32, (Q_TILE, Q_TILE), 0
        ) <= lax.broadcasted_iota(jnp.int32, (Q_TILE, Q_TILE), 1)
        key, value_t = read_keys(keys, at, Q_TILE)
        state = fold(empty_state(), score(q, key, causal), value_t)

        def earlier(tile, state):
            key, value_t = read_keys(keys, pl.multiple_of(tile * Q_TILE, Q_TILE), Q_TILE)
            return fold(state, score(q, key), value_t)

        store_state(lax.fori_loop(0, place, earlier, state), state_ref)

    whole = constant_spec((rows, HD))
    whole_kv = constant_spec((rows, 2 * HD))
    return pl.pallas_call(
        kernel,
        grid_spec=pltpu.PrefetchScalarGridSpec(
            num_scalar_prefetch=1,
            grid=(tiles,),
            in_specs=[whole, whole, whole_kv, whole_kv],
            out_specs=pl.BlockSpec(
                (1, STATE_ROWS, Q_TILE),
                lambda i, core: ((i + core[0] * per_block) % tiles, 0, 0),
            ),
            scratch_shapes=[
                pltpu.VMEM((2 * rows, 2 * HD), BF),
                pltpu.VMEM((2 * rows, HD), BF),
            ],
        ),
        out_shape=jax.ShapeDtypeStruct((tiles, STATE_ROWS, Q_TILE), F32),
        compiler_params=pltpu.CompilerParams(vmem_limit_bytes=VMEM_BYTES),
        cost_estimate=pl.CostEstimate(
            flops=10 * Q_TILE * Q_TILE * HD * 4,
            bytes_accessed=4 << 20,
            transcendentals=10 * Q_TILE * Q_TILE,
        ),
    )(core, query, query_other, kv, kv_other)


def attend_other(query, query_other, state, sources, use, last=False):
    rows = query.shape[0]
    per_block = rows // Q_TILE
    tiles = 2 * per_block
    count = len(sources)

    def kernel(use_ref, query_ref, query_other_ref, before_ref, *refs):
        source_refs = refs[:count]
        *out_refs, after, q_ref = refs[count:]
        tile = pl.program_id(0)

        @pl.when(tile < per_block)
        def _():
            q_ref[...] = query_ref[...]

        @pl.when(tile >= per_block)
        def _():
            q_ref[...] = query_other_ref[...]

        q = q_ref[...]
        after[...] = before_ref[...]

        def fold_in(refs):
            parts = [(ref, at) for ref in refs for at in range(0, rows, K_TILE)]
            state = load_state(after)
            scores = None
            for i, (ref, at) in enumerate(parts):
                key, value_t = read_keys(ref, at, K_TILE)
                if scores is None:
                    scores = score(q, key)
                later = None
                if i + 1 < len(parts):
                    next_ref, next_at = parts[i + 1]
                    later = score(q, next_ref[next_at : next_at + K_TILE, :HD])
                state = fold(state, scores, value_t)
                scores = later
            store_state(state, after)

        all_used = use_ref[0]
        for i in range(1, count):
            all_used = all_used & use_ref[i]

        @pl.when(all_used != 0)
        def _():
            fold_in(source_refs)

        for i, source_ref in enumerate(source_refs):

            @pl.when((all_used == 0) & (use_ref[i] != 0))
            def _(source_ref=source_ref):
                fold_in([source_ref])

        if last:
            _, total, summed = load_state(after)
            attended = (summed / total).T.astype(BF)
            for part, out_ref in enumerate(out_refs):

                @pl.when(tile // per_block == part)
                def _(out_ref=out_ref):
                    at = pl.multiple_of(tile % per_block * Q_TILE, Q_TILE)
                    out_ref[pl.ds(at, Q_TILE), :] = attended

        else:
            out_refs[0][...] = after[...]

    state_spec = pl.BlockSpec((1, STATE_ROWS, Q_TILE), lambda i, use: (i, 0, 0))
    if last:
        out_shape = (jax.ShapeDtypeStruct((rows, HD), BF),) * 2
        out_specs = (constant_spec((rows, HD)),) * 2
    else:
        out_shape = jax.ShapeDtypeStruct((tiles, STATE_ROWS, Q_TILE), F32)
        out_specs = state_spec
    return pl.pallas_call(
        kernel,
        grid_spec=pltpu.PrefetchScalarGridSpec(
            num_scalar_prefetch=1,
            grid=(tiles,),
            in_specs=[
                pl.BlockSpec((Q_TILE, HD), lambda i, use: (jnp.minimum(i, per_block - 1), 0)),
                pl.BlockSpec((Q_TILE, HD), lambda i, use: (jnp.maximum(i - per_block, 0), 0)),
                state_spec,
            ]
            + [constant_spec(source.shape) for source in sources],
            out_specs=out_specs,
            scratch_shapes=[
                pltpu.VMEM((1, STATE_ROWS, Q_TILE), F32),
                pltpu.VMEM((Q_TILE, HD), BF),
            ],
        ),
        out_shape=out_shape,
        compiler_params=pltpu.CompilerParams(vmem_limit_bytes=VMEM_BYTES),
        cost_estimate=pl.CostEstimate(
            flops=2 * rows * count * rows * HD * 4,
            bytes_accessed=6 << 20,
            transcendentals=2 * rows * count * rows,
        ),
    )(use, query, query_other, state, *sources)


def output_part(own, other, w_out, table, seg, sizes):
    blocks = table.shape[0]
    rows = own.shape[0]
    width = 2 * HD

    def kernel(table_ref, seg_ref, own_ref, other_ref, weight_ref, *refs):
        *out_refs, attended, left, right, total, result, weight_sem, out_sem = refs
        weight_copies = []
        for i in range(blocks):
            first = pl.multiple_of(table_ref[i] * width, width)
            weight_copies.append(
                pltpu.make_async_copy(
                    weight_ref.at[:, :, pl.ds(first, width)],
                    right.at[i // 2, :, :, pl.ds(i % 2 * width, width)],
                    weight_sem.at[i],
                )
            )
            weight_copies[i].start()
        core = seg_ref[2 * MODALITIES]
        for mine in range(2):

            @pl.when(core == mine)
            def _(mine=mine):
                attended[:, mine * HD : (mine + 1) * HD] = own_ref[...]
                attended[:, (1 - mine) * HD : (2 - mine) * HD] = other_ref[...]

        def mask(kind, at, keep):
            left[kind] = attended[at, :] * keep.astype(BF)

        for_runs(seg_ref, rows, mask)
        out_copies = []
        spans = [pl.ds(row, 2 * SPAN) for row in range(0, rows, 2 * SPAN)]
        for pair in range(blocks // 2):
            weight_copies[2 * pair].wait()
            weight_copies[2 * pair + 1].wait()
            total[...] = jnp.zeros_like(total)

            def run(kind, at, keep, pair=pair):
                total[at, :] += jnp.dot(left[kind], right[pair, kind], preferred_element_type=F32)

            for_runs(seg_ref, rows, run)
            for i in range(2):
                result[2 * pair + i] = total[:, i * width : (i + 1) * width].astype(BF)
            done = 0
            for size, out_ref in zip(sizes, out_refs):
                for i in range(max(size, 1)):
                    if done // 2 == pair:
                        target = out_ref.at[i] if size else out_ref
                        for k, span in enumerate(spans):
                            out_copies.append(
                                pltpu.make_async_copy(
                                    result.at[done, span, :], target.at[span, :], out_sem.at[done, k]
                                )
                            )
                            out_copies[-1].start()
                    done += 1
        for copy in out_copies:
            copy.wait()

    vmem = pl.BlockSpec(memory_space=pltpu.VMEM)
    shapes = [(size, rows, width) if size else (rows, width) for size in sizes]
    return pl.pallas_call(
        kernel,
        in_specs=[pl.BlockSpec(memory_space=pltpu.SMEM)] * 2
        + [vmem, vmem, pl.BlockSpec(memory_space=pl.ANY)],
        out_specs=(pl.BlockSpec(memory_space=pl.ANY),) * len(shapes),
        scratch_shapes=[
            pltpu.VMEM((rows, width), BF),
            pltpu.VMEM((MODALITIES, WINDOW, width), BF),
            pltpu.VMEM((blocks // 2, MODALITIES, width, 2 * width), BF),
            pltpu.VMEM((rows, 2 * width), F32),
            pltpu.VMEM((blocks, rows, width), BF),
            pltpu.SemaphoreType.DMA((blocks,)),
            pltpu.SemaphoreType.DMA((blocks, rows // SPAN // 2)),
        ],
        out_shape=tuple(jax.ShapeDtypeStruct(shape, BF) for shape in shapes),
        compiler_params=pltpu.CompilerParams(vmem_limit_bytes=VMEM_PROJECT),
        cost_estimate=pl.CostEstimate(
            flops=2 * 3 * WINDOW * blocks * width * width,
            bytes_accessed=blocks * (3 * width * width + rows * width) * 2,
            transcendentals=0,
        ),
    )(table, seg, own, other, w_out)


def add(*arrays):
    return sum(array.astype(F32) for array in arrays).astype(BF)


def local(tokens, modality, w_query, w_key, w_value, w_out):
    seg = segment_scalars(modality)
    core = seg[2 * MODALITIES :]
    weights = (w_key, w_value, w_query)

    low = jnp.stack([tokens, move(tokens, True, 1)])
    high = jnp.stack([move(tokens, True, -1), move(tokens, True, 2)])
    before_low = move(low, False, 1)
    after_high = move(high, False, -1)
    before_high = move(high, False, 1)
    after_low = move(low, False, -1)
    table = shard_table(np.tile(OFFSETS, 4), np.repeat(OFFSETS, 4))
    partial = project([low, high], weights, table[:4], seg)
    before_low, after_high, partial = lax.optimization_barrier((before_low, after_high, partial))
    far_low = move(before_low, False, 1)
    far_high = move(after_high, False, -1)
    partial = project(
        [before_low, after_high, before_high, after_low],
        weights,
        jnp.concatenate([table[4:6], table[10:12], table[6:10]]),
        seg,
        before=partial,
    )
    query, kv, query_send, kv_send = project(
        [far_low, far_high], weights, table[12:], seg, before=partial, last=True
    )

    kv_other = swap_core(kv_send)
    query_other = swap_core(query_send)
    kv_before = move_x(kv, 1)
    kv_other_after = move_x(kv_other, -1)
    kv_other_before = move_x(kv_other, 1)
    kv_after = move_x(kv, -1)
    chip = lax.axis_index("ctx") // 2
    near_use = jnp.stack([chip >= 1, chip == 3]).astype(jnp.int32)
    far_use = jnp.stack([chip >= 2, chip >= 2]).astype(jnp.int32)
    queries = (query, query_other)
    state = attend_own(*queries, kv, kv_other, core)
    kv_before, kv_other_after, state = lax.optimization_barrier((kv_before, kv_other_after, state))
    kv_far = move_x(kv_before, 1)
    kv_other_far = move_x(kv_other_after, -1)
    state = attend_other(*queries, state, [kv_before, kv_other_after], near_use)
    state = attend_other(*queries, state, [kv_other_before, kv_after], near_use)
    own, own_send = attend_other(*queries, state, [kv_far, kv_other_far], far_use, last=True)
    other = swap_core(own_send)

    part = functools.partial(output_part, own, other, w_out)
    here, plus, two, minus = (shard_table(np.full(4, offset), np.arange(4)) for offset in range(4))
    two_low, two_high = part(two, seg, (2, 2))
    plus_high, minus_low = part(jnp.concatenate([plus[2:], minus[:2]]), seg, (2, 2))
    two_low = move(two_low, True, 1)
    two_high = move(two_high, True, -1)
    plus_high = move(plus_high, True, 1)
    minus_low = move(minus_low, True, -1)
    plus_low, minus_high, *here = part(
        jnp.concatenate([plus[:2], minus[2:], here]), seg, (2, 2, 0, 0, 0, 0)
    )
    plus_low = move(add(plus_low, two_low), True, 1)
    minus_high = move(add(minus_high, two_high), True, -1)
    mine, plus, two, minus = (
        add(here[i], (plus_low, plus_high)[i // 2][i % 2], (minus_low, minus_high)[i // 2][i % 2])
        for i in range(4)
    )
    return add(
        tokens, mine, move(plus, False, 1), move(two, False, 2), move(minus, False, -1)
    )


def solution(mesh):
    in_specs = (
        P("ctx", "tp"),
        P("ctx"),
        P(None, None, "tp"),
        P(None, None, "tp"),
        P(None, None, "tp"),
        P(None, "tp", None),
    )
    return jax.shard_map(
        local, mesh=mesh, in_specs=in_specs, out_specs=P("ctx", "tp"), check_vma=False
    )
```

```python
import functools
import math

import jax
import jax.numpy as jnp
import numpy as np
from jax import lax
from jax.experimental import pallas as pl
from jax.experimental.pallas import tpu as pltpu
from jax.sharding import PartitionSpec as P

HD = 128
MODALITIES = 3
EPS = 1e-05
WINDOW = 528
ALIGN = 16
Q_TILE = 512
K_TILE = 1024
STATE_ROWS = HD + 16
AXES = ("ctx", "tp")
BF = jnp.bfloat16
F32 = jnp.float32
OFFSETS = np.array([0, 3, 1, 2])
VMEM_PROJECT = 47 * 1024 * 1024
VMEM_BYTES = 24 * 1024 * 1024
FEATURES = 4096
SPAN = 128
HEADROOM = 2.0**-13


def plane_perm(first, step):
    pairs = []
    for ctx in range(8):
        for z in range(4):
            for y in range(4):
                along_y = (ctx % 2 == 0) == first
                to_z = z if along_y else (z + step) % 4
                to_y = (y + step) % 4 if along_y else y
                pairs.append((ctx * 16 + z * 4 + y, ctx * 16 + to_z * 4 + to_y))
    return pairs


def move(array, first, step):
    return lax.ppermute(array, AXES, plane_perm(first, step))


def move_x(array, step):
    pairs = [(x * 2 + c, ((x + step) % 4) * 2 + c) for x in range(4) for c in range(2)]
    return lax.ppermute(array, "ctx", pairs)


def swap_core(array):
    return lax.ppermute(array, "ctx", [(i, i ^ 1) for i in range(8)])


def shard_table(first_offsets, second_offsets):
    core = lax.axis_index("ctx") % 2
    tp = lax.axis_index("tp")
    z, y = tp // 4, tp % 4
    first_offsets = jnp.asarray(first_offsets, jnp.int32)
    second_offsets = jnp.asarray(second_offsets, jnp.int32)
    first = (jnp.where(core == 0, y, z) + first_offsets) % 4
    second = (jnp.where(core == 0, z, y) + second_offsets) % 4
    return jnp.where(core == 0, second * 4 + first, first * 4 + second).astype(jnp.int32)


def segment_scalars(modality):
    rows = modality.shape[0]
    kinds = jnp.arange(MODALITIES, dtype=jnp.int32)[:, None]
    member = modality[None, :] == kinds
    positions = jnp.arange(rows, dtype=jnp.int32)[None, :]
    begin = jnp.min(jnp.where(member, positions, rows), axis=1)
    end = jnp.max(jnp.where(member, positions + 1, 0), axis=1)
    end = jnp.maximum(end, begin)
    core = lax.axis_index("ctx") % 2
    return jnp.concatenate([begin, end, core[None]]).astype(jnp.int32)


def for_runs(seg_ref, rows, body):
    for kind in range(MODALITIES):
        begin = seg_ref[kind]
        end = seg_ref[MODALITIES + kind]
        first = jnp.minimum(begin // ALIGN * ALIGN, rows - WINDOW)
        first = pl.multiple_of(first, ALIGN)
        positions = first + lax.broadcasted_iota(jnp.int32, (WINDOW, 1), 0)
        body(kind, pl.ds(first, WINDOW), (positions >= begin) & (positions < end))


def constant_spec(shape):
    return pl.BlockSpec(shape, lambda k, *scalars: (0,) * len(shape))


def project(pieces, weights, table, seg, before=None, last=False):
    count = len(pieces)
    shards, rows, width = pieces[0].shape
    depth = count * shards
    has_before = before is not None

    def kernel(table_ref, seg_ref, *refs):
        piece_refs = refs[:count]
        weight_refs = refs[count : count + 3]
        refs = refs[count + 3 :]
        if has_before:
            squares_before_ref, before_ref, *refs = refs
        if last:
            query_ref, kv_ref, query_send_ref, kv_send_ref, *refs = refs
        else:
            squares_ref, out_ref, *refs = refs
        held, normed, left, right, total, piece_sem, weight_sem, total_sem = refs

        spans = [pl.ds(row, SPAN) for row in range(0, rows, SPAN)]
        piece_copies = [
            pltpu.make_async_copy(
                piece_refs[i].at[:, span, :], held.at[i, :, span, :], piece_sem.at[k, i]
            )
            for k, span in enumerate(spans)
            for i in range(count)
        ]
        before_copies = []
        if has_before:
            before_copies = [
                pltpu.make_async_copy(
                    before_ref.at[span, :], total.at[span, :], total_sem.at[0, k]
                )
                for k, span in enumerate(spans)
            ]
        weight_copies = []
        for j in range(depth):
            first = pl.multiple_of(table_ref[j] * width, width)
            for i in range(3):
                weight_copies.append(
                    pltpu.make_async_copy(
                        weight_refs[i].at[:, pl.ds(first, width), :],
                        right.at[:, pl.ds(j * width, width), pl.ds(i * width, width)],
                        weight_sem.at[i, j],
                    )
                )
        for copy in piece_copies + before_copies + weight_copies:
            copy.start()
        if not has_before:
            total[...] = jnp.zeros_like(total)

        for row in range(0, rows, HD):
            at = slice(row, row + HD)
            if row % SPAN == 0:
                k = row // SPAN
                for copy in piece_copies[k * count : (k + 1) * count] + before_copies[k : k + 1]:
                    copy.wait()
            by_lane = jnp.zeros((HD, HD), F32)
            for i in range(count):
                for j in range(shards):
                    for column in range(0, width, HD):
                        by_lane += jnp.square(held[i, j, at, column : column + HD].astype(F32))
            squares = jnp.sum(by_lane, axis=1, keepdims=True)
            if has_before:
                squares_before = squares_before_ref[at, :]
                scale_before = lax.rsqrt(squares_before / FEATURES + EPS)
                squares += squares_before
            scale = lax.rsqrt(squares / FEATURES + EPS)
            if has_before:
                total[at, :] *= jnp.where(scale_before > 0.0, scale / scale_before, 0.0)
            if not last:
                squares_ref[at, :] = squares
            for j in range(depth):
                piece = held[j // shards, j % shards, at, :].astype(F32)
                normed[at, j * width : (j + 1) * width] = (piece * (scale * HEADROOM)).astype(BF)

        def mask(kind, at, keep):
            left[kind] = normed[at, :] * keep.astype(BF)

        for_runs(seg_ref, rows, mask)
        for copy in weight_copies:
            copy.wait()

        def run(kind, at, keep):
            total[at, :] += jnp.dot(left[kind], right[kind], preferred_element_type=F32)

        for_runs(seg_ref, rows, run)
        if not last:
            out_copies = [
                pltpu.make_async_copy(total.at[span, :], out_ref.at[span, :], total_sem.at[1, k])
                for k, span in enumerate(spans)
            ]
            for copy in out_copies:
                copy.start()
            for copy in out_copies:
                copy.wait()

        if last:
            query_scale = math.log2(math.e) / math.sqrt(HD) / HEADROOM
            core = seg_ref[2 * MODALITIES]
            for mine in range(2):

                @pl.when(core == mine)
                def _(mine=mine):
                    for head, q_out, kv_out in (
                        (mine, query_ref, kv_ref),
                        (1 - mine, query_send_ref, kv_send_ref),
                    ):
                        at = head * HD
                        kv_out[:, :HD] = (total[:, at : at + HD] / HEADROOM).astype(BF)
                        at += width
                        for row in range(0, rows, HD):
                            block = total[row : row + HD, at : at + HD] / HEADROOM
                            kv_out[row : row + HD, HD:] = block.T.astype(BF)
                        at += width
                        q_out[...] = (total[:, at : at + HD] * query_scale).astype(BF)

    vmem = pl.BlockSpec(memory_space=pltpu.VMEM)
    operands = [table, seg, *pieces, *weights]
    in_specs = [pl.BlockSpec(memory_space=pltpu.SMEM)] * 2
    in_specs += [pl.BlockSpec(memory_space=pl.ANY)] * count
    in_specs += [pl.BlockSpec(memory_space=pl.ANY)] * 3
    if has_before:
        operands += before
        in_specs += [vmem, pl.BlockSpec(memory_space=pl.ANY)]
    if last:
        shapes = [(rows, HD), (rows, 2 * HD)] * 2
        out_shape = tuple(jax.ShapeDtypeStruct(shape, BF) for shape in shapes)
        out_specs = (vmem,) * 4
    else:
        out_shape = (
            jax.ShapeDtypeStruct((rows, 1), F32),
            jax.ShapeDtypeStruct((rows, 3 * width), F32),
        )
        out_specs = (vmem, pl.BlockSpec(memory_space=pl.ANY))
    return pl.pallas_call(
        kernel,
        in_specs=in_specs,
        out_specs=out_specs,
        scratch_shapes=[
            pltpu.VMEM((count, shards, rows, width), BF),
            pltpu.VMEM((rows, depth * width), BF),
            pltpu.VMEM((MODALITIES, WINDOW, depth * width), BF),
            pltpu.VMEM((MODALITIES, depth * width, 3 * width), BF),
            pltpu.VMEM((rows, 3 * width), F32),
            pltpu.SemaphoreType.DMA((rows // SPAN, count)),
            pltpu.SemaphoreType.DMA((3, depth)),
            pltpu.SemaphoreType.DMA((2, rows // SPAN)),
        ],
        out_shape=out_shape,
        compiler_params=pltpu.CompilerParams(vmem_limit_bytes=VMEM_PROJECT),
        cost_estimate=pl.CostEstimate(
            flops=2 * depth * 3 * WINDOW * width * 3 * width,
            bytes_accessed=depth * (rows * width * 2 + 9 * width * width * 2),
            transcendentals=0,
        ),
    )(*operands)


def score(query, key, keep=None):
    scores = lax.dot_general(key, query, (((1,), (1,)), ((), ())), preferred_element_type=F32)
    return scores if keep is None else jnp.where(keep, scores, -1e30)


def fold(state, scores, value_t):
    top, total, summed = state
    new_top = jnp.maximum(top, jnp.max(scores, axis=0, keepdims=True))
    factor = jnp.exp2(top - new_top)
    weights = jnp.exp2(scores - new_top)
    total = total * factor + jnp.sum(weights, axis=0, keepdims=True)
    summed = summed * factor + jnp.dot(value_t, weights.astype(BF), preferred_element_type=F32)
    return new_top, total, summed


def empty_state():
    return (
        jnp.full((1, Q_TILE), -1e30, F32),
        jnp.zeros((1, Q_TILE), F32),
        jnp.zeros((HD, Q_TILE), F32),
    )


def store_state(state, state_ref):
    top, total, summed = state
    state_ref[0, :HD, :] = summed
    state_ref[0, HD : HD + 8, :] = jnp.broadcast_to(top, (8, Q_TILE))
    state_ref[0, HD + 8 :, :] = jnp.broadcast_to(total, (8, Q_TILE))


def load_state(state_ref):
    return (
        state_ref[0, HD : HD + 1, :],
        state_ref[0, HD + 8 : HD + 9, :],
        state_ref[0, :HD, :],
    )


def read_keys(ref, first, count):
    key = ref[pl.ds(first, count), :HD]
    blocks = [ref[pl.ds(first + i, HD), HD:] for i in range(0, count, HD)]
    return key, jnp.concatenate(blocks, axis=1)


def attend_own(query, query_other, kv, kv_other, core):
    rows = query.shape[0]
    per_block = rows // Q_TILE
    tiles = 2 * per_block

    def kernel(core_ref, query_ref, query_other_ref, kv_ref, kv_other_ref, state_ref, keys, both):
        place = pl.program_id(0)

        @pl.when(place == 0)
        def _():
            for mine in range(2):

                @pl.when(core_ref[0] == mine)
                def _(mine=mine):
                    at, other = mine * rows, (1 - mine) * rows
                    keys[at : at + rows, :] = kv_ref[...]
                    keys[other : other + rows, :] = kv_other_ref[...]
                    both[at : at + rows, :] = query_ref[...]
                    both[other : other + rows, :] = query_other_ref[...]

        at = pl.multiple_of(place * Q_TILE, Q_TILE)
        q = both[pl.ds(at, Q_TILE), :]
        causal = lax.broadcasted_iota(
            jnp.int32, (Q_TILE, Q_TILE), 0
        ) <= lax.broadcasted_iota(jnp.int32, (Q_TILE, Q_TILE), 1)
        key, value_t = read_keys(keys, at, Q_TILE)
        state = fold(empty_state(), score(q, key, causal), value_t)

        def earlier(tile, state):
            key, value_t = read_keys(keys, pl.multiple_of(tile * Q_TILE, Q_TILE), Q_TILE)
            return fold(state, score(q, key), value_t)

        store_state(lax.fori_loop(0, place, earlier, state), state_ref)

    whole = constant_spec((rows, HD))
    whole_kv = constant_spec((rows, 2 * HD))
    return pl.pallas_call(
        kernel,
        grid_spec=pltpu.PrefetchScalarGridSpec(
            num_scalar_prefetch=1,
            grid=(tiles,),
            in_specs=[whole, whole, whole_kv, whole_kv],
            out_specs=pl.BlockSpec(
                (1, STATE_ROWS, Q_TILE),
                lambda i, core: ((i + core[0] * per_block) % tiles, 0, 0),
            ),
            scratch_shapes=[
                pltpu.VMEM((2 * rows, 2 * HD), BF),
                pltpu.VMEM((2 * rows, HD), BF),
            ],
        ),
        out_shape=jax.ShapeDtypeStruct((tiles, STATE_ROWS, Q_TILE), F32),
        compiler_params=pltpu.CompilerParams(vmem_limit_bytes=VMEM_BYTES),
        cost_estimate=pl.CostEstimate(
            flops=10 * Q_TILE * Q_TILE * HD * 4,
            bytes_accessed=4 << 20,
            transcendentals=10 * Q_TILE * Q_TILE,
        ),
    )(core, query, query_other, kv, kv_other)


def attend_other(query, query_other, state, sources, use, last=False):
    rows = query.shape[0]
    per_block = rows // Q_TILE
    tiles = 2 * per_block
    count = len(sources)

    def kernel(use_ref, query_ref, query_other_ref, before_ref, *refs):
        source_refs = refs[:count]
        *out_refs, after, q_ref = refs[count:]
        tile = pl.program_id(0)

        @pl.when(tile < per_block)
        def _():
            q_ref[...] = query_ref[...]

        @pl.when(tile >= per_block)
        def _():
            q_ref[...] = query_other_ref[...]

        q = q_ref[...]
        after[...] = before_ref[...]

        def fold_in(refs):
            parts = [(ref, at) for ref in refs for at in range(0, rows, K_TILE)]
            state = load_state(after)
            scores = None
            for i, (ref, at) in enumerate(parts):
                key, value_t = read_keys(ref, at, K_TILE)
                if scores is None:
                    scores = score(q, key)
                later = None
                if i + 1 < len(parts):
                    next_ref, next_at = parts[i + 1]
                    later = score(q, next_ref[next_at : next_at + K_TILE, :HD])
                state = fold(state, scores, value_t)
                scores = later
            store_state(state, after)

        all_used = use_ref[0]
        for i in range(1, count):
            all_used = all_used & use_ref[i]

        @pl.when(all_used != 0)
        def _():
            fold_in(source_refs)

        for i, source_ref in enumerate(source_refs):

            @pl.when((all_used == 0) & (use_ref[i] != 0))
            def _(source_ref=source_ref):
                fold_in([source_ref])

        if last:
            _, total, summed = load_state(after)
            attended = (summed / total).T.astype(BF)
            for part, out_ref in enumerate(out_refs):

                @pl.when(tile // per_block == part)
                def _(out_ref=out_ref):
                    at = pl.multiple_of(tile % per_block * Q_TILE, Q_TILE)
                    out_ref[pl.ds(at, Q_TILE), :] = attended

        else:
            out_refs[0][...] = after[...]

    state_spec = pl.BlockSpec((1, STATE_ROWS, Q_TILE), lambda i, use: (i, 0, 0))
    if last:
        out_shape = (jax.ShapeDtypeStruct((rows, HD), BF),) * 2
        out_specs = (constant_spec((rows, HD)),) * 2
    else:
        out_shape = jax.ShapeDtypeStruct((tiles, STATE_ROWS, Q_TILE), F32)
        out_specs = state_spec
    return pl.pallas_call(
        kernel,
        grid_spec=pltpu.PrefetchScalarGridSpec(
            num_scalar_prefetch=1,
            grid=(tiles,),
            in_specs=[
                pl.BlockSpec((Q_TILE, HD), lambda i, use: (jnp.minimum(i, per_block - 1), 0)),
                pl.BlockSpec((Q_TILE, HD), lambda i, use: (jnp.maximum(i - per_block, 0), 0)),
                state_spec,
            ]
            + [constant_spec(source.shape) for source in sources],
            out_specs=out_specs,
            scratch_shapes=[
                pltpu.VMEM((1, STATE_ROWS, Q_TILE), F32),
                pltpu.VMEM((Q_TILE, HD), BF),
            ],
        ),
        out_shape=out_shape,
        compiler_params=pltpu.CompilerParams(vmem_limit_bytes=VMEM_BYTES),
        cost_estimate=pl.CostEstimate(
            flops=2 * rows * count * rows * HD * 4,
            bytes_accessed=6 << 20,
            transcendentals=2 * rows * count * rows,
        ),
    )(use, query, query_other, state, *sources)


def order_weights(w_out, table):
    groups = table.shape[0] // 4
    depth, width = w_out.shape[1], 2 * HD

    def kernel(table_ref, weight_ref, *out_refs):
        for i, out_ref in enumerate(out_refs):

            @pl.when(pl.program_id(0) // 4 == i)
            def _(out_ref=out_ref):
                out_ref[0] = weight_ref[...]

    return pl.pallas_call(
        kernel,
        grid_spec=pltpu.PrefetchScalarGridSpec(
            num_scalar_prefetch=1,
            grid=(4 * groups,),
            in_specs=[pl.BlockSpec((MODALITIES, depth, width), lambda k, t: (0, 0, t[k]))],
            out_specs=tuple(
                pl.BlockSpec(
                    (1, MODALITIES, depth, width),
                    lambda k, t, i=i: (jnp.clip(k - 4 * i, 0, 3), 0, 0, 0),
                )
                for i in range(groups)
            ),
        ),
        out_shape=(jax.ShapeDtypeStruct((4, MODALITIES, depth, width), BF),) * groups,
        compiler_params=pltpu.CompilerParams(vmem_limit_bytes=VMEM_PROJECT),
        cost_estimate=pl.CostEstimate(
            flops=0, bytes_accessed=4 * groups * MODALITIES * depth * width * 4, transcendentals=0
        ),
    )(table, w_out)


def output_part(own, other, seg, weights, sizes):
    blocks = weights.shape[0]
    rows = own.shape[0]
    width = 2 * HD

    def kernel(seg_ref, own_ref, other_ref, weight_ref, *refs):
        *out_refs, attended, left, right, total, result, weight_sem, out_sem = refs
        weight_copies = []
        for i in range(blocks):
            weight_copies.append(
                pltpu.make_async_copy(
                    weight_ref.at[i],
                    right.at[i // 2, :, :, pl.ds(i % 2 * width, width)],
                    weight_sem.at[i],
                )
            )
            weight_copies[i].start()
        core = seg_ref[2 * MODALITIES]
        for mine in range(2):

            @pl.when(core == mine)
            def _(mine=mine):
                attended[:, mine * HD : (mine + 1) * HD] = own_ref[...]
                attended[:, (1 - mine) * HD : (2 - mine) * HD] = other_ref[...]

        def mask(kind, at, keep):
            left[kind] = attended[at, :] * keep.astype(BF)

        for_runs(seg_ref, rows, mask)
        out_copies = []
        spans = [pl.ds(row, 2 * SPAN) for row in range(0, rows, 2 * SPAN)]
        for pair in range(blocks // 2):
            weight_copies[2 * pair].wait()
            weight_copies[2 * pair + 1].wait()
            total[...] = jnp.zeros_like(total)

            def run(kind, at, keep, pair=pair):
                total[at, :] += jnp.dot(left[kind], right[pair, kind], preferred_element_type=F32)

            for_runs(seg_ref, rows, run)
            for i in range(2):
                result[2 * pair + i] = total[:, i * width : (i + 1) * width].astype(BF)
            done = 0
            for size, out_ref in zip(sizes, out_refs):
                for i in range(max(size, 1)):
                    if done // 2 == pair:
                        target = out_ref.at[i] if size else out_ref
                        for k, span in enumerate(spans):
                            out_copies.append(
                                pltpu.make_async_copy(
                                    result.at[done, span, :], target.at[span, :], out_sem.at[done, k]
                                )
                            )
                            out_copies[-1].start()
                    done += 1
        for copy in out_copies:
            copy.wait()

    vmem = pl.BlockSpec(memory_space=pltpu.VMEM)
    shapes = [(size, rows, width) if size else (rows, width) for size in sizes]
    return pl.pallas_call(
        kernel,
        in_specs=[pl.BlockSpec(memory_space=pltpu.SMEM), vmem, vmem]
        + [pl.BlockSpec(memory_space=pl.ANY)],
        out_specs=(pl.BlockSpec(memory_space=pl.ANY),) * len(shapes),
        scratch_shapes=[
            pltpu.VMEM((rows, width), BF),
            pltpu.VMEM((MODALITIES, WINDOW, width), BF),
            pltpu.VMEM((blocks // 2, MODALITIES, width, 2 * width), BF),
            pltpu.VMEM((rows, 2 * width), F32),
            pltpu.VMEM((blocks, rows, width), BF),
            pltpu.SemaphoreType.DMA((blocks,)),
            pltpu.SemaphoreType.DMA((blocks, rows // SPAN // 2)),
        ],
        out_shape=tuple(jax.ShapeDtypeStruct(shape, BF) for shape in shapes),
        compiler_params=pltpu.CompilerParams(vmem_limit_bytes=VMEM_PROJECT),
        cost_estimate=pl.CostEstimate(flops=0, bytes_accessed=rows, transcendentals=0),
    )(seg, own, other, weights)


def add(*arrays):
    return sum(array.astype(F32) for array in arrays).astype(BF)


def local(tokens, modality, w_query, w_key, w_value, w_out):
    seg = segment_scalars(modality)
    core = seg[2 * MODALITIES :]
    weights = (w_key, w_value, w_query)

    low = jnp.stack([tokens, move(tokens, True, 1)])
    high = jnp.stack([move(tokens, True, -1), move(tokens, True, 2)])
    before_low = move(low, False, 1)
    after_high = move(high, False, -1)
    before_high = move(high, False, 1)
    after_low = move(low, False, -1)
    table = shard_table(np.tile(OFFSETS, 4), np.repeat(OFFSETS, 4))
    partial = project([low, high], weights, table[:4], seg)
    before_low, after_high, partial = lax.optimization_barrier((before_low, after_high, partial))
    far_low = move(before_low, False, 1)
    far_high = move(after_high, False, -1)
    here, plus, two, minus = (shard_table(np.full(4, offset), np.arange(4)) for offset in range(4))
    order = jnp.concatenate([two, plus[2:], minus[:2], plus[:2], minus[2:], here])
    before_high, after_low, *w_ordered = lax.optimization_barrier(
        (before_high, after_low, *order_weights(w_out, order))
    )
    w_two, w_first, w_later, w_here = w_ordered
    partial = project(
        [before_low, after_high, before_high, after_low],
        weights,
        jnp.concatenate([table[4:6], table[10:12], table[6:10]]),
        seg,
        before=partial,
    )
    query, kv, query_send, kv_send = project(
        [far_low, far_high], weights, table[12:], seg, before=partial, last=True
    )

    kv_other = swap_core(kv_send)
    query_other = swap_core(query_send)
    kv_before = move_x(kv, 1)
    kv_other_after = move_x(kv_other, -1)
    kv_other_before = move_x(kv_other, 1)
    kv_after = move_x(kv, -1)
    chip = lax.axis_index("ctx") // 2
    near_use = jnp.stack([chip >= 1, chip == 3]).astype(jnp.int32)
    far_use = jnp.stack([chip >= 2, chip >= 2]).astype(jnp.int32)
    queries = (query, query_other)
    state = attend_own(*queries, kv, kv_other, core)
    kv_before, kv_other_after, state = lax.optimization_barrier((kv_before, kv_other_after, state))
    kv_far = move_x(kv_before, 1)
    kv_other_far = move_x(kv_other_after, -1)
    state = attend_other(*queries, state, [kv_before, kv_other_after], near_use)
    state = attend_other(*queries, state, [kv_other_before, kv_after], near_use)
    own, own_send = attend_other(*queries, state, [kv_far, kv_other_far], far_use, last=True)
    other = swap_core(own_send)

    part = functools.partial(output_part, own, other, seg)
    two_low, two_high = part(w_two, (2, 2))
    two_low = move(two_low, True, 1)
    two_high = move(two_high, True, -1)
    plus_high, minus_low = part(w_first, (2, 2))
    plus_high = move(plus_high, True, 1)
    minus_low = move(minus_low, True, -1)
    plus_low, minus_high = part(w_later, (2, 2))
    plus_low = add(plus_low, two_low)
    minus_high = add(minus_high, two_high)
    plus_low, minus_high, own, other = lax.optimization_barrier((plus_low, minus_high, own, other))
    here = output_part(own, other, seg, w_here, (0, 0, 0, 0))
    plus_low = move(plus_low, True, 1)
    minus_high = move(minus_high, True, -1)
    plus_low, plus_high, minus_low, minus_high = lax.optimization_barrier(
        (plus_low, plus_high, minus_low, minus_high)
    )
    mine, plus, two, minus = (
        add(here[i], (plus_low, plus_high)[i // 2][i % 2], (minus_low, minus_high)[i // 2][i % 2])
        for i in range(4)
    )
    return add(
        tokens, mine, move(plus, False, 1), move(two, False, 2), move(minus, False, -1)
    )


def solution(mesh):
    in_specs = (
        P("ctx", "tp"),
        P("ctx"),
        P(None, None, "tp"),
        P(None, None, "tp"),
        P(None, None, "tp"),
        P(None, "tp", None),
    )
    return jax.shard_map(
        local, mesh=mesh, in_specs=in_specs, out_specs=P("ctx", "tp"), check_vma=False
    )
```

```python
import functools
import math

import jax
import jax.numpy as jnp
import numpy as np
from jax import lax
from jax.experimental import pallas as pl
from jax.experimental.pallas import tpu as pltpu
from jax.sharding import PartitionSpec as P

HD = 128
MODALITIES = 3
EPS = 1e-05
WINDOW = 528
ALIGN = 16
Q_TILE = 512
K_TILE = 1024
STATE_ROWS = HD + 16
AXES = ("ctx", "tp")
BF = jnp.bfloat16
F32 = jnp.float32
OFFSETS = np.array([0, 3, 1, 2])
VMEM_PROJECT = 47 * 1024 * 1024
VMEM_BYTES = 24 * 1024 * 1024
FEATURES = 4096
SPAN = 256
HEADROOM = 2.0**-13


def plane_perm(first, step):
    pairs = []
    for ctx in range(8):
        for z in range(4):
            for y in range(4):
                along_y = (ctx % 2 == 0) == first
                to_z = z if along_y else (z + step) % 4
                to_y = (y + step) % 4 if along_y else y
                pairs.append((ctx * 16 + z * 4 + y, ctx * 16 + to_z * 4 + to_y))
    return pairs


def move(array, first, step):
    return lax.ppermute(array, AXES, plane_perm(first, step))


def move_x(array, step):
    pairs = [(x * 2 + c, ((x + step) % 4) * 2 + c) for x in range(4) for c in range(2)]
    return lax.ppermute(array, "ctx", pairs)


def swap_core(array):
    return lax.ppermute(array, "ctx", [(i, i ^ 1) for i in range(8)])


def shard_table(first_offsets, second_offsets):
    core = lax.axis_index("ctx") % 2
    tp = lax.axis_index("tp")
    z, y = tp // 4, tp % 4
    first_offsets = jnp.asarray(first_offsets, jnp.int32)
    second_offsets = jnp.asarray(second_offsets, jnp.int32)
    first = (jnp.where(core == 0, y, z) + first_offsets) % 4
    second = (jnp.where(core == 0, z, y) + second_offsets) % 4
    return jnp.where(core == 0, second * 4 + first, first * 4 + second).astype(jnp.int32)


def segment_scalars(modality):
    rows = modality.shape[0]
    kinds = jnp.arange(MODALITIES, dtype=jnp.int32)[:, None]
    member = modality[None, :] == kinds
    positions = jnp.arange(rows, dtype=jnp.int32)[None, :]
    begin = jnp.min(jnp.where(member, positions, rows), axis=1)
    end = jnp.max(jnp.where(member, positions + 1, 0), axis=1)
    end = jnp.maximum(end, begin)
    core = lax.axis_index("ctx") % 2
    return jnp.concatenate([begin, end, core[None]]).astype(jnp.int32)


def for_runs(seg_ref, rows, body):
    for kind in range(MODALITIES):
        begin = seg_ref[kind]
        end = seg_ref[MODALITIES + kind]
        first = jnp.minimum(begin // ALIGN * ALIGN, rows - WINDOW)
        first = pl.multiple_of(first, ALIGN)
        positions = first + lax.broadcasted_iota(jnp.int32, (WINDOW, 1), 0)
        body(kind, pl.ds(first, WINDOW), (positions >= begin) & (positions < end))


def constant_spec(shape):
    return pl.BlockSpec(shape, lambda k, *scalars: (0,) * len(shape))


def project(pieces, weights, table, seg, before=None, last=False):
    count = len(pieces)
    shards, rows, width = pieces[0].shape
    depth = count * shards
    out_width = 3 * width
    has_before = before is not None

    def kernel(table_ref, seg_ref, *refs):
        piece_refs = refs[:count]
        weight_refs = refs[count : count + 3]
        refs = refs[count + 3 :]
        if has_before:
            squares_before_ref, before_ref, *refs = refs
        if last:
            query_ref, kv_ref, query_send_ref, kv_send_ref, *refs = refs
        else:
            squares_ref, out_ref, *refs = refs
        held, normed, left, right, total, shrink, piece_sem, weight_sem, total_sem = refs

        spans = [pl.ds(row, SPAN) for row in range(0, rows, SPAN)]
        piece_copies = [
            pltpu.make_async_copy(
                piece_refs[i].at[:, span, :], held.at[i, :, span, :], piece_sem.at[k, i]
            )
            for k, span in enumerate(spans)
            for i in range(count)
        ]
        groups = ((0, 2 * width), (2 * width, out_width))
        weight_copies = ([], [])
        before_copies = ([], [])
        out_copies = []
        for g, (low, high) in enumerate(groups):
            columns = pl.ds(low, high - low)
            for j in range(depth):
                first = pl.multiple_of(table_ref[j] * width, width)
                for i in range(low // width, high // width):
                    weight_copies[g].append(
                        pltpu.make_async_copy(
                            weight_refs[i].at[:, pl.ds(first, width), :],
                            right.at[:, pl.ds(j * width, width), pl.ds(i * width, width)],
                            weight_sem.at[i, j],
                        )
                    )
            for k, span in enumerate(spans):
                if has_before:
                    before_copies[g].append(
                        pltpu.make_async_copy(
                            before_ref.at[span, columns],
                            total.at[span, columns],
                            total_sem.at[0, g, k],
                        )
                    )
                if not last:
                    out_copies.append(
                        pltpu.make_async_copy(
                            total.at[span, columns],
                            out_ref.at[span, columns],
                            total_sem.at[1, g, k],
                        )
                    )
        for copy in piece_copies:
            copy.start()
        for g in range(2):
            for copy in weight_copies[g] + before_copies[g]:
                copy.start()

        for row in range(0, rows, HD):
            at = slice(row, row + HD)
            if row % SPAN == 0:
                k = row // SPAN
                for copy in piece_copies[k * count : (k + 1) * count]:
                    copy.wait()
            by_lane = jnp.zeros((HD, HD), F32)
            for i in range(count):
                for j in range(shards):
                    for column in range(0, width, HD):
                        by_lane += jnp.square(held[i, j, at, column : column + HD].astype(F32))
            squares = jnp.sum(by_lane, axis=1, keepdims=True)
            if has_before:
                squares_before = squares_before_ref[at, :]
                scale_before = lax.rsqrt(squares_before / FEATURES + EPS)
                squares += squares_before
            scale = lax.rsqrt(squares / FEATURES + EPS)
            if has_before:
                shrink[at, :] = jnp.where(scale_before > 0.0, scale / scale_before, 0.0)
            if not last:
                squares_ref[at, :] = squares
            for j in range(depth):
                piece = held[j // shards, j % shards, at, :].astype(F32)
                normed[at, j * width : (j + 1) * width] = (piece * (scale * HEADROOM)).astype(BF)

        def mask(kind, at, keep):
            left[kind] = normed[at, :] * keep.astype(BF)

        for_runs(seg_ref, rows, mask)
        for g, (low, high) in enumerate(groups):
            for copy in weight_copies[g] + before_copies[g]:
                copy.wait()
            if has_before:
                total[:, low:high] *= shrink[...]
            else:
                total[:, low:high] = jnp.zeros((rows, high - low), F32)

            def run(kind, at, keep, low=low, high=high):
                total[at, low:high] += jnp.dot(
                    left[kind], right[kind, :, low:high], preferred_element_type=F32
                )

            for_runs(seg_ref, rows, run)
            if not last:
                for copy in out_copies[g * len(spans) : (g + 1) * len(spans)]:
                    copy.start()
        for copy in out_copies:
            copy.wait()

        if last:
            query_scale = math.log2(math.e) / math.sqrt(HD) / HEADROOM
            core = seg_ref[2 * MODALITIES]
            for mine in range(2):

                @pl.when(core == mine)
                def _(mine=mine):
                    for head, q_out, kv_out in (
                        (mine, query_ref, kv_ref),
                        (1 - mine, query_send_ref, kv_send_ref),
                    ):
                        at = head * HD
                        kv_out[:, :HD] = (total[:, at : at + HD] / HEADROOM).astype(BF)
                        at += width
                        for row in range(0, rows, HD):
                            block = total[row : row + HD, at : at + HD] / HEADROOM
                            kv_out[row : row + HD, HD:] = block.T.astype(BF)
                        at += width
                        q_out[...] = (total[:, at : at + HD] * query_scale).astype(BF)

    vmem = pl.BlockSpec(memory_space=pltpu.VMEM)
    operands = [table, seg, *pieces, *weights]
    in_specs = [pl.BlockSpec(memory_space=pltpu.SMEM)] * 2
    in_specs += [pl.BlockSpec(memory_space=pl.ANY)] * count
    in_specs += [pl.BlockSpec(memory_space=pl.ANY)] * 3
    if has_before:
        operands += before
        in_specs += [vmem, pl.BlockSpec(memory_space=pl.ANY)]
    if last:
        shapes = [(rows, HD), (rows, 2 * HD)] * 2
        out_shape = tuple(jax.ShapeDtypeStruct(shape, BF) for shape in shapes)
        out_specs = (vmem,) * 4
    else:
        out_shape = (
            jax.ShapeDtypeStruct((rows, 1), F32),
            jax.ShapeDtypeStruct((rows, 3 * width), F32),
        )
        out_specs = (vmem, pl.BlockSpec(memory_space=pl.ANY))
    return pl.pallas_call(
        kernel,
        in_specs=in_specs,
        out_specs=out_specs,
        scratch_shapes=[
            pltpu.VMEM((count, shards, rows, width), BF),
            pltpu.VMEM((rows, depth * width), BF),
            pltpu.VMEM((MODALITIES, WINDOW, depth * width), BF),
            pltpu.VMEM((MODALITIES, depth * width, 3 * width), BF),
            pltpu.VMEM((rows, out_width), F32),
            pltpu.VMEM((rows, 1), F32),
            pltpu.SemaphoreType.DMA((rows // SPAN, count)),
            pltpu.SemaphoreType.DMA((3, depth)),
            pltpu.SemaphoreType.DMA((2, 2, rows // SPAN)),
        ],
        out_shape=out_shape,
        compiler_params=pltpu.CompilerParams(vmem_limit_bytes=VMEM_PROJECT),
        cost_estimate=pl.CostEstimate(
            flops=2 * depth * 3 * WINDOW * width * 3 * width,
            bytes_accessed=depth * (rows * width * 2 + 9 * width * width * 2),
            transcendentals=0,
        ),
    )(*operands)


def score(query, key, keep=None):
    scores = lax.dot_general(key, query, (((1,), (1,)), ((), ())), preferred_element_type=F32)
    return scores if keep is None else jnp.where(keep, scores, -1e30)


def fold(state, scores, value_t):
    top, total, summed = state
    new_top = jnp.maximum(top, jnp.max(scores, axis=0, keepdims=True))
    factor = jnp.exp2(top - new_top)
    weights = jnp.exp2(scores - new_top)
    total = total * factor + jnp.sum(weights, axis=0, keepdims=True)
    summed = summed * factor + jnp.dot(value_t, weights.astype(BF), preferred_element_type=F32)
    return new_top, total, summed


def empty_state():
    return (
        jnp.full((1, Q_TILE), -1e30, F32),
        jnp.zeros((1, Q_TILE), F32),
        jnp.zeros((HD, Q_TILE), F32),
    )


def store_state(state, state_ref):
    top, total, summed = state
    state_ref[0, :HD, :] = summed
    state_ref[0, HD : HD + 8, :] = jnp.broadcast_to(top, (8, Q_TILE))
    state_ref[0, HD + 8 :, :] = jnp.broadcast_to(total, (8, Q_TILE))


def load_state(state_ref):
    return (
        state_ref[0, HD : HD + 1, :],
        state_ref[0, HD + 8 : HD + 9, :],
        state_ref[0, :HD, :],
    )


def read_keys(ref, first, count):
    key = ref[pl.ds(first, count), :HD]
    blocks = [ref[pl.ds(first + i, HD), HD:] for i in range(0, count, HD)]
    return key, jnp.concatenate(blocks, axis=1)


def attend_own(query, query_other, kv, kv_other, core):
    rows = query.shape[0]
    per_block = rows // Q_TILE
    tiles = 2 * per_block

    def kernel(core_ref, query_ref, query_other_ref, kv_ref, kv_other_ref, state_ref, keys, both):
        place = pl.program_id(0)

        @pl.when(place == 0)
        def _():
            for mine in range(2):

                @pl.when(core_ref[0] == mine)
                def _(mine=mine):
                    at, other = mine * rows, (1 - mine) * rows
                    keys[at : at + rows, :] = kv_ref[...]
                    keys[other : other + rows, :] = kv_other_ref[...]
                    both[at : at + rows, :] = query_ref[...]
                    both[other : other + rows, :] = query_other_ref[...]

        at = pl.multiple_of(place * Q_TILE, Q_TILE)
        q = both[pl.ds(at, Q_TILE), :]
        causal = lax.broadcasted_iota(
            jnp.int32, (Q_TILE, Q_TILE), 0
        ) <= lax.broadcasted_iota(jnp.int32, (Q_TILE, Q_TILE), 1)
        key, value_t = read_keys(keys, at, Q_TILE)
        state = fold(empty_state(), score(q, key, causal), value_t)

        def earlier(tile, state):
            key, value_t = read_keys(keys, pl.multiple_of(tile * Q_TILE, Q_TILE), Q_TILE)
            return fold(state, score(q, key), value_t)

        store_state(lax.fori_loop(0, place, earlier, state), state_ref)

    whole = constant_spec((rows, HD))
    whole_kv = constant_spec((rows, 2 * HD))
    return pl.pallas_call(
        kernel,
        grid_spec=pltpu.PrefetchScalarGridSpec(
            num_scalar_prefetch=1,
            grid=(tiles,),
            in_specs=[whole, whole, whole_kv, whole_kv],
            out_specs=pl.BlockSpec(
                (1, STATE_ROWS, Q_TILE),
                lambda i, core: ((i + core[0] * per_block) % tiles, 0, 0),
            ),
            scratch_shapes=[
                pltpu.VMEM((2 * rows, 2 * HD), BF),
                pltpu.VMEM((2 * rows, HD), BF),
            ],
        ),
        out_shape=jax.ShapeDtypeStruct((tiles, STATE_ROWS, Q_TILE), F32),
        compiler_params=pltpu.CompilerParams(vmem_limit_bytes=VMEM_BYTES),
        cost_estimate=pl.CostEstimate(
            flops=10 * Q_TILE * Q_TILE * HD * 4,
            bytes_accessed=4 << 20,
            transcendentals=10 * Q_TILE * Q_TILE,
        ),
    )(core, query, query_other, kv, kv_other)


def attend_other(query, query_other, state, sources, use, last=False):
    rows = query.shape[0]
    per_block = rows // Q_TILE
    tiles = 2 * per_block
    count = len(sources)

    def kernel(use_ref, query_ref, query_other_ref, before_ref, *refs):
        source_refs = refs[:count]
        *out_refs, after, q_ref = refs[count:]
        tile = pl.program_id(0)

        @pl.when(tile < per_block)
        def _():
            q_ref[...] = query_ref[...]

        @pl.when(tile >= per_block)
        def _():
            q_ref[...] = query_other_ref[...]

        q = q_ref[...]
        after[...] = before_ref[...]

        def fold_in(refs):
            parts = [(ref, at) for ref in refs for at in range(0, rows, K_TILE)]
            state = load_state(after)
            scores = None
            for i, (ref, at) in enumerate(parts):
                key, value_t = read_keys(ref, at, K_TILE)
                if scores is None:
                    scores = score(q, key)
                later = None
                if i + 1 < len(parts):
                    next_ref, next_at = parts[i + 1]
                    later = score(q, next_ref[next_at : next_at + K_TILE, :HD])
                state = fold(state, scores, value_t)
                scores = later
            store_state(state, after)

        all_used = use_ref[0]
        for i in range(1, count):
            all_used = all_used & use_ref[i]

        @pl.when(all_used != 0)
        def _():
            fold_in(source_refs)

        for i, source_ref in enumerate(source_refs):

            @pl.when((all_used == 0) & (use_ref[i] != 0))
            def _(source_ref=source_ref):
                fold_in([source_ref])

        if last:
            _, total, summed = load_state(after)
            attended = (summed / total).T.astype(BF)
            for part, out_ref in enumerate(out_refs):

                @pl.when(tile // per_block == part)
                def _(out_ref=out_ref):
                    at = pl.multiple_of(tile % per_block * Q_TILE, Q_TILE)
                    out_ref[pl.ds(at, Q_TILE), :] = attended

        else:
            out_refs[0][...] = after[...]

    state_spec = pl.BlockSpec((1, STATE_ROWS, Q_TILE), lambda i, use: (i, 0, 0))
    if last:
        out_shape = (jax.ShapeDtypeStruct((rows, HD), BF),) * 2
        out_specs = (constant_spec((rows, HD)),) * 2
    else:
        out_shape = jax.ShapeDtypeStruct((tiles, STATE_ROWS, Q_TILE), F32)
        out_specs = state_spec
    return pl.pallas_call(
        kernel,
        grid_spec=pltpu.PrefetchScalarGridSpec(
            num_scalar_prefetch=1,
            grid=(tiles,),
            in_specs=[
                pl.BlockSpec((Q_TILE, HD), lambda i, use: (jnp.minimum(i, per_block - 1), 0)),
                pl.BlockSpec((Q_TILE, HD), lambda i, use: (jnp.maximum(i - per_block, 0), 0)),
                state_spec,
            ]
            + [constant_spec(source.shape) for source in sources],
            out_specs=out_specs,
            scratch_shapes=[
                pltpu.VMEM((1, STATE_ROWS, Q_TILE), F32),
                pltpu.VMEM((Q_TILE, HD), BF),
            ],
        ),
        out_shape=out_shape,
        compiler_params=pltpu.CompilerParams(vmem_limit_bytes=VMEM_BYTES),
        cost_estimate=pl.CostEstimate(
            flops=2 * rows * count * rows * HD * 4,
            bytes_accessed=6 << 20,
            transcendentals=2 * rows * count * rows,
        ),
    )(use, query, query_other, state, *sources)


def pick_weights(w_out, table):
    depth, width = w_out.shape[1], 2 * HD

    def kernel(table_ref, weight_ref, out_ref):
        out_ref[0] = weight_ref[...]

    return pl.pallas_call(
        kernel,
        grid_spec=pltpu.PrefetchScalarGridSpec(
            num_scalar_prefetch=1,
            grid=(4,),
            in_specs=[pl.BlockSpec((MODALITIES, depth, width), lambda k, t: (0, 0, t[k]))],
            out_specs=pl.BlockSpec((1, MODALITIES, depth, width), lambda k, t: (k, 0, 0, 0)),
        ),
        out_shape=jax.ShapeDtypeStruct((4, MODALITIES, depth, width), BF),
        compiler_params=pltpu.CompilerParams(vmem_limit_bytes=VMEM_BYTES),
        cost_estimate=pl.CostEstimate(flops=0, bytes_accessed=3 << 20, transcendentals=0),
    )(table, w_out)


def output_part(own, other, weights, table, seg, sizes):
    blocks = table.shape[0]
    rows = own.shape[0]
    width = 2 * HD
    picked = weights.ndim == 4

    def kernel(table_ref, seg_ref, own_ref, other_ref, weight_ref, *refs):
        *out_refs, attended, left, right, total, result, weight_sem, out_sem = refs
        weight_copies = []
        for i in range(blocks):
            first = pl.multiple_of(table_ref[i] * width, width)
            weight_copies.append(
                pltpu.make_async_copy(
                    weight_ref.at[i] if picked else weight_ref.at[:, :, pl.ds(first, width)],
                    right.at[i // 2, :, :, pl.ds(i % 2 * width, width)],
                    weight_sem.at[i],
                )
            )
            weight_copies[i].start()
        core = seg_ref[2 * MODALITIES]
        for mine in range(2):

            @pl.when(core == mine)
            def _(mine=mine):
                attended[:, mine * HD : (mine + 1) * HD] = own_ref[...]
                attended[:, (1 - mine) * HD : (2 - mine) * HD] = other_ref[...]

        def mask(kind, at, keep):
            left[kind] = attended[at, :] * keep.astype(BF)

        for_runs(seg_ref, rows, mask)
        out_copies = []
        for pair in range(blocks // 2):
            weight_copies[2 * pair].wait()
            weight_copies[2 * pair + 1].wait()
            total[...] = jnp.zeros_like(total)

            def run(kind, at, keep, pair=pair):
                total[at, :] += jnp.dot(left[kind], right[pair, kind], preferred_element_type=F32)

            for_runs(seg_ref, rows, run)
            for i in range(2):
                result[2 * pair + i] = total[:, i * width : (i + 1) * width].astype(BF)
            done = 0
            for size, out_ref in zip(sizes, out_refs):
                if done // 2 == pair:
                    source = result.at[pl.ds(done, 2)] if size else result.at[done]
                    out_copies.append(
                        pltpu.make_async_copy(source, out_ref, out_sem.at[len(out_copies)])
                    )
                    out_copies[-1].start()
                done += max(size, 1)
        for copy in out_copies:
            copy.wait()

    vmem = pl.BlockSpec(memory_space=pltpu.VMEM)
    shapes = [(size, rows, width) if size else (rows, width) for size in sizes]
    return pl.pallas_call(
        kernel,
        in_specs=[pl.BlockSpec(memory_space=pltpu.SMEM)] * 2
        + [vmem, vmem, pl.BlockSpec(memory_space=pl.ANY)],
        out_specs=(pl.BlockSpec(memory_space=pl.ANY),) * len(shapes),
        scratch_shapes=[
            pltpu.VMEM((rows, width), BF),
            pltpu.VMEM((MODALITIES, WINDOW, width), BF),
            pltpu.VMEM((blocks // 2, MODALITIES, width, 2 * width), BF),
            pltpu.VMEM((rows, 2 * width), F32),
            pltpu.VMEM((blocks, rows, width), BF),
            pltpu.SemaphoreType.DMA((blocks,)),
            pltpu.SemaphoreType.DMA((len(shapes),)),
        ],
        out_shape=tuple(jax.ShapeDtypeStruct(shape, BF) for shape in shapes),
        compiler_params=pltpu.CompilerParams(vmem_limit_bytes=VMEM_BYTES),
        cost_estimate=pl.CostEstimate(flops=0, bytes_accessed=rows, transcendentals=0),
    )(table, seg, own, other, weights)


def add(*arrays):
    return sum(array.astype(F32) for array in arrays).astype(BF)


def local(tokens, modality, w_query, w_key, w_value, w_out):
    seg = segment_scalars(modality)
    core = seg[2 * MODALITIES :]
    weights = (w_key, w_value, w_query)

    low = jnp.stack([tokens, move(tokens, True, 1)])
    high = jnp.stack([move(tokens, True, -1), move(tokens, True, 2)])
    before_low = move(low, False, 1)
    after_high = move(high, False, -1)
    before_high = move(high, False, 1)
    after_low = move(low, False, -1)
    table = shard_table(np.tile(OFFSETS, 4), np.repeat(OFFSETS, 4))
    partial = project([low, high], weights, table[:4], seg)
    before_low, after_high, partial = lax.optimization_barrier((before_low, after_high, partial))
    far_low = move(before_low, False, 1)
    far_high = move(after_high, False, -1)
    first = jnp.concatenate([table[4:6], table[10:12]])
    partial = project([before_low, after_high], weights, first, seg, before=partial)
    partial = project([before_high, after_low], weights, table[6:10], seg, before=partial)
    query, kv, query_send, kv_send = project(
        [far_low, far_high], weights, table[12:], seg, before=partial, last=True
    )

    kv_other = swap_core(kv_send)
    query_other = swap_core(query_send)
    kv_before = move_x(kv, 1)
    kv_other_after = move_x(kv_other, -1)
    kv_other_before = move_x(kv_other, 1)
    kv_after = move_x(kv, -1)
    chip = lax.axis_index("ctx") // 2
    near_use = jnp.stack([chip >= 1, chip == 3]).astype(jnp.int32)
    far_use = jnp.stack([chip >= 2, chip >= 2]).astype(jnp.int32)
    queries = (query, query_other)
    state = attend_own(*queries, kv, kv_other, core)
    here, plus, two, minus = (shard_table(np.full(4, offset), np.arange(4)) for offset in range(4))
    kv_before, kv_other_after, state, w_two = lax.optimization_barrier(
        (kv_before, kv_other_after, state, pick_weights(w_out, two))
    )
    kv_far = move_x(kv_before, 1)
    kv_other_far = move_x(kv_other_after, -1)
    state = attend_other(*queries, state, [kv_before, kv_other_after], near_use)
    state = attend_other(*queries, state, [kv_other_before, kv_after], near_use)
    own, own_send = attend_other(*queries, state, [kv_far, kv_other_far], far_use, last=True)
    other = swap_core(own_send)

    part = functools.partial(output_part, own, other)
    two_low, two_high = part(w_two, two, seg, (2, 2))
    two_low = move(two_low, True, 1)
    two_high = move(two_high, True, -1)
    first = jnp.concatenate([plus[2:], minus[:2]])
    plus_high, minus_low = part(w_out, first, seg, (2, 2))
    plus_high = move(plus_high, True, 1)
    minus_low = move(minus_low, True, -1)
    later = jnp.concatenate([plus[:2], minus[2:]])
    plus_low, minus_high = part(w_out, later, seg, (2, 2))
    plus_low = add(plus_low, two_low)
    minus_high = add(minus_high, two_high)
    plus_low, minus_high, own, other = lax.optimization_barrier((plus_low, minus_high, own, other))
    here = output_part(own, other, w_out, here, seg, (0, 0, 0, 0))
    plus_low = move(plus_low, True, 1)
    minus_high = move(minus_high, True, -1)
    plus_low, plus_high, minus_low, minus_high = lax.optimization_barrier(
        (plus_low, plus_high, minus_low, minus_high)
    )
    mine, plus, two, minus = (
        add(here[i], (plus_low, plus_high)[i // 2][i % 2], (minus_low, minus_high)[i // 2][i % 2])
        for i in range(4)
    )
    return add(
        tokens, mine, move(plus, False, 1), move(two, False, 2), move(minus, False, -1)
    )


def solution(mesh):
    in_specs = (
        P("ctx", "tp"),
        P("ctx"),
        P(None, None, "tp"),
        P(None, None, "tp"),
        P(None, None, "tp"),
        P(None, "tp", None),
    )
    return jax.shard_map(
        local, mesh=mesh, in_specs=in_specs, out_specs=P("ctx", "tp"), check_vma=False
    )
```

```python
import functools
import math

import jax
import jax.numpy as jnp
import numpy as np
from jax import lax
from jax.experimental import pallas as pl
from jax.experimental.pallas import tpu as pltpu
from jax.sharding import PartitionSpec as P

HD = 128
MODALITIES = 3
EPS = 1e-05
WINDOW = 528
ALIGN = 16
Q_TILE = 512
K_TILE = 1024
STATE_ROWS = HD + 16
AXES = ("ctx", "tp")
BF = jnp.bfloat16
F32 = jnp.float32
VMEM_PROJECT = 50 * 1024 * 1024
VMEM_BYTES = 24 * 1024 * 1024
FEATURES = 4096
SPAN = 256
HEADROOM = 2.0**-13


def plane_perm(first, step):
    pairs = []
    for ctx in range(8):
        for z in range(4):
            for y in range(4):
                along_y = (ctx % 2 == 0) == first
                to_z = z if along_y else (z + step) % 4
                to_y = (y + step) % 4 if along_y else y
                pairs.append((ctx * 16 + z * 4 + y, ctx * 16 + to_z * 4 + to_y))
    return pairs


def move(array, first, step):
    return lax.ppermute(array, AXES, plane_perm(first, step))


def move_x(array, step):
    pairs = [(x * 2 + c, ((x + step) % 4) * 2 + c) for x in range(4) for c in range(2)]
    return lax.ppermute(array, "ctx", pairs)


def swap_core(array):
    return lax.ppermute(array, "ctx", [(i, i ^ 1) for i in range(8)])


def shard_table(first_offsets, second_offsets):
    core = lax.axis_index("ctx") % 2
    tp = lax.axis_index("tp")
    z, y = tp // 4, tp % 4
    first_offsets = jnp.asarray(first_offsets, jnp.int32)
    second_offsets = jnp.asarray(second_offsets, jnp.int32)
    first = (jnp.where(core == 0, y, z) + first_offsets) % 4
    second = (jnp.where(core == 0, z, y) + second_offsets) % 4
    return jnp.where(core == 0, second * 4 + first, first * 4 + second).astype(jnp.int32)


def segment_scalars(modality):
    rows = modality.shape[0]
    kinds = jnp.arange(MODALITIES, dtype=jnp.int32)[:, None]
    member = modality[None, :] == kinds
    positions = jnp.arange(rows, dtype=jnp.int32)[None, :]
    begin = jnp.min(jnp.where(member, positions, rows), axis=1)
    end = jnp.max(jnp.where(member, positions + 1, 0), axis=1)
    end = jnp.maximum(end, begin)
    core = lax.axis_index("ctx") % 2
    return jnp.concatenate([begin, end, core[None]]).astype(jnp.int32)


def for_runs(seg_ref, rows, body):
    for kind in range(MODALITIES):
        begin = seg_ref[kind]
        end = seg_ref[MODALITIES + kind]
        first = jnp.minimum(begin // ALIGN * ALIGN, rows - WINDOW)
        first = pl.multiple_of(first, ALIGN)
        positions = first + lax.broadcasted_iota(jnp.int32, (WINDOW, 1), 0)
        body(kind, pl.ds(first, WINDOW), (positions >= begin) & (positions < end))


def constant_spec(shape):
    return pl.BlockSpec(shape, lambda k, *scalars: (0,) * len(shape))


def project(pieces, weights, table, seg, before=None, last=False):
    count = len(pieces)
    counts = [piece.shape[0] for piece in pieces]
    firsts = [sum(counts[:i]) for i in range(count)]
    depth = sum(counts)
    rows, width = pieces[0].shape[1:]
    out_width = 3 * width
    has_before = before is not None

    def kernel(table_ref, seg_ref, *refs):
        piece_refs = refs[:count]
        weight_refs = refs[count : count + 3]
        refs = refs[count + 3 :]
        if has_before:
            squares_before_ref, before_ref, *refs = refs
        if last:
            query_ref, kv_ref, query_send_ref, kv_send_ref, *refs = refs
        else:
            squares_ref, out_ref, *refs = refs
        held, normed, left, right, total, shrink, piece_sem, weight_sem, total_sem = refs

        spans = [pl.ds(row, SPAN) for row in range(0, rows, SPAN)]
        piece_copies = [
            pltpu.make_async_copy(
                piece_refs[i].at[:, span, :],
                held.at[pl.ds(firsts[i], counts[i]), span, :],
                piece_sem.at[k, i],
            )
            for k, span in enumerate(spans)
            for i in range(count)
        ]
        groups = ((0, 2 * width), (2 * width, out_width))
        weight_copies = ([], [])
        before_copies = ([], [])
        out_copies = []
        for g, (low, high) in enumerate(groups):
            columns = pl.ds(low, high - low)
            for j in range(depth):
                first = pl.multiple_of(table_ref[j] * width, width)
                for i in range(low // width, high // width):
                    weight_copies[g].append(
                        pltpu.make_async_copy(
                            weight_refs[i].at[:, pl.ds(first, width), :],
                            right.at[:, pl.ds(j * width, width), pl.ds(i * width, width)],
                            weight_sem.at[i, j],
                        )
                    )
            for k, span in enumerate(spans):
                if has_before:
                    before_copies[g].append(
                        pltpu.make_async_copy(
                            before_ref.at[span, columns],
                            total.at[span, columns],
                            total_sem.at[0, g, k],
                        )
                    )
                if not last:
                    out_copies.append(
                        pltpu.make_async_copy(
                            total.at[span, columns],
                            out_ref.at[span, columns],
                            total_sem.at[1, g, k],
                        )
                    )
        for copy in piece_copies:
            copy.start()
        for g in range(2):
            for copy in weight_copies[g] + before_copies[g]:
                copy.start()

        for row in range(0, rows, HD):
            at = slice(row, row + HD)
            if row % SPAN == 0:
                k = row // SPAN
                for copy in piece_copies[k * count : (k + 1) * count]:
                    copy.wait()
            by_lane = jnp.zeros((HD, HD), F32)
            for j in range(depth):
                for column in range(0, width, HD):
                    by_lane += jnp.square(held[j, at, column : column + HD].astype(F32))
            squares = jnp.sum(by_lane, axis=1, keepdims=True)
            if has_before:
                squares_before = squares_before_ref[at, :]
                scale_before = lax.rsqrt(squares_before / FEATURES + EPS)
                squares += squares_before
            scale = lax.rsqrt(squares / FEATURES + EPS)
            if has_before:
                shrink[at, :] = jnp.where(scale_before > 0.0, scale / scale_before, 0.0)
            if not last:
                squares_ref[at, :] = squares
            for j in range(depth):
                piece = held[j, at, :].astype(F32)
                normed[at, j * width : (j + 1) * width] = (piece * (scale * HEADROOM)).astype(BF)

        def mask(kind, at, keep):
            left[kind] = normed[at, :] * keep.astype(BF)

        for_runs(seg_ref, rows, mask)
        for g, (low, high) in enumerate(groups):
            for copy in weight_copies[g] + before_copies[g]:
                copy.wait()
            if has_before:
                total[:, low:high] *= shrink[...]
            else:
                total[:, low:high] = jnp.zeros((rows, high - low), F32)

            def run(kind, at, keep, low=low, high=high):
                total[at, low:high] += jnp.dot(
                    left[kind], right[kind, :, low:high], preferred_element_type=F32
                )

            for_runs(seg_ref, rows, run)
            if not last:
                for copy in out_copies[g * len(spans) : (g + 1) * len(spans)]:
                    copy.start()
        for copy in out_copies:
            copy.wait()

        if last:
            query_scale = math.log2(math.e) / math.sqrt(HD) / HEADROOM
            core = seg_ref[2 * MODALITIES]
            for mine in range(2):

                @pl.when(core == mine)
                def _(mine=mine):
                    for head, q_out, kv_out in (
                        (mine, query_ref, kv_ref),
                        (1 - mine, query_send_ref, kv_send_ref),
                    ):
                        at = head * HD
                        kv_out[:, :HD] = (total[:, at : at + HD] / HEADROOM).astype(BF)
                        at += width
                        for row in range(0, rows, HD):
                            block = total[row : row + HD, at : at + HD] / HEADROOM
                            kv_out[row : row + HD, HD:] = block.T.astype(BF)
                        at += width
                        q_out[...] = (total[:, at : at + HD] * query_scale).astype(BF)

    vmem = pl.BlockSpec(memory_space=pltpu.VMEM)
    operands = [table, seg, *pieces, *weights]
    in_specs = [pl.BlockSpec(memory_space=pltpu.SMEM)] * 2
    in_specs += [pl.BlockSpec(memory_space=pl.ANY)] * count
    in_specs += [pl.BlockSpec(memory_space=pl.ANY)] * 3
    if has_before:
        operands += before
        in_specs += [vmem, pl.BlockSpec(memory_space=pl.ANY)]
    if last:
        shapes = [(rows, HD), (rows, 2 * HD)] * 2
        out_shape = tuple(jax.ShapeDtypeStruct(shape, BF) for shape in shapes)
        out_specs = (vmem,) * 4
    else:
        out_shape = (
            jax.ShapeDtypeStruct((rows, 1), F32),
            jax.ShapeDtypeStruct((rows, 3 * width), F32),
        )
        out_specs = (vmem, pl.BlockSpec(memory_space=pl.ANY))
    return pl.pallas_call(
        kernel,
        in_specs=in_specs,
        out_specs=out_specs,
        scratch_shapes=[
            pltpu.VMEM((depth, rows, width), BF),
            pltpu.VMEM((rows, depth * width), BF),
            pltpu.VMEM((MODALITIES, WINDOW, depth * width), BF),
            pltpu.VMEM((MODALITIES, depth * width, 3 * width), BF),
            pltpu.VMEM((rows, out_width), F32),
            pltpu.VMEM((rows, 1), F32),
            pltpu.SemaphoreType.DMA((rows // SPAN, count)),
            pltpu.SemaphoreType.DMA((3, depth)),
            pltpu.SemaphoreType.DMA((2, 2, rows // SPAN)),
        ],
        out_shape=out_shape,
        compiler_params=pltpu.CompilerParams(vmem_limit_bytes=VMEM_PROJECT),
        cost_estimate=pl.CostEstimate(
            flops=2 * depth * 3 * WINDOW * width * 3 * width,
            bytes_accessed=depth * (rows * width * 2 + 9 * width * width * 2),
            transcendentals=0,
        ),
    )(*operands)


def score(query, key, keep=None):
    scores = lax.dot_general(key, query, (((1,), (1,)), ((), ())), preferred_element_type=F32)
    return scores if keep is None else jnp.where(keep, scores, -1e30)


def fold(state, scores, value_t):
    top, total, summed = state
    new_top = jnp.maximum(top, jnp.max(scores, axis=0, keepdims=True))
    factor = jnp.exp2(top - new_top)
    weights = jnp.exp2(scores - new_top)
    total = total * factor + jnp.sum(weights, axis=0, keepdims=True)
    summed = summed * factor + jnp.dot(value_t, weights.astype(BF), preferred_element_type=F32)
    return new_top, total, summed


def empty_state():
    return (
        jnp.full((1, Q_TILE), -1e30, F32),
        jnp.zeros((1, Q_TILE), F32),
        jnp.zeros((HD, Q_TILE), F32),
    )


def store_state(state, state_ref):
    top, total, summed = state
    state_ref[0, :HD, :] = summed
    state_ref[0, HD : HD + 8, :] = jnp.broadcast_to(top, (8, Q_TILE))
    state_ref[0, HD + 8 :, :] = jnp.broadcast_to(total, (8, Q_TILE))


def load_state(state_ref):
    return (
        state_ref[0, HD : HD + 1, :],
        state_ref[0, HD + 8 : HD + 9, :],
        state_ref[0, :HD, :],
    )


def read_keys(ref, first, count):
    key = ref[pl.ds(first, count), :HD]
    blocks = [ref[pl.ds(first + i, HD), HD:] for i in range(0, count, HD)]
    return key, jnp.concatenate(blocks, axis=1)


def attend_own(query, query_other, kv, kv_other, core):
    rows = query.shape[0]
    per_block = rows // Q_TILE
    tiles = 2 * per_block

    def kernel(core_ref, query_ref, query_other_ref, kv_ref, kv_other_ref, state_ref, keys, both):
        place = pl.program_id(0)

        @pl.when(place == 0)
        def _():
            for mine in range(2):

                @pl.when(core_ref[0] == mine)
                def _(mine=mine):
                    at, other = mine * rows, (1 - mine) * rows
                    keys[at : at + rows, :] = kv_ref[...]
                    keys[other : other + rows, :] = kv_other_ref[...]
                    both[at : at + rows, :] = query_ref[...]
                    both[other : other + rows, :] = query_other_ref[...]

        at = pl.multiple_of(place * Q_TILE, Q_TILE)
        q = both[pl.ds(at, Q_TILE), :]
        causal = lax.broadcasted_iota(
            jnp.int32, (Q_TILE, Q_TILE), 0
        ) <= lax.broadcasted_iota(jnp.int32, (Q_TILE, Q_TILE), 1)
        key, value_t = read_keys(keys, at, Q_TILE)
        state = fold(empty_state(), score(q, key, causal), value_t)

        def earlier(tile, state):
            key, value_t = read_keys(keys, pl.multiple_of(tile * Q_TILE, Q_TILE), Q_TILE)
            return fold(state, score(q, key), value_t)

        store_state(lax.fori_loop(0, place, earlier, state), state_ref)

    whole = constant_spec((rows, HD))
    whole_kv = constant_spec((rows, 2 * HD))
    return pl.pallas_call(
        kernel,
        grid_spec=pltpu.PrefetchScalarGridSpec(
            num_scalar_prefetch=1,
            grid=(tiles,),
            in_specs=[whole, whole, whole_kv, whole_kv],
            out_specs=pl.BlockSpec(
                (1, STATE_ROWS, Q_TILE),
                lambda i, core: ((i + core[0] * per_block) % tiles, 0, 0),
            ),
            scratch_shapes=[
                pltpu.VMEM((2 * rows, 2 * HD), BF),
                pltpu.VMEM((2 * rows, HD), BF),
            ],
        ),
        out_shape=jax.ShapeDtypeStruct((tiles, STATE_ROWS, Q_TILE), F32),
        compiler_params=pltpu.CompilerParams(vmem_limit_bytes=VMEM_BYTES),
        cost_estimate=pl.CostEstimate(
            flops=10 * Q_TILE * Q_TILE * HD * 4,
            bytes_accessed=4 << 20,
            transcendentals=10 * Q_TILE * Q_TILE,
        ),
    )(core, query, query_other, kv, kv_other)


def attend_other(query, query_other, state, sources, use, last=False):
    rows = query.shape[0]
    per_block = rows // Q_TILE
    tiles = 2 * per_block
    count = len(sources)

    def kernel(use_ref, query_ref, query_other_ref, before_ref, *refs):
        source_refs = refs[:count]
        *out_refs, after, q_ref = refs[count:]
        tile = pl.program_id(0)

        @pl.when(tile < per_block)
        def _():
            q_ref[...] = query_ref[...]

        @pl.when(tile >= per_block)
        def _():
            q_ref[...] = query_other_ref[...]

        q = q_ref[...]
        after[...] = before_ref[...]

        def fold_in(refs):
            parts = [(ref, at) for ref in refs for at in range(0, rows, K_TILE)]
            state = load_state(after)
            scores = None
            for i, (ref, at) in enumerate(parts):
                key, value_t = read_keys(ref, at, K_TILE)
                if scores is None:
                    scores = score(q, key)
                later = None
                if i + 1 < len(parts):
                    next_ref, next_at = parts[i + 1]
                    later = score(q, next_ref[next_at : next_at + K_TILE, :HD])
                state = fold(state, scores, value_t)
                scores = later
            store_state(state, after)

        all_used = use_ref[0]
        for i in range(1, count):
            all_used = all_used & use_ref[i]

        @pl.when(all_used != 0)
        def _():
            fold_in(source_refs)

        for i, source_ref in enumerate(source_refs):

            @pl.when((all_used == 0) & (use_ref[i] != 0))
            def _(source_ref=source_ref):
                fold_in([source_ref])

        if last:
            _, total, summed = load_state(after)
            attended = (summed / total).T.astype(BF)
            for part, out_ref in enumerate(out_refs):

                @pl.when(tile // per_block == part)
                def _(out_ref=out_ref):
                    at = pl.multiple_of(tile % per_block * Q_TILE, Q_TILE)
                    out_ref[pl.ds(at, Q_TILE), :] = attended

        else:
            out_refs[0][...] = after[...]

    state_spec = pl.BlockSpec((1, STATE_ROWS, Q_TILE), lambda i, use: (i, 0, 0))
    if last:
        out_shape = (jax.ShapeDtypeStruct((rows, HD), BF),) * 2
        out_specs = (constant_spec((rows, HD)),) * 2
    else:
        out_shape = jax.ShapeDtypeStruct((tiles, STATE_ROWS, Q_TILE), F32)
        out_specs = state_spec
    return pl.pallas_call(
        kernel,
        grid_spec=pltpu.PrefetchScalarGridSpec(
            num_scalar_prefetch=1,
            grid=(tiles,),
            in_specs=[
                pl.BlockSpec((Q_TILE, HD), lambda i, use: (jnp.minimum(i, per_block - 1), 0)),
                pl.BlockSpec((Q_TILE, HD), lambda i, use: (jnp.maximum(i - per_block, 0), 0)),
                state_spec,
            ]
            + [constant_spec(source.shape) for source in sources],
            out_specs=out_specs,
            scratch_shapes=[
                pltpu.VMEM((1, STATE_ROWS, Q_TILE), F32),
                pltpu.VMEM((Q_TILE, HD), BF),
            ],
        ),
        out_shape=out_shape,
        compiler_params=pltpu.CompilerParams(vmem_limit_bytes=VMEM_BYTES),
        cost_estimate=pl.CostEstimate(
            flops=2 * rows * count * rows * HD * 4,
            bytes_accessed=6 << 20,
            transcendentals=2 * rows * count * rows,
        ),
    )(use, query, query_other, state, *sources)


def pick_weights(w_out, table):
    depth, width = w_out.shape[1], 2 * HD

    def kernel(table_ref, weight_ref, out_ref):
        out_ref[0] = weight_ref[...]

    return pl.pallas_call(
        kernel,
        grid_spec=pltpu.PrefetchScalarGridSpec(
            num_scalar_prefetch=1,
            grid=(4,),
            in_specs=[pl.BlockSpec((MODALITIES, depth, width), lambda k, t: (0, 0, t[k]))],
            out_specs=pl.BlockSpec((1, MODALITIES, depth, width), lambda k, t: (k, 0, 0, 0)),
        ),
        out_shape=jax.ShapeDtypeStruct((4, MODALITIES, depth, width), BF),
        compiler_params=pltpu.CompilerParams(vmem_limit_bytes=VMEM_BYTES),
        cost_estimate=pl.CostEstimate(flops=0, bytes_accessed=3 << 20, transcendentals=0),
    )(table, w_out)


def output_part(own, other, weights, table, seg, sizes):
    blocks = table.shape[0]
    rows = own.shape[0]
    width = 2 * HD
    picked = weights.ndim == 4

    def kernel(table_ref, seg_ref, own_ref, other_ref, weight_ref, *refs):
        *out_refs, attended, left, right, total, result, weight_sem, out_sem = refs
        weight_copies = []
        for i in range(blocks):
            first = pl.multiple_of(table_ref[i] * width, width)
            weight_copies.append(
                pltpu.make_async_copy(
                    weight_ref.at[i] if picked else weight_ref.at[:, :, pl.ds(first, width)],
                    right.at[i // 2, :, :, pl.ds(i % 2 * width, width)],
                    weight_sem.at[i],
                )
            )
            weight_copies[i].start()
        core = seg_ref[2 * MODALITIES]
        for mine in range(2):

            @pl.when(core == mine)
            def _(mine=mine):
                attended[:, mine * HD : (mine + 1) * HD] = own_ref[...]
                attended[:, (1 - mine) * HD : (2 - mine) * HD] = other_ref[...]

        def mask(kind, at, keep):
            left[kind] = attended[at, :] * keep.astype(BF)

        for_runs(seg_ref, rows, mask)
        out_copies = []
        for pair in range(blocks // 2):
            weight_copies[2 * pair].wait()
            weight_copies[2 * pair + 1].wait()
            total[...] = jnp.zeros_like(total)

            def run(kind, at, keep, pair=pair):
                total[at, :] += jnp.dot(left[kind], right[pair, kind], preferred_element_type=F32)

            for_runs(seg_ref, rows, run)
            for i in range(2):
                result[2 * pair + i] = total[:, i * width : (i + 1) * width].astype(BF)
            done = 0
            for size, out_ref in zip(sizes, out_refs):
                if done // 2 == pair:
                    source = result.at[pl.ds(done, 2)] if size else result.at[done]
                    out_copies.append(
                        pltpu.make_async_copy(source, out_ref, out_sem.at[len(out_copies)])
                    )
                    out_copies[-1].start()
                done += max(size, 1)
        for copy in out_copies:
            copy.wait()

    vmem = pl.BlockSpec(memory_space=pltpu.VMEM)
    shapes = [(size, rows, width) if size else (rows, width) for size in sizes]
    return pl.pallas_call(
        kernel,
        in_specs=[pl.BlockSpec(memory_space=pltpu.SMEM)] * 2
        + [vmem, vmem, pl.BlockSpec(memory_space=pl.ANY)],
        out_specs=(pl.BlockSpec(memory_space=pl.ANY),) * len(shapes),
        scratch_shapes=[
            pltpu.VMEM((rows, width), BF),
            pltpu.VMEM((MODALITIES, WINDOW, width), BF),
            pltpu.VMEM((blocks // 2, MODALITIES, width, 2 * width), BF),
            pltpu.VMEM((rows, 2 * width), F32),
            pltpu.VMEM((blocks, rows, width), BF),
            pltpu.SemaphoreType.DMA((blocks,)),
            pltpu.SemaphoreType.DMA((len(shapes),)),
        ],
        out_shape=tuple(jax.ShapeDtypeStruct(shape, BF) for shape in shapes),
        compiler_params=pltpu.CompilerParams(vmem_limit_bytes=VMEM_BYTES),
        cost_estimate=pl.CostEstimate(flops=0, bytes_accessed=rows, transcendentals=0),
    )(table, seg, own, other, weights)


def add(*arrays):
    return sum(array.astype(F32) for array in arrays).astype(BF)


def local(tokens, modality, w_query, w_key, w_value, w_out):
    seg = segment_scalars(modality)
    core = seg[2 * MODALITIES :]
    weights = (w_key, w_value, w_query)

    before, after = move(tokens, True, 1), move(tokens, True, -1)
    opposite = move(tokens, True, 2)
    plus_first = jnp.stack([tokens, before])
    minus_first = jnp.stack([tokens, after])
    before_first = move(plus_first, False, 1)
    after_first = move(minus_first, False, -1)
    before, after, opposite, _ = lax.optimization_barrier((before, after, opposite, plus_first))
    plus_second = jnp.stack([after, opposite])
    minus_second = jnp.stack([before, opposite])
    before_second = move(plus_second, False, 1)
    after_second = move(minus_second, False, -1)
    names = dict(self=0, before=3, after=1, opposite=2)

    def shards(second, *firsts):
        return [(names[first], second) for first in firsts]

    lists = [
        shards(0, "self", "before", "after", "opposite"),
        shards(3, "self", "before") + shards(1, "self", "after"),
        shards(3, "after", "opposite") + shards(1, "before", "opposite") + shards(2, "after"),
        shards(2, "self", "before", "opposite"),
    ]
    tables = [shard_table(*zip(*chosen)) for chosen in lists]
    partial = project([plus_first, plus_second], weights, tables[0], seg)
    before_first, after_first, partial = lax.optimization_barrier(
        (before_first, after_first, partial)
    )
    far_first = move(before_first, False, 1)
    far_after = move(after_first[1:], False, -1)
    partial = project([before_first, after_first], weights, tables[1], seg, before=partial)
    after_second, partial = lax.optimization_barrier((after_second, partial))
    far_opposite = move(after_second[1:], False, -1)
    partial = project(
        [before_second, after_second, far_after], weights, tables[2], seg, before=partial
    )
    query, kv, query_send, kv_send = project(
        [far_first, far_opposite], weights, tables[3], seg, before=partial, last=True
    )

    kv_other = swap_core(kv_send)
    query_other = swap_core(query_send)
    kv_before = move_x(kv, 1)
    kv_other_after = move_x(kv_other, -1)
    kv_other_before = move_x(kv_other, 1)
    kv_after = move_x(kv, -1)
    chip = lax.axis_index("ctx") // 2
    near_use = jnp.stack([chip >= 1, chip == 3]).astype(jnp.int32)
    far_use = jnp.stack([chip >= 2, chip >= 2]).astype(jnp.int32)
    queries = (query, query_other)
    state = attend_own(*queries, kv, kv_other, core)
    here, plus, two, minus = (shard_table(np.full(4, offset), np.arange(4)) for offset in range(4))
    kv_before, kv_other_after, state, w_two = lax.optimization_barrier(
        (kv_before, kv_other_after, state, pick_weights(w_out, two))
    )
    kv_far = move_x(kv_before, 1)
    kv_other_far = move_x(kv_other_after, -1)
    state = attend_other(*queries, state, [kv_before, kv_other_after], near_use)
    state = attend_other(*queries, state, [kv_other_before, kv_after], near_use)
    own, own_send = attend_other(*queries, state, [kv_far, kv_other_far], far_use, last=True)
    other = swap_core(own_send)

    part = functools.partial(output_part, own, other)
    two_low, two_high = part(w_two, two, seg, (2, 2))
    two_low = move(two_low, True, 1)
    two_high = move(two_high, True, -1)
    first = jnp.concatenate([plus[2:], minus[:2]])
    plus_high, minus_low = part(w_out, first, seg, (2, 2))
    plus_high = move(plus_high, True, 1)
    minus_low = move(minus_low, True, -1)
    later = jnp.concatenate([plus[:2], minus[2:]])
    plus_low, minus_high = part(w_out, later, seg, (2, 2))
    plus_low = add(plus_low, two_low)
    minus_high = add(minus_high, two_high)
    plus_low, minus_high, own, other = lax.optimization_barrier((plus_low, minus_high, own, other))
    here = output_part(own, other, w_out, here, seg, (0, 0, 0, 0))
    plus_low = move(plus_low, True, 1)
    minus_high = move(minus_high, True, -1)
    plus_low, plus_high, minus_low, minus_high = lax.optimization_barrier(
        (plus_low, plus_high, minus_low, minus_high)
    )
    mine, plus, two, minus = (
        add(here[i], (plus_low, plus_high)[i // 2][i % 2], (minus_low, minus_high)[i // 2][i % 2])
        for i in range(4)
    )
    return add(
        tokens, mine, move(plus, False, 1), move(two, False, 2), move(minus, False, -1)
    )


def solution(mesh):
    in_specs = (
        P("ctx", "tp"),
        P("ctx"),
        P(None, None, "tp"),
        P(None, None, "tp"),
        P(None, None, "tp"),
        P(None, "tp", None),
    )
    return jax.shard_map(
        local, mesh=mesh, in_specs=in_specs, out_specs=P("ctx", "tp"), check_vma=False
    )
```

```python
import functools
import math

import jax
import jax.numpy as jnp
import numpy as np
from jax import lax
from jax.experimental import pallas as pl
from jax.experimental.pallas import tpu as pltpu
from jax.sharding import PartitionSpec as P

HD = 128
MODALITIES = 3
EPS = 1e-05
WINDOW = 528
ALIGN = 16
Q_TILE = 512
K_TILE = 1024
STATE_ROWS = HD + 16
AXES = ("ctx", "tp")
BF = jnp.bfloat16
F32 = jnp.float32
VMEM_PROJECT = 50 * 1024 * 1024
VMEM_BYTES = 24 * 1024 * 1024
FEATURES = 4096
SPAN = 256
HEADROOM = 2.0**-13


def plane_perm(first, step):
    pairs = []
    for ctx in range(8):
        for z in range(4):
            for y in range(4):
                along_y = (ctx % 2 == 0) == first
                to_z = z if along_y else (z + step) % 4
                to_y = (y + step) % 4 if along_y else y
                pairs.append((ctx * 16 + z * 4 + y, ctx * 16 + to_z * 4 + to_y))
    return pairs


def move(array, first, step):
    return lax.ppermute(array, AXES, plane_perm(first, step))


def move_x(array, step):
    pairs = [(x * 2 + c, ((x + step) % 4) * 2 + c) for x in range(4) for c in range(2)]
    return lax.ppermute(array, "ctx", pairs)


def swap_core(array):
    return lax.ppermute(array, "ctx", [(i, i ^ 1) for i in range(8)])


def shard_table(first_offsets, second_offsets):
    core = lax.axis_index("ctx") % 2
    tp = lax.axis_index("tp")
    z, y = tp // 4, tp % 4
    first_offsets = jnp.asarray(first_offsets, jnp.int32)
    second_offsets = jnp.asarray(second_offsets, jnp.int32)
    first = (jnp.where(core == 0, y, z) + first_offsets) % 4
    second = (jnp.where(core == 0, z, y) + second_offsets) % 4
    return jnp.where(core == 0, second * 4 + first, first * 4 + second).astype(jnp.int32)


def segment_scalars(modality):
    rows = modality.shape[0]
    kinds = jnp.arange(MODALITIES, dtype=jnp.int32)[:, None]
    member = modality[None, :] == kinds
    positions = jnp.arange(rows, dtype=jnp.int32)[None, :]
    begin = jnp.min(jnp.where(member, positions, rows), axis=1)
    end = jnp.max(jnp.where(member, positions + 1, 0), axis=1)
    end = jnp.maximum(end, begin)
    core = lax.axis_index("ctx") % 2
    return jnp.concatenate([begin, end, core[None]]).astype(jnp.int32)


def for_runs(seg_ref, rows, body):
    for kind in range(MODALITIES):
        begin = seg_ref[kind]
        end = seg_ref[MODALITIES + kind]
        first = jnp.minimum(begin // ALIGN * ALIGN, rows - WINDOW)
        first = pl.multiple_of(first, ALIGN)
        positions = first + lax.broadcasted_iota(jnp.int32, (WINDOW, 1), 0)
        body(kind, pl.ds(first, WINDOW), (positions >= begin) & (positions < end))


def constant_spec(shape):
    return pl.BlockSpec(shape, lambda k, *scalars: (0,) * len(shape))


def project(pieces, weights, table, seg, before=None, last=False):
    count = len(pieces)
    counts = [piece.shape[0] for piece in pieces]
    firsts = [sum(counts[:i]) for i in range(count)]
    depth = sum(counts)
    rows, width = pieces[0].shape[1:]
    out_width = 3 * width
    has_before = before is not None

    def kernel(table_ref, seg_ref, *refs):
        piece_refs = refs[:count]
        weight_refs = refs[count : count + 3]
        refs = refs[count + 3 :]
        if has_before:
            squares_before_ref, before_ref, *refs = refs
        if last:
            query_ref, kv_ref, query_send_ref, kv_send_ref, *refs = refs
        else:
            squares_ref, out_ref, *refs = refs
        held, normed, left, right, total, shrink, piece_sem, weight_sem, total_sem = refs

        spans = [pl.ds(row, SPAN) for row in range(0, rows, SPAN)]
        piece_copies = [
            pltpu.make_async_copy(
                piece_refs[i].at[:, span, :],
                held.at[pl.ds(firsts[i], counts[i]), span, :],
                piece_sem.at[k, i],
            )
            for k, span in enumerate(spans)
            for i in range(count)
        ]
        groups = ((0, 2 * width), (2 * width, out_width))
        weight_copies = ([], [])
        before_copies = ([], [])
        out_copies = []
        for g, (low, high) in enumerate(groups):
            columns = pl.ds(low, high - low)
            for j in range(depth):
                first = pl.multiple_of(table_ref[j] * width, width)
                for i in range(low // width, high // width):
                    weight_copies[g].append(
                        pltpu.make_async_copy(
                            weight_refs[i].at[:, pl.ds(first, width), :],
                            right.at[:, pl.ds(j * width, width), pl.ds(i * width, width)],
                            weight_sem.at[i, j],
                        )
                    )
            for k, span in enumerate(spans):
                if has_before:
                    before_copies[g].append(
                        pltpu.make_async_copy(
                            before_ref.at[span, columns],
                            total.at[span, columns],
                            total_sem.at[0, g, k],
                        )
                    )
                if not last:
                    out_copies.append(
                        pltpu.make_async_copy(
                            total.at[span, columns],
                            out_ref.at[span, columns],
                            total_sem.at[1, g, k],
                        )
                    )
        for copy in piece_copies:
            copy.start()
        for g in range(2):
            for copy in weight_copies[g] + before_copies[g]:
                copy.start()

        for row in range(0, rows, HD):
            at = slice(row, row + HD)
            if row % SPAN == 0:
                k = row // SPAN
                for copy in piece_copies[k * count : (k + 1) * count]:
                    copy.wait()
            by_lane = jnp.zeros((HD, HD), F32)
            for j in range(depth):
                for column in range(0, width, HD):
                    by_lane += jnp.square(held[j, at, column : column + HD].astype(F32))
            squares = jnp.sum(by_lane, axis=1, keepdims=True)
            if has_before:
                squares_before = squares_before_ref[at, :]
                scale_before = lax.rsqrt(squares_before / FEATURES + EPS)
                squares += squares_before
            scale = lax.rsqrt(squares / FEATURES + EPS)
            if has_before:
                shrink[at, :] = jnp.where(scale_before > 0.0, scale / scale_before, 0.0)
            if not last:
                squares_ref[at, :] = squares
            for j in range(depth):
                piece = held[j, at, :].astype(F32)
                normed[at, j * width : (j + 1) * width] = (piece * (scale * HEADROOM)).astype(BF)

        def mask(kind, at, keep):
            left[kind] = normed[at, :] * keep.astype(BF)

        for_runs(seg_ref, rows, mask)
        for g, (low, high) in enumerate(groups):
            for copy in weight_copies[g] + before_copies[g]:
                copy.wait()
            if has_before:
                total[:, low:high] *= shrink[...]
            else:
                total[:, low:high] = jnp.zeros((rows, high - low), F32)

            def run(kind, at, keep, low=low, high=high):
                total[at, low:high] += jnp.dot(
                    left[kind], right[kind, :, low:high], preferred_element_type=F32
                )

            for_runs(seg_ref, rows, run)
            if not last:
                for copy in out_copies[g * len(spans) : (g + 1) * len(spans)]:
                    copy.start()
        for copy in out_copies:
            copy.wait()

        if last:
            query_scale = math.log2(math.e) / math.sqrt(HD) / HEADROOM
            core = seg_ref[2 * MODALITIES]
            for mine in range(2):

                @pl.when(core == mine)
                def _(mine=mine):
                    for head, q_out, kv_out in (
                        (mine, query_ref, kv_ref),
                        (1 - mine, query_send_ref, kv_send_ref),
                    ):
                        at = head * HD
                        kv_out[:, :HD] = (total[:, at : at + HD] / HEADROOM).astype(BF)
                        at += width
                        for row in range(0, rows, HD):
                            block = total[row : row + HD, at : at + HD] / HEADROOM
                            kv_out[row : row + HD, HD:] = block.T.astype(BF)
                        at += width
                        q_out[...] = (total[:, at : at + HD] * query_scale).astype(BF)

    vmem = pl.BlockSpec(memory_space=pltpu.VMEM)
    operands = [table, seg, *pieces, *weights]
    in_specs = [pl.BlockSpec(memory_space=pltpu.SMEM)] * 2
    in_specs += [pl.BlockSpec(memory_space=pl.ANY)] * count
    in_specs += [pl.BlockSpec(memory_space=pl.ANY)] * 3
    if has_before:
        operands += before
        in_specs += [vmem, pl.BlockSpec(memory_space=pl.ANY)]
    if last:
        shapes = [(rows, HD), (rows, 2 * HD)] * 2
        out_shape = tuple(jax.ShapeDtypeStruct(shape, BF) for shape in shapes)
        out_specs = (vmem,) * 4
    else:
        out_shape = (
            jax.ShapeDtypeStruct((rows, 1), F32),
            jax.ShapeDtypeStruct((rows, 3 * width), F32),
        )
        out_specs = (vmem, pl.BlockSpec(memory_space=pl.ANY))
    return pl.pallas_call(
        kernel,
        in_specs=in_specs,
        out_specs=out_specs,
        scratch_shapes=[
            pltpu.VMEM((depth, rows, width), BF),
            pltpu.VMEM((rows, depth * width), BF),
            pltpu.VMEM((MODALITIES, WINDOW, depth * width), BF),
            pltpu.VMEM((MODALITIES, depth * width, 3 * width), BF),
            pltpu.VMEM((rows, out_width), F32),
            pltpu.VMEM((rows, 1), F32),
            pltpu.SemaphoreType.DMA((rows // SPAN, count)),
            pltpu.SemaphoreType.DMA((3, depth)),
            pltpu.SemaphoreType.DMA((2, 2, rows // SPAN)),
        ],
        out_shape=out_shape,
        compiler_params=pltpu.CompilerParams(vmem_limit_bytes=VMEM_PROJECT),
        cost_estimate=pl.CostEstimate(
            flops=2 * depth * 3 * WINDOW * width * 3 * width,
            bytes_accessed=depth * (rows * width * 2 + 9 * width * width * 2),
            transcendentals=0,
        ),
    )(*operands)


def score(query, key, keep=None):
    scores = lax.dot_general(key, query, (((1,), (1,)), ((), ())), preferred_element_type=F32)
    return scores if keep is None else jnp.where(keep, scores, -1e30)


def fold(state, scores, value_t):
    top, total, summed = state
    new_top = jnp.maximum(top, jnp.max(scores, axis=0, keepdims=True))
    factor = jnp.exp2(top - new_top)
    weights = jnp.exp2(scores - new_top)
    total = total * factor + jnp.sum(weights, axis=0, keepdims=True)
    summed = summed * factor + jnp.dot(value_t, weights.astype(BF), preferred_element_type=F32)
    return new_top, total, summed


def empty_state():
    return (
        jnp.full((1, Q_TILE), -1e30, F32),
        jnp.zeros((1, Q_TILE), F32),
        jnp.zeros((HD, Q_TILE), F32),
    )


def store_state(state, state_ref):
    top, total, summed = state
    state_ref[0, :HD, :] = summed
    state_ref[0, HD : HD + 8, :] = jnp.broadcast_to(top, (8, Q_TILE))
    state_ref[0, HD + 8 :, :] = jnp.broadcast_to(total, (8, Q_TILE))


def load_state(state_ref):
    return (
        state_ref[0, HD : HD + 1, :],
        state_ref[0, HD + 8 : HD + 9, :],
        state_ref[0, :HD, :],
    )


def read_keys(ref, first, count):
    key = ref[pl.ds(first, count), :HD]
    blocks = [ref[pl.ds(first + i, HD), HD:] for i in range(0, count, HD)]
    return key, jnp.concatenate(blocks, axis=1)


def attend_own(query, query_other, kv, kv_other, core):
    rows = query.shape[0]
    per_block = rows // Q_TILE
    tiles = 2 * per_block

    def kernel(core_ref, query_ref, query_other_ref, kv_ref, kv_other_ref, state_ref, keys, both):
        place = pl.program_id(0)

        @pl.when(place == 0)
        def _():
            for mine in range(2):

                @pl.when(core_ref[0] == mine)
                def _(mine=mine):
                    at, other = mine * rows, (1 - mine) * rows
                    keys[at : at + rows, :] = kv_ref[...]
                    keys[other : other + rows, :] = kv_other_ref[...]
                    both[at : at + rows, :] = query_ref[...]
                    both[other : other + rows, :] = query_other_ref[...]

        at = pl.multiple_of(place * Q_TILE, Q_TILE)
        q = both[pl.ds(at, Q_TILE), :]
        causal = lax.broadcasted_iota(
            jnp.int32, (Q_TILE, Q_TILE), 0
        ) <= lax.broadcasted_iota(jnp.int32, (Q_TILE, Q_TILE), 1)
        key, value_t = read_keys(keys, at, Q_TILE)
        state = fold(empty_state(), score(q, key, causal), value_t)

        def earlier(tile, state):
            key, value_t = read_keys(keys, pl.multiple_of(tile * Q_TILE, Q_TILE), Q_TILE)
            return fold(state, score(q, key), value_t)

        store_state(lax.fori_loop(0, place, earlier, state), state_ref)

    whole = constant_spec((rows, HD))
    whole_kv = constant_spec((rows, 2 * HD))
    return pl.pallas_call(
        kernel,
        grid_spec=pltpu.PrefetchScalarGridSpec(
            num_scalar_prefetch=1,
            grid=(tiles,),
            in_specs=[whole, whole, whole_kv, whole_kv],
            out_specs=pl.BlockSpec(
                (1, STATE_ROWS, Q_TILE),
                lambda i, core: ((i + core[0] * per_block) % tiles, 0, 0),
            ),
            scratch_shapes=[
                pltpu.VMEM((2 * rows, 2 * HD), BF),
                pltpu.VMEM((2 * rows, HD), BF),
            ],
        ),
        out_shape=jax.ShapeDtypeStruct((tiles, STATE_ROWS, Q_TILE), F32),
        compiler_params=pltpu.CompilerParams(vmem_limit_bytes=VMEM_BYTES),
        cost_estimate=pl.CostEstimate(
            flops=10 * Q_TILE * Q_TILE * HD * 4,
            bytes_accessed=4 << 20,
            transcendentals=10 * Q_TILE * Q_TILE,
        ),
    )(core, query, query_other, kv, kv_other)


def attend_other(query, query_other, state, sources, use, last=False):
    rows = query.shape[0]
    per_block = rows // Q_TILE
    tiles = 2 * per_block
    count = len(sources)

    def kernel(use_ref, query_ref, query_other_ref, before_ref, *refs):
        source_refs = refs[:count]
        *out_refs, after, q_ref = refs[count:]
        tile = pl.program_id(0)

        @pl.when(tile < per_block)
        def _():
            q_ref[...] = query_ref[...]

        @pl.when(tile >= per_block)
        def _():
            q_ref[...] = query_other_ref[...]

        q = q_ref[...]
        after[...] = before_ref[...]

        def fold_in(refs):
            parts = [(ref, at) for ref in refs for at in range(0, rows, K_TILE)]
            state = load_state(after)
            scores = None
            for i, (ref, at) in enumerate(parts):
                key, value_t = read_keys(ref, at, K_TILE)
                if scores is None:
                    scores = score(q, key)
                later = None
                if i + 1 < len(parts):
                    next_ref, next_at = parts[i + 1]
                    later = score(q, next_ref[next_at : next_at + K_TILE, :HD])
                state = fold(state, scores, value_t)
                scores = later
            store_state(state, after)

        all_used = use_ref[0]
        for i in range(1, count):
            all_used = all_used & use_ref[i]

        @pl.when(all_used != 0)
        def _():
            fold_in(source_refs)

        for i, source_ref in enumerate(source_refs):

            @pl.when((all_used == 0) & (use_ref[i] != 0))
            def _(source_ref=source_ref):
                fold_in([source_ref])

        if last:
            _, total, summed = load_state(after)
            attended = (summed / total).T.astype(BF)
            for part, out_ref in enumerate(out_refs):

                @pl.when(tile // per_block == part)
                def _(out_ref=out_ref):
                    at = pl.multiple_of(tile % per_block * Q_TILE, Q_TILE)
                    out_ref[pl.ds(at, Q_TILE), :] = attended

        else:
            out_refs[0][...] = after[...]

    state_spec = pl.BlockSpec((1, STATE_ROWS, Q_TILE), lambda i, use: (i, 0, 0))
    if last:
        out_shape = (jax.ShapeDtypeStruct((rows, HD), BF),) * 2
        out_specs = (constant_spec((rows, HD)),) * 2
    else:
        out_shape = jax.ShapeDtypeStruct((tiles, STATE_ROWS, Q_TILE), F32)
        out_specs = state_spec
    return pl.pallas_call(
        kernel,
        grid_spec=pltpu.PrefetchScalarGridSpec(
            num_scalar_prefetch=1,
            grid=(tiles,),
            in_specs=[
                pl.BlockSpec((Q_TILE, HD), lambda i, use: (jnp.minimum(i, per_block - 1), 0)),
                pl.BlockSpec((Q_TILE, HD), lambda i, use: (jnp.maximum(i - per_block, 0), 0)),
                state_spec,
            ]
            + [constant_spec(source.shape) for source in sources],
            out_specs=out_specs,
            scratch_shapes=[
                pltpu.VMEM((1, STATE_ROWS, Q_TILE), F32),
                pltpu.VMEM((Q_TILE, HD), BF),
            ],
        ),
        out_shape=out_shape,
        compiler_params=pltpu.CompilerParams(vmem_limit_bytes=VMEM_BYTES),
        cost_estimate=pl.CostEstimate(
            flops=2 * rows * count * rows * HD * 4,
            bytes_accessed=6 << 20,
            transcendentals=2 * rows * count * rows,
        ),
    )(use, query, query_other, state, *sources)


def pick_weights(w_out, table):
    depth, width = w_out.shape[1], 2 * HD

    def kernel(table_ref, weight_ref, out_ref):
        out_ref[0] = weight_ref[...]

    return pl.pallas_call(
        kernel,
        grid_spec=pltpu.PrefetchScalarGridSpec(
            num_scalar_prefetch=1,
            grid=(4,),
            in_specs=[pl.BlockSpec((MODALITIES, depth, width), lambda k, t: (0, 0, t[k]))],
            out_specs=pl.BlockSpec((1, MODALITIES, depth, width), lambda k, t: (k, 0, 0, 0)),
        ),
        out_shape=jax.ShapeDtypeStruct((4, MODALITIES, depth, width), BF),
        compiler_params=pltpu.CompilerParams(vmem_limit_bytes=VMEM_BYTES),
        cost_estimate=pl.CostEstimate(flops=0, bytes_accessed=3 << 20, transcendentals=0),
    )(table, w_out)


def output_part(own, other, weights, table, seg, sizes):
    blocks = table.shape[0]
    rows = own.shape[0]
    width = 2 * HD
    picked = weights.ndim == 4

    def kernel(table_ref, seg_ref, own_ref, other_ref, weight_ref, *refs):
        *out_refs, attended, left, right, total, result, weight_sem, out_sem = refs
        weight_copies = []
        for i in range(blocks):
            first = pl.multiple_of(table_ref[i] * width, width)
            weight_copies.append(
                pltpu.make_async_copy(
                    weight_ref.at[i] if picked else weight_ref.at[:, :, pl.ds(first, width)],
                    right.at[i // 2, :, :, pl.ds(i % 2 * width, width)],
                    weight_sem.at[i],
                )
            )
            weight_copies[i].start()
        core = seg_ref[2 * MODALITIES]
        for mine in range(2):

            @pl.when(core == mine)
            def _(mine=mine):
                attended[:, mine * HD : (mine + 1) * HD] = own_ref[...]
                attended[:, (1 - mine) * HD : (2 - mine) * HD] = other_ref[...]

        def mask(kind, at, keep):
            left[kind] = attended[at, :] * keep.astype(BF)

        for_runs(seg_ref, rows, mask)
        out_copies = []
        for pair in range(blocks // 2):
            weight_copies[2 * pair].wait()
            weight_copies[2 * pair + 1].wait()
            total[...] = jnp.zeros_like(total)

            def run(kind, at, keep, pair=pair):
                total[at, :] += jnp.dot(left[kind], right[pair, kind], preferred_element_type=F32)

            for_runs(seg_ref, rows, run)
            for i in range(2):
                result[2 * pair + i] = total[:, i * width : (i + 1) * width].astype(BF)
            done = 0
            for size, out_ref in zip(sizes, out_refs):
                if done // 2 == pair:
                    source = result.at[pl.ds(done, 2)] if size else result.at[done]
                    out_copies.append(
                        pltpu.make_async_copy(source, out_ref, out_sem.at[len(out_copies)])
                    )
                    out_copies[-1].start()
                done += max(size, 1)
        for copy in out_copies:
            copy.wait()

    vmem = pl.BlockSpec(memory_space=pltpu.VMEM)
    shapes = [(size, rows, width) if size else (rows, width) for size in sizes]
    return pl.pallas_call(
        kernel,
        in_specs=[pl.BlockSpec(memory_space=pltpu.SMEM)] * 2
        + [vmem, vmem, pl.BlockSpec(memory_space=pl.ANY)],
        out_specs=(pl.BlockSpec(memory_space=pl.ANY),) * len(shapes),
        scratch_shapes=[
            pltpu.VMEM((rows, width), BF),
            pltpu.VMEM((MODALITIES, WINDOW, width), BF),
            pltpu.VMEM((blocks // 2, MODALITIES, width, 2 * width), BF),
            pltpu.VMEM((rows, 2 * width), F32),
            pltpu.VMEM((blocks, rows, width), BF),
            pltpu.SemaphoreType.DMA((blocks,)),
            pltpu.SemaphoreType.DMA((len(shapes),)),
        ],
        out_shape=tuple(jax.ShapeDtypeStruct(shape, BF) for shape in shapes),
        compiler_params=pltpu.CompilerParams(vmem_limit_bytes=VMEM_BYTES),
        cost_estimate=pl.CostEstimate(flops=0, bytes_accessed=rows, transcendentals=0),
    )(table, seg, own, other, weights)


def add(*arrays):
    return sum(array.astype(F32) for array in arrays).astype(BF)


def local(tokens, modality, w_query, w_key, w_value, w_out):
    seg = segment_scalars(modality)
    core = seg[2 * MODALITIES :]
    weights = (w_key, w_value, w_query)

    before, after = move(tokens, True, 1), move(tokens, True, -1)
    opposite = move(tokens, True, 2)
    plus_first = jnp.stack([tokens, before])
    minus_first = jnp.stack([tokens, after])
    before_first = move(plus_first, False, 1)
    after_first = move(minus_first, False, -1)
    before, after, opposite, _ = lax.optimization_barrier((before, after, opposite, plus_first))
    plus_second = jnp.stack([after, opposite])
    minus_second = jnp.stack([before, opposite])
    before_second = move(plus_second, False, 1)
    after_second = move(minus_second, False, -1)
    names = dict(self=0, before=3, after=1, opposite=2)

    def shards(second, *firsts):
        return [(names[first], second) for first in firsts]

    lists = [
        shards(0, "self", "before", "after", "opposite"),
        shards(3, "self", "before") + shards(1, "self", "after"),
        shards(3, "after", "opposite") + shards(1, "before", "opposite") + shards(2, "after"),
        shards(2, "self", "before", "opposite"),
    ]
    tables = [shard_table(*zip(*chosen)) for chosen in lists]
    partial = project([plus_first, plus_second], weights, tables[0], seg)
    before_first, after_first, partial = lax.optimization_barrier(
        (before_first, after_first, partial)
    )
    far_first = move(before_first, False, 1)
    far_after = move(after_first[1:], False, -1)
    partial = project([before_first, after_first], weights, tables[1], seg, before=partial)
    after_second, partial = lax.optimization_barrier((after_second, partial))
    far_opposite = move(after_second[1:], False, -1)
    partial = project(
        [before_second, after_second, far_after], weights, tables[2], seg, before=partial
    )
    query, kv, query_send, kv_send = project(
        [far_first, far_opposite], weights, tables[3], seg, before=partial, last=True
    )

    kv_other = swap_core(kv_send)
    query_other = swap_core(query_send)
    kv_before = move_x(kv, 1)
    kv_other_after = move_x(kv_other, -1)
    kv_other_before = move_x(kv_other, 1)
    kv_after = move_x(kv, -1)
    chip = lax.axis_index("ctx") // 2
    near_use = jnp.stack([chip >= 1, chip == 3]).astype(jnp.int32)
    far_use = jnp.stack([chip >= 2, chip >= 2]).astype(jnp.int32)
    queries = (query, query_other)
    state = attend_own(*queries, kv, kv_other, core)
    here, plus, two, minus = (shard_table(np.full(4, offset), np.arange(4)) for offset in range(4))
    kv_before, kv_other_after, state, w_two = lax.optimization_barrier(
        (kv_before, kv_other_after, state, pick_weights(w_out, two))
    )
    kv_far = move_x(kv_before, 1)
    kv_other_far = move_x(kv_other_after, -1)
    state = attend_other(*queries, state, [kv_before, kv_other_after], near_use)
    state = attend_other(*queries, state, [kv_other_before, kv_after], near_use)
    own, own_send = attend_other(*queries, state, [kv_far, kv_other_far], far_use, last=True)
    other = swap_core(own_send)

    part = functools.partial(output_part, own, other)
    two_low, two_high = part(w_two, two, seg, (2, 2))
    two_low = move(two_low, True, 1)
    two_high = move(two_high, True, -1)
    first = jnp.concatenate([plus[2:], minus[:2]])
    plus_high, minus_low = part(w_out, first, seg, (2, 2))
    plus_high = move(plus_high, True, 1)
    minus_low = move(minus_low, True, -1)
    later = jnp.concatenate([plus[1:2], plus[:1], minus[2:]])
    plus_1, plus_0, minus_high = part(w_out, later, seg, (0, 0, 2))
    plus_1 = add(plus_1, two_low[1])
    plus_0 = add(plus_0, two_low[0])
    minus_high = add(minus_high, two_high)
    plus_1, plus_0, minus_high, own, other = lax.optimization_barrier(
        (plus_1, plus_0, minus_high, own, other)
    )
    here = output_part(own, other, w_out, here, seg, (0, 0, 0, 0))
    plus_1 = move(plus_1, True, 1)
    minus_high = move(minus_high, True, -1)
    plus_0 = move(plus_0, True, 1)
    plus_1, plus_high, minus_low, minus_high = lax.optimization_barrier(
        (plus_1, plus_high, minus_low, minus_high)
    )
    sums = [
        add(here[1], plus_1, minus_low[1]),
        add(here[2], plus_high[0], minus_high[0]),
        add(here[3], plus_high[1], minus_high[1]),
    ]
    after, opposite, before = (move(part, False, step) for part, step in zip(sums, (1, 2, -1)))
    plus_0, *_ = lax.optimization_barrier((plus_0, *sums))
    mine = lax.optimization_barrier(add(here[0], plus_0, minus_low[0]))
    return add(tokens, mine, after, opposite, before)


def solution(mesh):
    in_specs = (
        P("ctx", "tp"),
        P("ctx"),
        P(None, None, "tp"),
        P(None, None, "tp"),
        P(None, None, "tp"),
        P(None, "tp", None),
    )
    return jax.shard_map(
        local, mesh=mesh, in_specs=in_specs, out_specs=P("ctx", "tp"), check_vma=False
    )
```

```python
import functools
import math

import jax
import jax.numpy as jnp
import numpy as np
from jax import lax
from jax.experimental import pallas as pl
from jax.experimental.pallas import tpu as pltpu
from jax.sharding import PartitionSpec as P

HD = 128
MODALITIES = 3
EPS = 1e-05
WINDOW = 528
ALIGN = 16
Q_TILE = 512
K_TILE = 1024
STATE_ROWS = HD + 16
AXES = ("ctx", "tp")
BF = jnp.bfloat16
F32 = jnp.float32
VMEM_PROJECT = 50 * 1024 * 1024
VMEM_BYTES = 24 * 1024 * 1024
FEATURES = 4096
SPAN = 256
HEADROOM = 2.0**-13


def plane_perm(first, step):
    pairs = []
    for ctx in range(8):
        for z in range(4):
            for y in range(4):
                along_y = (ctx % 2 == 0) == first
                to_z = z if along_y else (z + step) % 4
                to_y = (y + step) % 4 if along_y else y
                pairs.append((ctx * 16 + z * 4 + y, ctx * 16 + to_z * 4 + to_y))
    return pairs


def move(array, first, step):
    return lax.ppermute(array, AXES, plane_perm(first, step))


def move_x(array, step):
    pairs = [(x * 2 + c, ((x + step) % 4) * 2 + c) for x in range(4) for c in range(2)]
    return lax.ppermute(array, "ctx", pairs)


def swap_core(array):
    return lax.ppermute(array, "ctx", [(i, i ^ 1) for i in range(8)])


def shard_table(first_offsets, second_offsets):
    core = lax.axis_index("ctx") % 2
    tp = lax.axis_index("tp")
    z, y = tp // 4, tp % 4
    first_offsets = jnp.asarray(first_offsets, jnp.int32)
    second_offsets = jnp.asarray(second_offsets, jnp.int32)
    first = (jnp.where(core == 0, y, z) + first_offsets) % 4
    second = (jnp.where(core == 0, z, y) + second_offsets) % 4
    return jnp.where(core == 0, second * 4 + first, first * 4 + second).astype(jnp.int32)


def segment_scalars(modality):
    rows = modality.shape[0]
    kinds = jnp.arange(MODALITIES, dtype=jnp.int32)[:, None]
    member = modality[None, :] == kinds
    positions = jnp.arange(rows, dtype=jnp.int32)[None, :]
    begin = jnp.min(jnp.where(member, positions, rows), axis=1)
    end = jnp.max(jnp.where(member, positions + 1, 0), axis=1)
    end = jnp.maximum(end, begin)
    core = lax.axis_index("ctx") % 2
    return jnp.concatenate([begin, end, core[None]]).astype(jnp.int32)


def for_runs(seg_ref, rows, body):
    for kind in range(MODALITIES):
        begin = seg_ref[kind]
        end = seg_ref[MODALITIES + kind]
        first = jnp.minimum(begin // ALIGN * ALIGN, rows - WINDOW)
        first = pl.multiple_of(first, ALIGN)
        positions = first + lax.broadcasted_iota(jnp.int32, (WINDOW, 1), 0)
        body(kind, pl.ds(first, WINDOW), (positions >= begin) & (positions < end))


def constant_spec(shape):
    return pl.BlockSpec(shape, lambda k, *scalars: (0,) * len(shape))


def project(pieces, weights, table, seg, before=None, last=False):
    count = len(pieces)
    counts = [piece.shape[0] for piece in pieces]
    firsts = [sum(counts[:i]) for i in range(count)]
    depth = sum(counts)
    rows, width = pieces[0].shape[1:]
    out_width = 3 * width
    has_before = before is not None

    def kernel(table_ref, seg_ref, *refs):
        piece_refs = refs[:count]
        weight_refs = refs[count : count + 3]
        refs = refs[count + 3 :]
        if has_before:
            squares_before_ref, before_ref, *refs = refs
        if last:
            query_ref, kv_ref, query_send_ref, kv_send_ref, *refs = refs
        else:
            squares_ref, out_ref, *refs = refs
        held, normed, left, right, total, shrink, piece_sem, weight_sem, total_sem = refs

        spans = [pl.ds(row, SPAN) for row in range(0, rows, SPAN)]
        piece_copies = [
            pltpu.make_async_copy(
                piece_refs[i].at[:, span, :],
                held.at[pl.ds(firsts[i], counts[i]), span, :],
                piece_sem.at[k, i],
            )
            for k, span in enumerate(spans)
            for i in range(count)
        ]
        groups = ((0, 2 * width), (2 * width, out_width))
        weight_copies = ([], [])
        before_copies = ([], [])
        out_copies = []
        for g, (low, high) in enumerate(groups):
            columns = pl.ds(low, high - low)
            for j in range(depth):
                first = pl.multiple_of(table_ref[j] * width, width)
                for i in range(low // width, high // width):
                    weight_copies[g].append(
                        pltpu.make_async_copy(
                            weight_refs[i].at[:, pl.ds(first, width), :],
                            right.at[:, pl.ds(j * width, width), pl.ds(i * width, width)],
                            weight_sem.at[i, j],
                        )
                    )
            for k, span in enumerate(spans):
                if has_before:
                    before_copies[g].append(
                        pltpu.make_async_copy(
                            before_ref.at[span, columns],
                            total.at[span, columns],
                            total_sem.at[0, g, k],
                        )
                    )
                if not last:
                    out_copies.append(
                        pltpu.make_async_copy(
                            total.at[span, columns],
                            out_ref.at[span, columns],
                            total_sem.at[1, g, k],
                        )
                    )
        for copy in piece_copies:
            copy.start()
        for g in range(2):
            for copy in weight_copies[g] + before_copies[g]:
                copy.start()

        for row in range(0, rows, HD):
            at = slice(row, row + HD)
            if row % SPAN == 0:
                k = row // SPAN
                for copy in piece_copies[k * count : (k + 1) * count]:
                    copy.wait()
            by_lane = jnp.zeros((HD, HD), F32)
            for j in range(depth):
                for column in range(0, width, HD):
                    by_lane += jnp.square(held[j, at, column : column + HD].astype(F32))
            squares = jnp.sum(by_lane, axis=1, keepdims=True)
            if has_before:
                squares_before = squares_before_ref[at, :]
                scale_before = lax.rsqrt(squares_before / FEATURES + EPS)
                squares += squares_before
            scale = lax.rsqrt(squares / FEATURES + EPS)
            if has_before:
                shrink[at, :] = jnp.where(scale_before > 0.0, scale / scale_before, 0.0)
            if not last:
                squares_ref[at, :] = squares
            for j in range(depth):
                piece = held[j, at, :].astype(F32)
                normed[at, j * width : (j + 1) * width] = (piece * (scale * HEADROOM)).astype(BF)

        def mask(kind, at, keep):
            left[kind] = normed[at, :] * keep.astype(BF)

        for_runs(seg_ref, rows, mask)
        for g, (low, high) in enumerate(groups):
            for copy in weight_copies[g] + before_copies[g]:
                copy.wait()
            if has_before:
                total[:, low:high] *= shrink[...]
            else:
                total[:, low:high] = jnp.zeros((rows, high - low), F32)

            def run(kind, at, keep, low=low, high=high):
                total[at, low:high] += jnp.dot(
                    left[kind], right[kind, :, low:high], preferred_element_type=F32
                )

            for_runs(seg_ref, rows, run)
            if not last:
                for copy in out_copies[g * len(spans) : (g + 1) * len(spans)]:
                    copy.start()
        for copy in out_copies:
            copy.wait()

        if last:
            query_scale = math.log2(math.e) / math.sqrt(HD) / HEADROOM
            core = seg_ref[2 * MODALITIES]
            for mine in range(2):

                @pl.when(core == mine)
                def _(mine=mine):
                    for head, q_out, kv_out in (
                        (mine, query_ref, kv_ref),
                        (1 - mine, query_send_ref, kv_send_ref),
                    ):
                        at = head * HD
                        kv_out[:, :HD] = (total[:, at : at + HD] / HEADROOM).astype(BF)
                        at += width
                        for row in range(0, rows, HD):
                            block = total[row : row + HD, at : at + HD] / HEADROOM
                            kv_out[row : row + HD, HD:] = block.T.astype(BF)
                        at += width
                        q_out[...] = (total[:, at : at + HD] * query_scale).astype(BF)

    vmem = pl.BlockSpec(memory_space=pltpu.VMEM)
    operands = [table, seg, *pieces, *weights]
    in_specs = [pl.BlockSpec(memory_space=pltpu.SMEM)] * 2
    in_specs += [pl.BlockSpec(memory_space=pl.ANY)] * count
    in_specs += [pl.BlockSpec(memory_space=pl.ANY)] * 3
    if has_before:
        operands += before
        in_specs += [vmem, pl.BlockSpec(memory_space=pl.ANY)]
    if last:
        shapes = [(rows, HD), (rows, 2 * HD)] * 2
        out_shape = tuple(jax.ShapeDtypeStruct(shape, BF) for shape in shapes)
        out_specs = (vmem,) * 4
    else:
        out_shape = (
            jax.ShapeDtypeStruct((rows, 1), F32),
            jax.ShapeDtypeStruct((rows, 3 * width), F32),
        )
        out_specs = (vmem, pl.BlockSpec(memory_space=pl.ANY))
    return pl.pallas_call(
        kernel,
        in_specs=in_specs,
        out_specs=out_specs,
        scratch_shapes=[
            pltpu.VMEM((depth, rows, width), BF),
            pltpu.VMEM((rows, depth * width), BF),
            pltpu.VMEM((MODALITIES, WINDOW, depth * width), BF),
            pltpu.VMEM((MODALITIES, depth * width, 3 * width), BF),
            pltpu.VMEM((rows, out_width), F32),
            pltpu.VMEM((rows, 1), F32),
            pltpu.SemaphoreType.DMA((rows // SPAN, count)),
            pltpu.SemaphoreType.DMA((3, depth)),
            pltpu.SemaphoreType.DMA((2, 2, rows // SPAN)),
        ],
        out_shape=out_shape,
        compiler_params=pltpu.CompilerParams(vmem_limit_bytes=VMEM_PROJECT),
        cost_estimate=pl.CostEstimate(
            flops=2 * depth * 3 * WINDOW * width * 3 * width,
            bytes_accessed=depth * (rows * width * 2 + 9 * width * width * 2),
            transcendentals=0,
        ),
    )(*operands)


def score(query, key, keep=None):
    scores = lax.dot_general(key, query, (((1,), (1,)), ((), ())), preferred_element_type=F32)
    return scores if keep is None else jnp.where(keep, scores, -1e30)


def fold(state, scores, value_t):
    top, total, summed = state
    new_top = jnp.maximum(top, jnp.max(scores, axis=0, keepdims=True))
    factor = jnp.exp2(top - new_top)
    weights = jnp.exp2(scores - new_top)
    total = total * factor + jnp.sum(weights, axis=0, keepdims=True)
    summed = summed * factor + jnp.dot(value_t, weights.astype(BF), preferred_element_type=F32)
    return new_top, total, summed


def empty_state():
    return (
        jnp.full((1, Q_TILE), -1e30, F32),
        jnp.zeros((1, Q_TILE), F32),
        jnp.zeros((HD, Q_TILE), F32),
    )


def store_state(state, state_ref):
    top, total, summed = state
    state_ref[0, :HD, :] = summed
    state_ref[0, HD : HD + 8, :] = jnp.broadcast_to(top, (8, Q_TILE))
    state_ref[0, HD + 8 :, :] = jnp.broadcast_to(total, (8, Q_TILE))


def load_state(state_ref):
    return (
        state_ref[0, HD : HD + 1, :],
        state_ref[0, HD + 8 : HD + 9, :],
        state_ref[0, :HD, :],
    )


def read_keys(ref, first, count):
    key = ref[pl.ds(first, count), :HD]
    blocks = [ref[pl.ds(first + i, HD), HD:] for i in range(0, count, HD)]
    return key, jnp.concatenate(blocks, axis=1)


def attend_own(query, query_other, kv, kv_other, core):
    rows = query.shape[0]
    per_block = rows // Q_TILE
    tiles = 2 * per_block

    def kernel(core_ref, query_ref, query_other_ref, kv_ref, kv_other_ref, state_ref, keys, both):
        place = pl.program_id(0)

        @pl.when(place == 0)
        def _():
            for mine in range(2):

                @pl.when(core_ref[0] == mine)
                def _(mine=mine):
                    at, other = mine * rows, (1 - mine) * rows
                    keys[at : at + rows, :] = kv_ref[...]
                    keys[other : other + rows, :] = kv_other_ref[...]
                    both[at : at + rows, :] = query_ref[...]
                    both[other : other + rows, :] = query_other_ref[...]

        at = pl.multiple_of(place * Q_TILE, Q_TILE)
        q = both[pl.ds(at, Q_TILE), :]
        causal = lax.broadcasted_iota(
            jnp.int32, (Q_TILE, Q_TILE), 0
        ) <= lax.broadcasted_iota(jnp.int32, (Q_TILE, Q_TILE), 1)
        key, value_t = read_keys(keys, at, Q_TILE)
        state = fold(empty_state(), score(q, key, causal), value_t)

        def earlier(tile, state):
            key, value_t = read_keys(keys, pl.multiple_of(tile * Q_TILE, Q_TILE), Q_TILE)
            return fold(state, score(q, key), value_t)

        store_state(lax.fori_loop(0, place, earlier, state), state_ref)

    whole = constant_spec((rows, HD))
    whole_kv = constant_spec((rows, 2 * HD))
    return pl.pallas_call(
        kernel,
        grid_spec=pltpu.PrefetchScalarGridSpec(
            num_scalar_prefetch=1,
            grid=(tiles,),
            in_specs=[whole, whole, whole_kv, whole_kv],
            out_specs=pl.BlockSpec(
                (1, STATE_ROWS, Q_TILE),
                lambda i, core: ((i + core[0] * per_block) % tiles, 0, 0),
            ),
            scratch_shapes=[
                pltpu.VMEM((2 * rows, 2 * HD), BF),
                pltpu.VMEM((2 * rows, HD), BF),
            ],
        ),
        out_shape=jax.ShapeDtypeStruct((tiles, STATE_ROWS, Q_TILE), F32),
        compiler_params=pltpu.CompilerParams(vmem_limit_bytes=VMEM_BYTES),
        cost_estimate=pl.CostEstimate(
            flops=10 * Q_TILE * Q_TILE * HD * 4,
            bytes_accessed=4 << 20,
            transcendentals=10 * Q_TILE * Q_TILE,
        ),
    )(core, query, query_other, kv, kv_other)


def attend_other(query, query_other, state, sources, use, last=False):
    rows = query.shape[0]
    per_block = rows // Q_TILE
    tiles = 2 * per_block
    count = len(sources)

    def kernel(use_ref, query_ref, query_other_ref, before_ref, *refs):
        source_refs = refs[:count]
        *out_refs, after, q_ref = refs[count:]
        tile = pl.program_id(0)

        @pl.when(tile < per_block)
        def _():
            q_ref[...] = query_ref[...]

        @pl.when(tile >= per_block)
        def _():
            q_ref[...] = query_other_ref[...]

        q = q_ref[...]
        after[...] = before_ref[...]

        def fold_in(refs):
            parts = [(ref, at) for ref in refs for at in range(0, rows, K_TILE)]
            state = load_state(after)
            scores = None
            for i, (ref, at) in enumerate(parts):
                key, value_t = read_keys(ref, at, K_TILE)
                if scores is None:
                    scores = score(q, key)
                later = None
                if i + 1 < len(parts):
                    next_ref, next_at = parts[i + 1]
                    later = score(q, next_ref[next_at : next_at + K_TILE, :HD])
                state = fold(state, scores, value_t)
                scores = later
            store_state(state, after)

        all_used = use_ref[0]
        for i in range(1, count):
            all_used = all_used & use_ref[i]

        @pl.when(all_used != 0)
        def _():
            fold_in(source_refs)

        for i, source_ref in enumerate(source_refs):

            @pl.when((all_used == 0) & (use_ref[i] != 0))
            def _(source_ref=source_ref):
                fold_in([source_ref])

        if last:
            _, total, summed = load_state(after)
            attended = (summed / total).T.astype(BF)
            for part, out_ref in enumerate(out_refs):

                @pl.when(tile // per_block == part)
                def _(out_ref=out_ref):
                    at = pl.multiple_of(tile % per_block * Q_TILE, Q_TILE)
                    out_ref[pl.ds(at, Q_TILE), :] = attended

        else:
            out_refs[0][...] = after[...]

    state_spec = pl.BlockSpec((1, STATE_ROWS, Q_TILE), lambda i, use: (i, 0, 0))
    if last:
        out_shape = (jax.ShapeDtypeStruct((rows, HD), BF),) * 2
        out_specs = (constant_spec((rows, HD)),) * 2
    else:
        out_shape = jax.ShapeDtypeStruct((tiles, STATE_ROWS, Q_TILE), F32)
        out_specs = state_spec
    return pl.pallas_call(
        kernel,
        grid_spec=pltpu.PrefetchScalarGridSpec(
            num_scalar_prefetch=1,
            grid=(tiles,),
            in_specs=[
                pl.BlockSpec((Q_TILE, HD), lambda i, use: (jnp.minimum(i, per_block - 1), 0)),
                pl.BlockSpec((Q_TILE, HD), lambda i, use: (jnp.maximum(i - per_block, 0), 0)),
                state_spec,
            ]
            + [constant_spec(source.shape) for source in sources],
            out_specs=out_specs,
            scratch_shapes=[
                pltpu.VMEM((1, STATE_ROWS, Q_TILE), F32),
                pltpu.VMEM((Q_TILE, HD), BF),
            ],
        ),
        out_shape=out_shape,
        compiler_params=pltpu.CompilerParams(vmem_limit_bytes=VMEM_BYTES),
        cost_estimate=pl.CostEstimate(
            flops=2 * rows * count * rows * HD * 4,
            bytes_accessed=6 << 20,
            transcendentals=2 * rows * count * rows,
        ),
    )(use, query, query_other, state, *sources)


def pick_weights(w_out, tables):
    depth, width = w_out.shape[1], 2 * HD
    groups = len(tables)

    def kernel(*refs):
        weight_ref, *out_refs = refs[groups:]
        for i, out_ref in enumerate(out_refs):

            @pl.when(pl.program_id(0) // 4 == i)
            def _(out_ref=out_ref):
                out_ref[0] = weight_ref[...]

    def column(k, *table_refs):
        place = table_refs[0][k % 4]
        for i in range(1, groups):
            place = jnp.where(k // 4 == i, table_refs[i][k % 4], place)
        return (0, 0, place)

    return pl.pallas_call(
        kernel,
        grid_spec=pltpu.PrefetchScalarGridSpec(
            num_scalar_prefetch=groups,
            grid=(4 * groups,),
            in_specs=[pl.BlockSpec((MODALITIES, depth, width), column)],
            out_specs=tuple(
                pl.BlockSpec(
                    (1, MODALITIES, depth, width),
                    lambda k, *t, i=i: (jnp.clip(k - 4 * i, 0, 3), 0, 0, 0),
                )
                for i in range(groups)
            ),
        ),
        out_shape=(jax.ShapeDtypeStruct((4, MODALITIES, depth, width), BF),) * groups,
        compiler_params=pltpu.CompilerParams(vmem_limit_bytes=VMEM_BYTES),
        cost_estimate=pl.CostEstimate(
            flops=0, bytes_accessed=groups * (3 << 20), transcendentals=0
        ),
    )(*tables, w_out)


def output_part(own, other, weights, table, seg, sizes):
    blocks = table.shape[0]
    rows = own.shape[0]
    width = 2 * HD
    picked = weights.ndim == 4

    def kernel(table_ref, seg_ref, own_ref, other_ref, weight_ref, *refs):
        *out_refs, attended, left, right, total, result, weight_sem, out_sem = refs
        weight_copies = []
        for i in range(blocks):
            first = pl.multiple_of(table_ref[i] * width, width)
            weight_copies.append(
                pltpu.make_async_copy(
                    weight_ref.at[i] if picked else weight_ref.at[:, :, pl.ds(first, width)],
                    right.at[i // 2, :, :, pl.ds(i % 2 * width, width)],
                    weight_sem.at[i],
                )
            )
            weight_copies[i].start()
        core = seg_ref[2 * MODALITIES]
        for mine in range(2):

            @pl.when(core == mine)
            def _(mine=mine):
                attended[:, mine * HD : (mine + 1) * HD] = own_ref[...]
                attended[:, (1 - mine) * HD : (2 - mine) * HD] = other_ref[...]

        def mask(kind, at, keep):
            left[kind] = attended[at, :] * keep.astype(BF)

        for_runs(seg_ref, rows, mask)
        out_copies = []
        for pair in range(blocks // 2):
            weight_copies[2 * pair].wait()
            weight_copies[2 * pair + 1].wait()
            total[...] = jnp.zeros_like(total)

            def run(kind, at, keep, pair=pair):
                total[at, :] += jnp.dot(left[kind], right[pair, kind], preferred_element_type=F32)

            for_runs(seg_ref, rows, run)
            for i in range(2):
                result[2 * pair + i] = total[:, i * width : (i + 1) * width].astype(BF)
            done = 0
            for size, out_ref in zip(sizes, out_refs):
                if done // 2 == pair:
                    source = result.at[pl.ds(done, 2)] if size else result.at[done]
                    out_copies.append(
                        pltpu.make_async_copy(source, out_ref, out_sem.at[len(out_copies)])
                    )
                    out_copies[-1].start()
                done += max(size, 1)
        for copy in out_copies:
            copy.wait()

    vmem = pl.BlockSpec(memory_space=pltpu.VMEM)
    shapes = [(size, rows, width) if size else (rows, width) for size in sizes]
    return pl.pallas_call(
        kernel,
        in_specs=[pl.BlockSpec(memory_space=pltpu.SMEM)] * 2
        + [vmem, vmem, pl.BlockSpec(memory_space=pl.ANY)],
        out_specs=(pl.BlockSpec(memory_space=pl.ANY),) * len(shapes),
        scratch_shapes=[
            pltpu.VMEM((rows, width), BF),
            pltpu.VMEM((MODALITIES, WINDOW, width), BF),
            pltpu.VMEM((blocks // 2, MODALITIES, width, 2 * width), BF),
            pltpu.VMEM((rows, 2 * width), F32),
            pltpu.VMEM((blocks, rows, width), BF),
            pltpu.SemaphoreType.DMA((blocks,)),
            pltpu.SemaphoreType.DMA((len(shapes),)),
        ],
        out_shape=tuple(jax.ShapeDtypeStruct(shape, BF) for shape in shapes),
        compiler_params=pltpu.CompilerParams(vmem_limit_bytes=VMEM_BYTES),
        cost_estimate=pl.CostEstimate(flops=0, bytes_accessed=rows, transcendentals=0),
    )(table, seg, own, other, weights)


def add(*arrays):
    return sum(array.astype(F32) for array in arrays).astype(BF)


def local(tokens, modality, w_query, w_key, w_value, w_out):
    seg = segment_scalars(modality)
    core = seg[2 * MODALITIES :]
    weights = (w_key, w_value, w_query)

    before, after = move(tokens, True, 1), move(tokens, True, -1)
    opposite = move(tokens, True, 2)
    plus_first = jnp.stack([tokens, before])
    minus_first = jnp.stack([tokens, after])
    before_first = move(plus_first, False, 1)
    after_first = move(minus_first, False, -1)
    before, after, opposite, _ = lax.optimization_barrier((before, after, opposite, plus_first))
    plus_second = jnp.stack([after, opposite])
    minus_second = jnp.stack([before, opposite])
    before_second = move(plus_second, False, 1)
    after_second = move(minus_second, False, -1)
    names = dict(self=0, before=3, after=1, opposite=2)

    def shards(second, *firsts):
        return [(names[first], second) for first in firsts]

    lists = [
        shards(0, "self", "before", "after", "opposite"),
        shards(3, "self", "before") + shards(1, "self", "after"),
        shards(3, "after", "opposite") + shards(1, "before", "opposite") + shards(2, "after"),
        shards(2, "self", "before", "opposite"),
    ]
    tables = [shard_table(*zip(*chosen)) for chosen in lists]
    partial = project([plus_first, plus_second], weights, tables[0], seg)
    before_first, after_first, partial = lax.optimization_barrier(
        (before_first, after_first, partial)
    )
    far_first = move(before_first, False, 1)
    far_after = move(after_first[1:], False, -1)
    partial = project([before_first, after_first], weights, tables[1], seg, before=partial)
    after_second, partial = lax.optimization_barrier((after_second, partial))
    far_opposite = move(after_second[1:], False, -1)
    partial = project(
        [before_second, after_second, far_after], weights, tables[2], seg, before=partial
    )
    query, kv, query_send, kv_send = project(
        [far_first, far_opposite], weights, tables[3], seg, before=partial, last=True
    )

    kv_other = swap_core(kv_send)
    query_other = swap_core(query_send)
    kv_before = move_x(kv, 1)
    kv_other_after = move_x(kv_other, -1)
    kv_other_before = move_x(kv_other, 1)
    kv_after = move_x(kv, -1)
    chip = lax.axis_index("ctx") // 2
    near_use = jnp.stack([chip >= 1, chip == 3]).astype(jnp.int32)
    far_use = jnp.stack([chip >= 2, chip >= 2]).astype(jnp.int32)
    queries = (query, query_other)
    state = attend_own(*queries, kv, kv_other, core)
    order = [
        [(2, 0), (2, 2), (2, 1), (2, 3)],
        [(1, 1), (1, 3), (3, 0), (3, 2)],
        [(1, 2), (1, 0), (3, 1), (3, 3)],
        [(0, 0), (0, 2), (0, 1), (0, 3)],
    ]
    t_two, t_first, t_later, t_here = (shard_table(*zip(*blocks)) for blocks in order)
    picked = pick_weights(w_out, [t_two, t_first, t_later])
    kv_before, kv_other_after, state, *picked = lax.optimization_barrier(
        (kv_before, kv_other_after, state, *picked)
    )
    w_two, w_first, w_later = picked
    kv_far = move_x(kv_before, 1)
    kv_other_far = move_x(kv_other_after, -1)
    state = attend_other(*queries, state, [kv_before, kv_other_after], near_use)
    state = attend_other(*queries, state, [kv_other_before, kv_after], near_use)
    own, own_send = attend_other(*queries, state, [kv_far, kv_other_far], far_use, last=True)
    other = swap_core(own_send)

    part = functools.partial(output_part, own, other)
    two_low, two_high = part(w_two, t_two, seg, (2, 2))
    two_low = move(two_low, True, 1)
    two_high = move(two_high, True, -1)
    plus_high, minus_low = part(w_first, t_first, seg, (2, 2))
    plus_high = move(plus_high, True, 1)
    minus_low = move(minus_low, True, -1)
    plus_2, plus_0, minus_high = part(w_later, t_later, seg, (0, 0, 2))
    plus_2 = add(plus_2, two_low[1])
    plus_0 = add(plus_0, two_low[0])
    minus_high = add(minus_high, two_high)
    plus_2, plus_0, minus_high, own, other = lax.optimization_barrier(
        (plus_2, plus_0, minus_high, own, other)
    )
    here = output_part(own, other, w_out, t_here, seg, (0, 0, 0, 0))
    plus_2 = move(plus_2, True, 1)
    minus_high = move(minus_high, True, -1)
    plus_0 = move(plus_0, True, 1)
    plus_2, plus_high, minus_low = lax.optimization_barrier((plus_2, plus_high, minus_low))
    sums = [
        add(here[1], plus_2, minus_low[1]),
        add(here[2], plus_high[0], minus_high[0]),
        add(here[3], plus_high[1], minus_high[1]),
    ]
    opposite, after, before = (move(part, False, step) for part, step in zip(sums, (2, 1, -1)))
    plus_0, *_ = lax.optimization_barrier((plus_0, *sums))
    mine = lax.optimization_barrier(add(here[0], plus_0, minus_low[0]))
    return add(tokens, mine, after, opposite, before)


def solution(mesh):
    in_specs = (
        P("ctx", "tp"),
        P("ctx"),
        P(None, None, "tp"),
        P(None, None, "tp"),
        P(None, None, "tp"),
        P(None, "tp", None),
    )
    return jax.shard_map(
        local, mesh=mesh, in_specs=in_specs, out_specs=P("ctx", "tp"), check_vma=False
    )
```

```python
import functools
import math

import jax
import jax.numpy as jnp
import numpy as np
from jax import lax
from jax.experimental import pallas as pl
from jax.experimental.pallas import tpu as pltpu
from jax.sharding import PartitionSpec as P

HD = 128
MODALITIES = 3
EPS = 1e-05
WINDOW = 528
ALIGN = 16
Q_TILE = 512
K_TILE = 1024
STATE_ROWS = HD + 16
AXES = ("ctx", "tp")
BF = jnp.bfloat16
F32 = jnp.float32
VMEM_PROJECT = 50 * 1024 * 1024
VMEM_BYTES = 24 * 1024 * 1024
FEATURES = 4096
SPAN = 256
HEADROOM = 2.0**-13


def plane_perm(first, step):
    pairs = []
    for ctx in range(8):
        for z in range(4):
            for y in range(4):
                along_y = (ctx % 2 == 0) == first
                to_z = z if along_y else (z + step) % 4
                to_y = (y + step) % 4 if along_y else y
                pairs.append((ctx * 16 + z * 4 + y, ctx * 16 + to_z * 4 + to_y))
    return pairs


def move(array, first, step):
    return lax.ppermute(array, AXES, plane_perm(first, step))


def move_x(array, step):
    pairs = [(x * 2 + c, ((x + step) % 4) * 2 + c) for x in range(4) for c in range(2)]
    return lax.ppermute(array, "ctx", pairs)


def swap_core(array):
    return lax.ppermute(array, "ctx", [(i, i ^ 1) for i in range(8)])


def shard_table(first_offsets, second_offsets):
    core = lax.axis_index("ctx") % 2
    tp = lax.axis_index("tp")
    z, y = tp // 4, tp % 4
    first_offsets = jnp.asarray(first_offsets, jnp.int32)
    second_offsets = jnp.asarray(second_offsets, jnp.int32)
    first = (jnp.where(core == 0, y, z) + first_offsets) % 4
    second = (jnp.where(core == 0, z, y) + second_offsets) % 4
    return jnp.where(core == 0, second * 4 + first, first * 4 + second).astype(jnp.int32)


def segment_scalars(modality):
    rows = modality.shape[0]
    kinds = jnp.arange(MODALITIES, dtype=jnp.int32)[:, None]
    member = modality[None, :] == kinds
    positions = jnp.arange(rows, dtype=jnp.int32)[None, :]
    begin = jnp.min(jnp.where(member, positions, rows), axis=1)
    end = jnp.max(jnp.where(member, positions + 1, 0), axis=1)
    end = jnp.maximum(end, begin)
    core = lax.axis_index("ctx") % 2
    return jnp.concatenate([begin, end, core[None]]).astype(jnp.int32)


def for_runs(seg_ref, rows, body):
    for kind in range(MODALITIES):
        begin = seg_ref[kind]
        end = seg_ref[MODALITIES + kind]
        first = jnp.minimum(begin // ALIGN * ALIGN, rows - WINDOW)
        first = pl.multiple_of(first, ALIGN)
        positions = first + lax.broadcasted_iota(jnp.int32, (WINDOW, 1), 0)
        body(kind, pl.ds(first, WINDOW), (positions >= begin) & (positions < end))


def constant_spec(shape):
    return pl.BlockSpec(shape, lambda k, *scalars: (0,) * len(shape))


def project(pieces, weights, table, seg, before=None, last=False):
    count = len(pieces)
    counts = [piece.shape[0] for piece in pieces]
    firsts = [sum(counts[:i]) for i in range(count)]
    depth = sum(counts)
    rows, width = pieces[0].shape[1:]
    out_width = 3 * width
    has_before = before is not None

    def kernel(table_ref, seg_ref, *refs):
        piece_refs = refs[:count]
        weight_refs = refs[count : count + 3]
        refs = refs[count + 3 :]
        if has_before:
            squares_before_ref, before_ref, *refs = refs
        if last:
            query_ref, kv_ref, query_send_ref, kv_send_ref, *refs = refs
        else:
            squares_ref, out_ref, *refs = refs
        held, normed, left, right, total, passed, shrink, piece_sem, weight_sem, total_sem = refs

        spans = [pl.ds(row, SPAN) for row in range(0, rows, SPAN)]
        piece_copies = [
            pltpu.make_async_copy(
                piece_refs[i].at[:, span, :],
                held.at[pl.ds(firsts[i], counts[i]), span, :],
                piece_sem.at[k, i],
            )
            for k, span in enumerate(spans)
            for i in range(count)
        ]
        groups = ((0, 2 * width), (2 * width, out_width))
        weight_copies = ([], [])
        before_copies = ([], [])
        out_copies = []
        for g, (low, high) in enumerate(groups):
            columns = pl.ds(low, high - low)
            for j in range(depth):
                first = pl.multiple_of(table_ref[j] * width, width)
                for i in range(low // width, high // width):
                    weight_copies[g].append(
                        pltpu.make_async_copy(
                            weight_refs[i].at[:, pl.ds(first, width), :],
                            right.at[:, pl.ds(j * width, width), pl.ds(i * width, width)],
                            weight_sem.at[i, j],
                        )
                    )
            for k, span in enumerate(spans):
                if has_before:
                    before_copies[g].append(
                        pltpu.make_async_copy(
                            before_ref.at[span, columns],
                            passed.at[span, columns],
                            total_sem.at[0, g, k],
                        )
                    )
                if not last:
                    out_copies.append(
                        pltpu.make_async_copy(
                            passed.at[span, columns],
                            out_ref.at[span, columns],
                            total_sem.at[1, g, k],
                        )
                    )
        for copy in piece_copies:
            copy.start()
        for g in range(2):
            for copy in weight_copies[g] + before_copies[g]:
                copy.start()

        for row in range(0, rows, HD):
            at = slice(row, row + HD)
            if row % SPAN == 0:
                k = row // SPAN
                for copy in piece_copies[k * count : (k + 1) * count]:
                    copy.wait()
            by_lane = jnp.zeros((HD, HD), F32)
            for j in range(depth):
                for column in range(0, width, HD):
                    by_lane += jnp.square(held[j, at, column : column + HD].astype(F32))
            squares = jnp.sum(by_lane, axis=1, keepdims=True)
            if has_before:
                squares_before = squares_before_ref[at, :]
                scale_before = lax.rsqrt(squares_before / FEATURES + EPS)
                squares += squares_before
            scale = lax.rsqrt(squares / FEATURES + EPS)
            if has_before:
                shrink[at, :] = jnp.where(scale_before > 0.0, scale / scale_before, 0.0)
            if not last:
                squares_ref[at, :] = squares
            for j in range(depth):
                piece = held[j, at, :].astype(F32)
                normed[at, j * width : (j + 1) * width] = (piece * (scale * HEADROOM)).astype(BF)

        def mask(kind, at, keep):
            left[kind] = normed[at, :] * keep.astype(BF)

        for_runs(seg_ref, rows, mask)
        for g, (low, high) in enumerate(groups):
            for copy in weight_copies[g] + before_copies[g]:
                copy.wait()
            if has_before:
                total[:, low:high] = passed[:, low:high].astype(F32) * shrink[...]
            else:
                total[:, low:high] = jnp.zeros((rows, high - low), F32)

            def run(kind, at, keep, low=low, high=high):
                total[at, low:high] += jnp.dot(
                    left[kind], right[kind, :, low:high], preferred_element_type=F32
                )

            for_runs(seg_ref, rows, run)
            if not last:
                passed[:, low:high] = total[:, low:high].astype(BF)
                for copy in out_copies[g * len(spans) : (g + 1) * len(spans)]:
                    copy.start()
        for copy in out_copies:
            copy.wait()

        if last:
            query_scale = math.log2(math.e) / math.sqrt(HD) / HEADROOM
            core = seg_ref[2 * MODALITIES]
            for mine in range(2):

                @pl.when(core == mine)
                def _(mine=mine):
                    for head, q_out, kv_out in (
                        (mine, query_ref, kv_ref),
                        (1 - mine, query_send_ref, kv_send_ref),
                    ):
                        at = head * HD
                        kv_out[:, :HD] = (total[:, at : at + HD] / HEADROOM).astype(BF)
                        at += width
                        for row in range(0, rows, HD):
                            block = total[row : row + HD, at : at + HD] / HEADROOM
                            kv_out[row : row + HD, HD:] = block.T.astype(BF)
                        at += width
                        q_out[...] = (total[:, at : at + HD] * query_scale).astype(BF)

    vmem = pl.BlockSpec(memory_space=pltpu.VMEM)
    operands = [table, seg, *pieces, *weights]
    in_specs = [pl.BlockSpec(memory_space=pltpu.SMEM)] * 2
    in_specs += [pl.BlockSpec(memory_space=pl.ANY)] * count
    in_specs += [pl.BlockSpec(memory_space=pl.ANY)] * 3
    if has_before:
        operands += before
        in_specs += [vmem, pl.BlockSpec(memory_space=pl.ANY)]
    if last:
        shapes = [(rows, HD), (rows, 2 * HD)] * 2
        out_shape = tuple(jax.ShapeDtypeStruct(shape, BF) for shape in shapes)
        out_specs = (vmem,) * 4
    else:
        out_shape = (
            jax.ShapeDtypeStruct((rows, 1), F32),
            jax.ShapeDtypeStruct((rows, out_width), BF),
        )
        out_specs = (vmem, pl.BlockSpec(memory_space=pl.ANY))
    return pl.pallas_call(
        kernel,
        in_specs=in_specs,
        out_specs=out_specs,
        scratch_shapes=[
            pltpu.VMEM((depth, rows, width), BF),
            pltpu.VMEM((rows, depth * width), BF),
            pltpu.VMEM((MODALITIES, WINDOW, depth * width), BF),
            pltpu.VMEM((MODALITIES, depth * width, 3 * width), BF),
            pltpu.VMEM((rows, out_width), F32),
            pltpu.VMEM((rows, out_width), BF),
            pltpu.VMEM((rows, 1), F32),
            pltpu.SemaphoreType.DMA((rows // SPAN, count)),
            pltpu.SemaphoreType.DMA((3, depth)),
            pltpu.SemaphoreType.DMA((2, 2, rows // SPAN)),
        ],
        out_shape=out_shape,
        compiler_params=pltpu.CompilerParams(vmem_limit_bytes=VMEM_PROJECT),
        cost_estimate=pl.CostEstimate(
            flops=2 * depth * 3 * WINDOW * width * 3 * width,
            bytes_accessed=depth * (rows * width * 2 + 9 * width * width * 2),
            transcendentals=0,
        ),
    )(*operands)


def score(query, key, keep=None):
    scores = lax.dot_general(key, query, (((1,), (1,)), ((), ())), preferred_element_type=F32)
    return scores if keep is None else jnp.where(keep, scores, -1e30)


def fold(state, scores, value_t):
    top, total, summed = state
    new_top = jnp.maximum(top, jnp.max(scores, axis=0, keepdims=True))
    factor = jnp.exp2(top - new_top)
    weights = jnp.exp2(scores - new_top)
    total = total * factor + jnp.sum(weights, axis=0, keepdims=True)
    summed = summed * factor + jnp.dot(value_t, weights.astype(BF), preferred_element_type=F32)
    return new_top, total, summed


def empty_state():
    return (
        jnp.full((1, Q_TILE), -1e30, F32),
        jnp.zeros((1, Q_TILE), F32),
        jnp.zeros((HD, Q_TILE), F32),
    )


def store_state(state, state_ref):
    top, total, summed = state
    state_ref[0, :HD, :] = summed
    state_ref[0, HD : HD + 8, :] = jnp.broadcast_to(top, (8, Q_TILE))
    state_ref[0, HD + 8 :, :] = jnp.broadcast_to(total, (8, Q_TILE))


def load_state(state_ref):
    return (
        state_ref[0, HD : HD + 1, :],
        state_ref[0, HD + 8 : HD + 9, :],
        state_ref[0, :HD, :],
    )


def read_keys(ref, first, count):
    key = ref[pl.ds(first, count), :HD]
    blocks = [ref[pl.ds(first + i, HD), HD:] for i in range(0, count, HD)]
    return key, jnp.concatenate(blocks, axis=1)


def attend_own(query, query_other, kv, kv_other, core):
    rows = query.shape[0]
    per_block = rows // Q_TILE
    tiles = 2 * per_block

    def kernel(core_ref, query_ref, query_other_ref, kv_ref, kv_other_ref, state_ref, keys, both):
        place = pl.program_id(0)

        @pl.when(place == 0)
        def _():
            for mine in range(2):

                @pl.when(core_ref[0] == mine)
                def _(mine=mine):
                    at, other = mine * rows, (1 - mine) * rows
                    keys[at : at + rows, :] = kv_ref[...]
                    keys[other : other + rows, :] = kv_other_ref[...]
                    both[at : at + rows, :] = query_ref[...]
                    both[other : other + rows, :] = query_other_ref[...]

        at = pl.multiple_of(place * Q_TILE, Q_TILE)
        q = both[pl.ds(at, Q_TILE), :]
        causal = lax.broadcasted_iota(
            jnp.int32, (Q_TILE, Q_TILE), 0
        ) <= lax.broadcasted_iota(jnp.int32, (Q_TILE, Q_TILE), 1)
        key, value_t = read_keys(keys, at, Q_TILE)
        state = fold(empty_state(), score(q, key, causal), value_t)

        def earlier(tile, state):
            key, value_t = read_keys(keys, pl.multiple_of(tile * Q_TILE, Q_TILE), Q_TILE)
            return fold(state, score(q, key), value_t)

        store_state(lax.fori_loop(0, place, earlier, state), state_ref)

    whole = constant_spec((rows, HD))
    whole_kv = constant_spec((rows, 2 * HD))
    return pl.pallas_call(
        kernel,
        grid_spec=pltpu.PrefetchScalarGridSpec(
            num_scalar_prefetch=1,
            grid=(tiles,),
            in_specs=[whole, whole, whole_kv, whole_kv],
            out_specs=pl.BlockSpec(
                (1, STATE_ROWS, Q_TILE),
                lambda i, core: ((i + core[0] * per_block) % tiles, 0, 0),
            ),
            scratch_shapes=[
                pltpu.VMEM((2 * rows, 2 * HD), BF),
                pltpu.VMEM((2 * rows, HD), BF),
            ],
        ),
        out_shape=jax.ShapeDtypeStruct((tiles, STATE_ROWS, Q_TILE), F32),
        compiler_params=pltpu.CompilerParams(vmem_limit_bytes=VMEM_BYTES),
        cost_estimate=pl.CostEstimate(
            flops=10 * Q_TILE * Q_TILE * HD * 4,
            bytes_accessed=4 << 20,
            transcendentals=10 * Q_TILE * Q_TILE,
        ),
    )(core, query, query_other, kv, kv_other)


def attend_other(query, query_other, state, sources, use, last=False):
    rows = query.shape[0]
    per_block = rows // Q_TILE
    tiles = 2 * per_block
    count = len(sources)

    def kernel(use_ref, query_ref, query_other_ref, before_ref, *refs):
        source_refs = refs[:count]
        *out_refs, after, q_ref = refs[count:]
        tile = pl.program_id(0)

        @pl.when(tile < per_block)
        def _():
            q_ref[...] = query_ref[...]

        @pl.when(tile >= per_block)
        def _():
            q_ref[...] = query_other_ref[...]

        q = q_ref[...]
        after[...] = before_ref[...]

        def fold_in(refs):
            parts = [(ref, at) for ref in refs for at in range(0, rows, K_TILE)]
            state = load_state(after)
            scores = None
            for i, (ref, at) in enumerate(parts):
                key, value_t = read_keys(ref, at, K_TILE)
                if scores is None:
                    scores = score(q, key)
                later = None
                if i + 1 < len(parts):
                    next_ref, next_at = parts[i + 1]
                    later = score(q, next_ref[next_at : next_at + K_TILE, :HD])
                state = fold(state, scores, value_t)
                scores = later
            store_state(state, after)

        all_used = use_ref[0]
        for i in range(1, count):
            all_used = all_used & use_ref[i]

        @pl.when(all_used != 0)
        def _():
            fold_in(source_refs)

        for i, source_ref in enumerate(source_refs):

            @pl.when((all_used == 0) & (use_ref[i] != 0))
            def _(source_ref=source_ref):
                fold_in([source_ref])

        if last:
            _, total, summed = load_state(after)
            attended = (summed / total).T.astype(BF)
            for part, out_ref in enumerate(out_refs):

                @pl.when(tile // per_block == part)
                def _(out_ref=out_ref):
                    at = pl.multiple_of(tile % per_block * Q_TILE, Q_TILE)
                    out_ref[pl.ds(at, Q_TILE), :] = attended

        else:
            out_refs[0][...] = after[...]

    state_spec = pl.BlockSpec((1, STATE_ROWS, Q_TILE), lambda i, use: (i, 0, 0))
    if last:
        out_shape = (jax.ShapeDtypeStruct((rows, HD), BF),) * 2
        out_specs = (constant_spec((rows, HD)),) * 2
    else:
        out_shape = jax.ShapeDtypeStruct((tiles, STATE_ROWS, Q_TILE), F32)
        out_specs = state_spec
    return pl.pallas_call(
        kernel,
        grid_spec=pltpu.PrefetchScalarGridSpec(
            num_scalar_prefetch=1,
            grid=(tiles,),
            in_specs=[
                pl.BlockSpec((Q_TILE, HD), lambda i, use: (jnp.minimum(i, per_block - 1), 0)),
                pl.BlockSpec((Q_TILE, HD), lambda i, use: (jnp.maximum(i - per_block, 0), 0)),
                state_spec,
            ]
            + [constant_spec(source.shape) for source in sources],
            out_specs=out_specs,
            scratch_shapes=[
                pltpu.VMEM((1, STATE_ROWS, Q_TILE), F32),
                pltpu.VMEM((Q_TILE, HD), BF),
            ],
        ),
        out_shape=out_shape,
        compiler_params=pltpu.CompilerParams(vmem_limit_bytes=VMEM_BYTES),
        cost_estimate=pl.CostEstimate(
            flops=2 * rows * count * rows * HD * 4,
            bytes_accessed=6 << 20,
            transcendentals=2 * rows * count * rows,
        ),
    )(use, query, query_other, state, *sources)


def pick_weights(w_out, tables):
    depth, width = w_out.shape[1], 2 * HD
    groups = len(tables)

    def kernel(*refs):
        weight_ref, *out_refs = refs[groups:]
        for i, out_ref in enumerate(out_refs):

            @pl.when(pl.program_id(0) // 4 == i)
            def _(out_ref=out_ref):
                out_ref[0] = weight_ref[...]

    def column(k, *table_refs):
        place = table_refs[0][k % 4]
        for i in range(1, groups):
            place = jnp.where(k // 4 == i, table_refs[i][k % 4], place)
        return (0, 0, place)

    return pl.pallas_call(
        kernel,
        grid_spec=pltpu.PrefetchScalarGridSpec(
            num_scalar_prefetch=groups,
            grid=(4 * groups,),
            in_specs=[pl.BlockSpec((MODALITIES, depth, width), column)],
            out_specs=tuple(
                pl.BlockSpec(
                    (1, MODALITIES, depth, width),
                    lambda k, *t, i=i: (jnp.clip(k - 4 * i, 0, 3), 0, 0, 0),
                )
                for i in range(groups)
            ),
        ),
        out_shape=(jax.ShapeDtypeStruct((4, MODALITIES, depth, width), BF),) * groups,
        compiler_params=pltpu.CompilerParams(vmem_limit_bytes=VMEM_BYTES),
        cost_estimate=pl.CostEstimate(
            flops=0, bytes_accessed=groups * (3 << 20), transcendentals=0
        ),
    )(*tables, w_out)


def output_part(own, other, weights, table, seg, sizes):
    blocks = table.shape[0]
    rows = own.shape[0]
    width = 2 * HD
    picked = weights.ndim == 4

    def kernel(table_ref, seg_ref, own_ref, other_ref, weight_ref, *refs):
        *out_refs, attended, left, right, total, result, weight_sem, out_sem = refs
        weight_copies = []
        for i in range(blocks):
            first = pl.multiple_of(table_ref[i] * width, width)
            weight_copies.append(
                pltpu.make_async_copy(
                    weight_ref.at[i] if picked else weight_ref.at[:, :, pl.ds(first, width)],
                    right.at[i // 2, :, :, pl.ds(i % 2 * width, width)],
                    weight_sem.at[i],
                )
            )
            weight_copies[i].start()
        core = seg_ref[2 * MODALITIES]
        for mine in range(2):

            @pl.when(core == mine)
            def _(mine=mine):
                attended[:, mine * HD : (mine + 1) * HD] = own_ref[...]
                attended[:, (1 - mine) * HD : (2 - mine) * HD] = other_ref[...]

        def mask(kind, at, keep):
            left[kind] = attended[at, :] * keep.astype(BF)

        for_runs(seg_ref, rows, mask)
        out_copies = []
        for pair in range(blocks // 2):
            weight_copies[2 * pair].wait()
            weight_copies[2 * pair + 1].wait()
            total[...] = jnp.zeros_like(total)

            def run(kind, at, keep, pair=pair):
                total[at, :] += jnp.dot(left[kind], right[pair, kind], preferred_element_type=F32)

            for_runs(seg_ref, rows, run)
            for i in range(2):
                result[2 * pair + i] = total[:, i * width : (i + 1) * width].astype(BF)
            done = 0
            for size, out_ref in zip(sizes, out_refs):
                if done // 2 == pair:
                    source = result.at[pl.ds(done, 2)] if size else result.at[done]
                    out_copies.append(
                        pltpu.make_async_copy(source, out_ref, out_sem.at[len(out_copies)])
                    )
                    out_copies[-1].start()
                done += max(size, 1)
        for copy in out_copies:
            copy.wait()

    vmem = pl.BlockSpec(memory_space=pltpu.VMEM)
    shapes = [(size, rows, width) if size else (rows, width) for size in sizes]
    return pl.pallas_call(
        kernel,
        in_specs=[pl.BlockSpec(memory_space=pltpu.SMEM)] * 2
        + [vmem, vmem, pl.BlockSpec(memory_space=pl.ANY)],
        out_specs=(pl.BlockSpec(memory_space=pl.ANY),) * len(shapes),
        scratch_shapes=[
            pltpu.VMEM((rows, width), BF),
            pltpu.VMEM((MODALITIES, WINDOW, width), BF),
            pltpu.VMEM((blocks // 2, MODALITIES, width, 2 * width), BF),
            pltpu.VMEM((rows, 2 * width), F32),
            pltpu.VMEM((blocks, rows, width), BF),
            pltpu.SemaphoreType.DMA((blocks,)),
            pltpu.SemaphoreType.DMA((len(shapes),)),
        ],
        out_shape=tuple(jax.ShapeDtypeStruct(shape, BF) for shape in shapes),
        compiler_params=pltpu.CompilerParams(vmem_limit_bytes=VMEM_BYTES),
        cost_estimate=pl.CostEstimate(flops=0, bytes_accessed=rows, transcendentals=0),
    )(table, seg, own, other, weights)


def add(*arrays):
    return sum(array.astype(F32) for array in arrays).astype(BF)


def local(tokens, modality, w_query, w_key, w_value, w_out):
    seg = segment_scalars(modality)
    core = seg[2 * MODALITIES :]
    weights = (w_key, w_value, w_query)

    before, after = move(tokens, True, 1), move(tokens, True, -1)
    opposite = move(tokens, True, 2)
    plus_first = jnp.stack([tokens, before])
    minus_first = jnp.stack([tokens, after])
    before_first = move(plus_first, False, 1)
    after_first = move(minus_first, False, -1)
    before, after, opposite, _ = lax.optimization_barrier((before, after, opposite, plus_first))
    plus_second = jnp.stack([after, opposite])
    minus_second = jnp.stack([before, opposite])
    before_second = move(plus_second, False, 1)
    after_second = move(minus_second, False, -1)
    names = dict(self=0, before=3, after=1, opposite=2)

    def shards(second, *firsts):
        return [(names[first], second) for first in firsts]

    lists = [
        shards(0, "self", "before", "after", "opposite"),
        shards(3, "self", "before") + shards(1, "self", "after"),
        shards(3, "after", "opposite") + shards(1, "before", "opposite") + shards(2, "after"),
        shards(2, "self", "before", "opposite"),
    ]
    tables = [shard_table(*zip(*chosen)) for chosen in lists]
    partial = project([plus_first, plus_second], weights, tables[0], seg)
    before_first, after_first, partial = lax.optimization_barrier(
        (before_first, after_first, partial)
    )
    far_first = move(before_first, False, 1)
    far_after = move(after_first[1:], False, -1)
    partial = project([before_first, after_first], weights, tables[1], seg, before=partial)
    after_second, partial = lax.optimization_barrier((after_second, partial))
    far_opposite = move(after_second[1:], False, -1)
    partial = project(
        [before_second, after_second, far_after], weights, tables[2], seg, before=partial
    )
    query, kv, query_send, kv_send = project(
        [far_first, far_opposite], weights, tables[3], seg, before=partial, last=True
    )

    kv_other = swap_core(kv_send)
    query_other = swap_core(query_send)
    kv_before = move_x(kv, 1)
    kv_other_after = move_x(kv_other, -1)
    kv_other_before = move_x(kv_other, 1)
    kv_after = move_x(kv, -1)
    chip = lax.axis_index("ctx") // 2
    near_use = jnp.stack([chip >= 1, chip == 3]).astype(jnp.int32)
    far_use = jnp.stack([chip >= 2, chip >= 2]).astype(jnp.int32)
    queries = (query, query_other)
    state = attend_own(*queries, kv, kv_other, core)
    order = [
        [(2, 0), (2, 2), (2, 1), (2, 3)],
        [(1, 1), (1, 3), (3, 0), (3, 2)],
        [(1, 2), (1, 0), (3, 1), (3, 3)],
        [(0, 0), (0, 2), (0, 1), (0, 3)],
    ]
    t_two, t_first, t_later, t_here = (shard_table(*zip(*blocks)) for blocks in order)
    picked = pick_weights(w_out, [t_two, t_first, t_later])
    kv_before, kv_other_after, state, *picked = lax.optimization_barrier(
        (kv_before, kv_other_after, state, *picked)
    )
    w_two, w_first, w_later = picked
    kv_far = move_x(kv_before, 1)
    kv_other_far = move_x(kv_other_after, -1)
    state = attend_other(*queries, state, [kv_before, kv_other_after], near_use)
    state = attend_other(*queries, state, [kv_other_before, kv_after], near_use)
    own, own_send = attend_other(*queries, state, [kv_far, kv_other_far], far_use, last=True)
    other = swap_core(own_send)

    part = functools.partial(output_part, own, other)
    two_low, two_high = part(w_two, t_two, seg, (2, 2))
    two_low = move(two_low, True, 1)
    two_high = move(two_high, True, -1)
    plus_high, minus_low = part(w_first, t_first, seg, (2, 2))
    plus_high = move(plus_high, True, 1)
    minus_low = move(minus_low, True, -1)
    plus_2, plus_0, minus_high = part(w_later, t_later, seg, (0, 0, 2))
    plus_2 = add(plus_2, two_low[1])
    plus_0 = add(plus_0, two_low[0])
    minus_high = add(minus_high, two_high)
    plus_2, plus_0, minus_high, own, other = lax.optimization_barrier(
        (plus_2, plus_0, minus_high, own, other)
    )
    here = output_part(own, other, w_out, t_here, seg, (0, 0, 0, 0))
    plus_2 = move(plus_2, True, 1)
    minus_high = move(minus_high, True, -1)
    plus_0 = move(plus_0, True, 1)
    plus_2, plus_high, minus_low = lax.optimization_barrier((plus_2, plus_high, minus_low))
    sums = [
        add(here[1], plus_2, minus_low[1]),
        add(here[2], plus_high[0], minus_high[0]),
        add(here[3], plus_high[1], minus_high[1]),
    ]
    opposite, after, before = (move(part, False, step) for part, step in zip(sums, (2, 1, -1)))
    plus_0, *_ = lax.optimization_barrier((plus_0, *sums))
    mine = lax.optimization_barrier(add(here[0], plus_0, minus_low[0]))
    return add(tokens, mine, after, opposite, before)


def solution(mesh):
    in_specs = (
        P("ctx", "tp"),
        P("ctx"),
        P(None, None, "tp"),
        P(None, None, "tp"),
        P(None, None, "tp"),
        P(None, "tp", None),
    )
    return jax.shard_map(
        local, mesh=mesh, in_specs=in_specs, out_specs=P("ctx", "tp"), check_vma=False
    )
```

```python
import functools
import math

import jax
import jax.numpy as jnp
import numpy as np
from jax import lax
from jax.experimental import pallas as pl
from jax.experimental.pallas import tpu as pltpu
from jax.sharding import PartitionSpec as P

HD = 128
MODALITIES = 3
EPS = 1e-05
WINDOW = 528
ALIGN = 16
Q_TILE = 1024
K_TILE = 1024
STATE_ROWS = HD + 16
AXES = ("ctx", "tp")
BF = jnp.bfloat16
F32 = jnp.float32
VMEM_PROJECT = 50 * 1024 * 1024
VMEM_BYTES = 24 * 1024 * 1024
FEATURES = 4096
SPAN = 256
HEADROOM = 2.0**-13


def plane_perm(first, step):
    pairs = []
    for ctx in range(8):
        for z in range(4):
            for y in range(4):
                along_y = (ctx % 2 == 0) == first
                to_z = z if along_y else (z + step) % 4
                to_y = (y + step) % 4 if along_y else y
                pairs.append((ctx * 16 + z * 4 + y, ctx * 16 + to_z * 4 + to_y))
    return pairs


def move(array, first, step):
    return lax.ppermute(array, AXES, plane_perm(first, step))


def move_x(array, step):
    pairs = [(x * 2 + c, ((x + step) % 4) * 2 + c) for x in range(4) for c in range(2)]
    return lax.ppermute(array, "ctx", pairs)


def swap_core(array):
    return lax.ppermute(array, "ctx", [(i, i ^ 1) for i in range(8)])


def shard_table(first_offsets, second_offsets):
    core = lax.axis_index("ctx") % 2
    tp = lax.axis_index("tp")
    z, y = tp // 4, tp % 4
    first_offsets = jnp.asarray(first_offsets, jnp.int32)
    second_offsets = jnp.asarray(second_offsets, jnp.int32)
    first = (jnp.where(core == 0, y, z) + first_offsets) % 4
    second = (jnp.where(core == 0, z, y) + second_offsets) % 4
    return jnp.where(core == 0, second * 4 + first, first * 4 + second).astype(jnp.int32)


def segment_scalars(modality):
    rows = modality.shape[0]
    kinds = jnp.arange(MODALITIES, dtype=jnp.int32)[:, None]
    member = modality[None, :] == kinds
    positions = jnp.arange(rows, dtype=jnp.int32)[None, :]
    begin = jnp.min(jnp.where(member, positions, rows), axis=1)
    end = jnp.max(jnp.where(member, positions + 1, 0), axis=1)
    end = jnp.maximum(end, begin)
    core = lax.axis_index("ctx") % 2
    return jnp.concatenate([begin, end, core[None]]).astype(jnp.int32)


def for_runs(seg_ref, rows, body):
    for kind in range(MODALITIES):
        begin = seg_ref[kind]
        end = seg_ref[MODALITIES + kind]
        first = jnp.minimum(begin // ALIGN * ALIGN, rows - WINDOW)
        first = pl.multiple_of(first, ALIGN)
        positions = first + lax.broadcasted_iota(jnp.int32, (WINDOW, 1), 0)
        body(kind, pl.ds(first, WINDOW), (positions >= begin) & (positions < end))


def constant_spec(shape):
    return pl.BlockSpec(shape, lambda k, *scalars: (0,) * len(shape))


def project(pieces, weights, table, seg, before=None, last=False):
    count = len(pieces)
    counts = [piece.shape[0] for piece in pieces]
    firsts = [sum(counts[:i]) for i in range(count)]
    depth = sum(counts)
    rows, width = pieces[0].shape[1:]
    out_width = 3 * width
    has_before = before is not None

    def kernel(table_ref, seg_ref, *refs):
        piece_refs = refs[:count]
        weight_refs = refs[count : count + 3]
        refs = refs[count + 3 :]
        if has_before:
            squares_before_ref, before_ref, *refs = refs
        if last:
            query_ref, kv_ref, query_send_ref, kv_send_ref, *refs = refs
        else:
            squares_ref, out_ref, *refs = refs
        held, normed, left, right, total, passed, shrink, piece_sem, weight_sem, total_sem = refs

        spans = [pl.ds(row, SPAN) for row in range(0, rows, SPAN)]
        piece_copies = [
            pltpu.make_async_copy(
                piece_refs[i].at[:, span, :],
                held.at[pl.ds(firsts[i], counts[i]), span, :],
                piece_sem.at[k, i],
            )
            for k, span in enumerate(spans)
            for i in range(count)
        ]
        groups = ((0, 2 * width), (2 * width, out_width))
        weight_copies = ([], [])
        before_copies = ([], [])
        out_copies = []
        for g, (low, high) in enumerate(groups):
            columns = pl.ds(low, high - low)
            for j in range(depth):
                first = pl.multiple_of(table_ref[j] * width, width)
                for i in range(low // width, high // width):
                    weight_copies[g].append(
                        pltpu.make_async_copy(
                            weight_refs[i].at[:, pl.ds(first, width), :],
                            right.at[:, pl.ds(j * width, width), pl.ds(i * width, width)],
                            weight_sem.at[i, j],
                        )
                    )
            for k, span in enumerate(spans):
                if has_before:
                    before_copies[g].append(
                        pltpu.make_async_copy(
                            before_ref.at[span, columns],
                            passed.at[span, columns],
                            total_sem.at[0, g, k],
                        )
                    )
                if not last:
                    out_copies.append(
                        pltpu.make_async_copy(
                            passed.at[span, columns],
                            out_ref.at[span, columns],
                            total_sem.at[1, g, k],
                        )
                    )
        for copy in piece_copies:
            copy.start()
        for g in range(2):
            for copy in weight_copies[g] + before_copies[g]:
                copy.start()

        for row in range(0, rows, HD):
            at = slice(row, row + HD)
            if row % SPAN == 0:
                k = row // SPAN
                for copy in piece_copies[k * count : (k + 1) * count]:
                    copy.wait()
            by_lane = jnp.zeros((HD, HD), F32)
            for j in range(depth):
                for column in range(0, width, HD):
                    by_lane += jnp.square(held[j, at, column : column + HD].astype(F32))
            squares = jnp.sum(by_lane, axis=1, keepdims=True)
            if has_before:
                squares_before = squares_before_ref[at, :]
                scale_before = lax.rsqrt(squares_before / FEATURES + EPS)
                squares += squares_before
            scale = lax.rsqrt(squares / FEATURES + EPS)
            if has_before:
                shrink[at, :] = jnp.where(scale_before > 0.0, scale / scale_before, 0.0)
            if not last:
                squares_ref[at, :] = squares
            for j in range(depth):
                piece = held[j, at, :].astype(F32)
                normed[at, j * width : (j + 1) * width] = (piece * (scale * HEADROOM)).astype(BF)

        def mask(kind, at, keep):
            left[kind] = normed[at, :] * keep.astype(BF)

        for g, (low, high) in enumerate(groups):
            for copy in weight_copies[g] + before_copies[g]:
                copy.wait()
            if has_before:
                total[:, low:high] = passed[:, low:high].astype(F32) * shrink[...]
            else:
                total[:, low:high] = jnp.zeros((rows, high - low), F32)

            def run(kind, at, keep, g=g, low=low, high=high):
                if g == 0:
                    mask(kind, at, keep)
                total[at, low:high] += jnp.dot(
                    left[kind], right[kind, :, low:high], preferred_element_type=F32
                )

            for_runs(seg_ref, rows, run)
            if not last:
                passed[:, low:high] = total[:, low:high].astype(BF)
                for copy in out_copies[g * len(spans) : (g + 1) * len(spans)]:
                    copy.start()
        for copy in out_copies:
            copy.wait()

        if last:
            query_scale = math.log2(math.e) / math.sqrt(HD) / HEADROOM
            core = seg_ref[2 * MODALITIES]
            for mine in range(2):

                @pl.when(core == mine)
                def _(mine=mine):
                    for head, q_out, kv_out in (
                        (mine, query_ref, kv_ref),
                        (1 - mine, query_send_ref, kv_send_ref),
                    ):
                        at = head * HD
                        kv_out[:, :HD] = (total[:, at : at + HD] / HEADROOM).astype(BF)
                        at += width
                        for row in range(0, rows, HD):
                            block = total[row : row + HD, at : at + HD] / HEADROOM
                            kv_out[row : row + HD, HD:] = block.T.astype(BF)
                        at += width
                        q_out[...] = (total[:, at : at + HD] * query_scale).astype(BF)

    vmem = pl.BlockSpec(memory_space=pltpu.VMEM)
    operands = [table, seg, *pieces, *weights]
    in_specs = [pl.BlockSpec(memory_space=pltpu.SMEM)] * 2
    in_specs += [pl.BlockSpec(memory_space=pl.ANY)] * count
    in_specs += [pl.BlockSpec(memory_space=pl.ANY)] * 3
    if has_before:
        operands += before
        in_specs += [vmem, pl.BlockSpec(memory_space=pl.ANY)]
    if last:
        shapes = [(rows, HD), (rows, 2 * HD)] * 2
        out_shape = tuple(jax.ShapeDtypeStruct(shape, BF) for shape in shapes)
        out_specs = (vmem,) * 4
    else:
        out_shape = (
            jax.ShapeDtypeStruct((rows, 1), F32),
            jax.ShapeDtypeStruct((rows, out_width), BF),
        )
        out_specs = (vmem, pl.BlockSpec(memory_space=pl.ANY))
    return pl.pallas_call(
        kernel,
        in_specs=in_specs,
        out_specs=out_specs,
        scratch_shapes=[
            pltpu.VMEM((depth, rows, width), BF),
            pltpu.VMEM((rows, depth * width), BF),
            pltpu.VMEM((MODALITIES, WINDOW, depth * width), BF),
            pltpu.VMEM((MODALITIES, depth * width, 3 * width), BF),
            pltpu.VMEM((rows, out_width), F32),
            pltpu.VMEM((rows, out_width), BF),
            pltpu.VMEM((rows, 1), F32),
            pltpu.SemaphoreType.DMA((rows // SPAN, count)),
            pltpu.SemaphoreType.DMA((3, depth)),
            pltpu.SemaphoreType.DMA((2, 2, rows // SPAN)),
        ],
        out_shape=out_shape,
        compiler_params=pltpu.CompilerParams(vmem_limit_bytes=VMEM_PROJECT),
        cost_estimate=pl.CostEstimate(
            flops=2 * depth * 3 * WINDOW * width * 3 * width,
            bytes_accessed=depth * (rows * width * 2 + 9 * width * width * 2),
            transcendentals=0,
        ),
    )(*operands)


def score(query, key, keep=None):
    scores = lax.dot_general(key, query, (((1,), (1,)), ((), ())), preferred_element_type=F32)
    return scores if keep is None else jnp.where(keep, scores, -1e30)


def fold(state, scores, value_t):
    top, total, summed = state
    new_top = jnp.maximum(top, jnp.max(scores, axis=0, keepdims=True))
    factor = jnp.exp2(top - new_top)
    weights = jnp.exp2(scores - new_top)
    total = total * factor + jnp.sum(weights, axis=0, keepdims=True)
    summed = summed * factor + jnp.dot(value_t, weights.astype(BF), preferred_element_type=F32)
    return new_top, total, summed


def empty_state():
    return (
        jnp.full((1, Q_TILE), -1e30, F32),
        jnp.zeros((1, Q_TILE), F32),
        jnp.zeros((HD, Q_TILE), F32),
    )


def store_state(state, state_ref):
    top, total, summed = state
    state_ref[0, :HD, :] = summed
    state_ref[0, HD : HD + 8, :] = jnp.broadcast_to(top, (8, Q_TILE))
    state_ref[0, HD + 8 :, :] = jnp.broadcast_to(total, (8, Q_TILE))


def load_state(state_ref):
    return (
        state_ref[0, HD : HD + 1, :],
        state_ref[0, HD + 8 : HD + 9, :],
        state_ref[0, :HD, :],
    )


def read_keys(ref, first, count):
    key = ref[pl.ds(first, count), :HD]
    blocks = [ref[pl.ds(first + i, HD), HD:] for i in range(0, count, HD)]
    return key, jnp.concatenate(blocks, axis=1)


def attend_own(query, query_other, kv, kv_other, core):
    rows = query.shape[0]
    per_block = rows // Q_TILE
    tiles = 2 * per_block

    def kernel(core_ref, query_ref, query_other_ref, kv_ref, kv_other_ref, state_ref, keys, both):
        place = pl.program_id(0)

        @pl.when(place == 0)
        def _():
            for mine in range(2):

                @pl.when(core_ref[0] == mine)
                def _(mine=mine):
                    at, other = mine * rows, (1 - mine) * rows
                    keys[at : at + rows, :] = kv_ref[...]
                    keys[other : other + rows, :] = kv_other_ref[...]
                    both[at : at + rows, :] = query_ref[...]
                    both[other : other + rows, :] = query_other_ref[...]

        at = pl.multiple_of(place * Q_TILE, Q_TILE)
        q = both[pl.ds(at, Q_TILE), :]
        causal = lax.broadcasted_iota(
            jnp.int32, (Q_TILE, Q_TILE), 0
        ) <= lax.broadcasted_iota(jnp.int32, (Q_TILE, Q_TILE), 1)
        key, value_t = read_keys(keys, at, Q_TILE)
        state = fold(empty_state(), score(q, key, causal), value_t)

        def earlier(tile, state):
            key, value_t = read_keys(keys, pl.multiple_of(tile * Q_TILE, Q_TILE), Q_TILE)
            return fold(state, score(q, key), value_t)

        store_state(lax.fori_loop(0, place, earlier, state), state_ref)

    whole = constant_spec((rows, HD))
    whole_kv = constant_spec((rows, 2 * HD))
    return pl.pallas_call(
        kernel,
        grid_spec=pltpu.PrefetchScalarGridSpec(
            num_scalar_prefetch=1,
            grid=(tiles,),
            in_specs=[whole, whole, whole_kv, whole_kv],
            out_specs=pl.BlockSpec(
                (1, STATE_ROWS, Q_TILE),
                lambda i, core: ((i + core[0] * per_block) % tiles, 0, 0),
            ),
            scratch_shapes=[
                pltpu.VMEM((2 * rows, 2 * HD), BF),
                pltpu.VMEM((2 * rows, HD), BF),
            ],
        ),
        out_shape=jax.ShapeDtypeStruct((tiles, STATE_ROWS, Q_TILE), F32),
        compiler_params=pltpu.CompilerParams(vmem_limit_bytes=VMEM_BYTES),
        cost_estimate=pl.CostEstimate(
            flops=10 * Q_TILE * Q_TILE * HD * 4,
            bytes_accessed=4 << 20,
            transcendentals=10 * Q_TILE * Q_TILE,
        ),
    )(core, query, query_other, kv, kv_other)


def attend_other(query, query_other, state, sources, use, last=False):
    rows = query.shape[0]
    per_block = rows // Q_TILE
    tiles = 2 * per_block
    count = len(sources)

    def kernel(use_ref, query_ref, query_other_ref, before_ref, *refs):
        source_refs = refs[:count]
        *out_refs, after, q_ref = refs[count:]
        tile = pl.program_id(0)

        @pl.when(tile < per_block)
        def _():
            q_ref[...] = query_ref[...]

        @pl.when(tile >= per_block)
        def _():
            q_ref[...] = query_other_ref[...]

        q = q_ref[...]
        after[...] = before_ref[...]

        def fold_in(refs):
            parts = [(ref, at) for ref in refs for at in range(0, rows, K_TILE)]
            state = load_state(after)
            scores = None
            for i, (ref, at) in enumerate(parts):
                key, value_t = read_keys(ref, at, K_TILE)
                if scores is None:
                    scores = score(q, key)
                later = None
                if i + 1 < len(parts):
                    next_ref, next_at = parts[i + 1]
                    later = score(q, next_ref[next_at : next_at + K_TILE, :HD])
                state = fold(state, scores, value_t)
                scores = later
            store_state(state, after)

        all_used = use_ref[0]
        for i in range(1, count):
            all_used = all_used & use_ref[i]

        @pl.when(all_used != 0)
        def _():
            fold_in(source_refs)

        for i, source_ref in enumerate(source_refs):

            @pl.when((all_used == 0) & (use_ref[i] != 0))
            def _(source_ref=source_ref):
                fold_in([source_ref])

        if last:
            _, total, summed = load_state(after)
            attended = (summed / total).T.astype(BF)
            for part, out_ref in enumerate(out_refs):

                @pl.when(tile // per_block == part)
                def _(out_ref=out_ref):
                    at = pl.multiple_of(tile % per_block * Q_TILE, Q_TILE)
                    out_ref[pl.ds(at, Q_TILE), :] = attended

        else:
            out_refs[0][...] = after[...]

    state_spec = pl.BlockSpec((1, STATE_ROWS, Q_TILE), lambda i, use: (i, 0, 0))
    if last:
        out_shape = (jax.ShapeDtypeStruct((rows, HD), BF),) * 2
        out_specs = (constant_spec((rows, HD)),) * 2
    else:
        out_shape = jax.ShapeDtypeStruct((tiles, STATE_ROWS, Q_TILE), F32)
        out_specs = state_spec
    return pl.pallas_call(
        kernel,
        grid_spec=pltpu.PrefetchScalarGridSpec(
            num_scalar_prefetch=1,
            grid=(tiles,),
            in_specs=[
                pl.BlockSpec((Q_TILE, HD), lambda i, use: (jnp.minimum(i, per_block - 1), 0)),
                pl.BlockSpec((Q_TILE, HD), lambda i, use: (jnp.maximum(i - per_block, 0), 0)),
                state_spec,
            ]
            + [constant_spec(source.shape) for source in sources],
            out_specs=out_specs,
            scratch_shapes=[
                pltpu.VMEM((1, STATE_ROWS, Q_TILE), F32),
                pltpu.VMEM((Q_TILE, HD), BF),
            ],
        ),
        out_shape=out_shape,
        compiler_params=pltpu.CompilerParams(vmem_limit_bytes=VMEM_BYTES),
        cost_estimate=pl.CostEstimate(
            flops=2 * rows * count * rows * HD * 4,
            bytes_accessed=6 << 20,
            transcendentals=2 * rows * count * rows,
        ),
    )(use, query, query_other, state, *sources)


def pick_weights(w_out, tables):
    depth, width = w_out.shape[1], 2 * HD
    groups = len(tables)

    def kernel(*refs):
        weight_ref, *out_refs = refs[groups:]
        for i, out_ref in enumerate(out_refs):

            @pl.when(pl.program_id(0) // 4 == i)
            def _(out_ref=out_ref):
                out_ref[0] = weight_ref[...]

    def column(k, *table_refs):
        place = table_refs[0][k % 4]
        for i in range(1, groups):
            place = jnp.where(k // 4 == i, table_refs[i][k % 4], place)
        return (0, 0, place)

    return pl.pallas_call(
        kernel,
        grid_spec=pltpu.PrefetchScalarGridSpec(
            num_scalar_prefetch=groups,
            grid=(4 * groups,),
            in_specs=[pl.BlockSpec((MODALITIES, depth, width), column)],
            out_specs=tuple(
                pl.BlockSpec(
                    (1, MODALITIES, depth, width),
                    lambda k, *t, i=i: (jnp.clip(k - 4 * i, 0, 3), 0, 0, 0),
                )
                for i in range(groups)
            ),
        ),
        out_shape=(jax.ShapeDtypeStruct((4, MODALITIES, depth, width), BF),) * groups,
        compiler_params=pltpu.CompilerParams(vmem_limit_bytes=VMEM_BYTES),
        cost_estimate=pl.CostEstimate(
            flops=0, bytes_accessed=groups * (3 << 20), transcendentals=0
        ),
    )(*tables, w_out)


def output_part(own, other, weights, table, seg, sizes):
    blocks = table.shape[0]
    rows = own.shape[0]
    width = 2 * HD
    picked = weights.ndim == 4

    def kernel(table_ref, seg_ref, own_ref, other_ref, weight_ref, *refs):
        *out_refs, attended, left, right, total, result, weight_sem, out_sem = refs
        weight_copies = []
        for i in range(blocks):
            first = pl.multiple_of(table_ref[i] * width, width)
            weight_copies.append(
                pltpu.make_async_copy(
                    weight_ref.at[i] if picked else weight_ref.at[:, :, pl.ds(first, width)],
                    right.at[i // 2, :, :, pl.ds(i % 2 * width, width)],
                    weight_sem.at[i],
                )
            )
            weight_copies[i].start()
        core = seg_ref[2 * MODALITIES]
        for mine in range(2):

            @pl.when(core == mine)
            def _(mine=mine):
                attended[:, mine * HD : (mine + 1) * HD] = own_ref[...]
                attended[:, (1 - mine) * HD : (2 - mine) * HD] = other_ref[...]

        def mask(kind, at, keep):
            left[kind] = attended[at, :] * keep.astype(BF)

        for_runs(seg_ref, rows, mask)
        out_copies = []
        for pair in range(blocks // 2):
            weight_copies[2 * pair].wait()
            weight_copies[2 * pair + 1].wait()
            total[...] = jnp.zeros_like(total)

            def run(kind, at, keep, pair=pair):
                total[at, :] += jnp.dot(left[kind], right[pair, kind], preferred_element_type=F32)

            for_runs(seg_ref, rows, run)
            for i in range(2):
                result[2 * pair + i] = total[:, i * width : (i + 1) * width].astype(BF)
            done = 0
            for size, out_ref in zip(sizes, out_refs):
                if done // 2 == pair:
                    source = result.at[pl.ds(done, 2)] if size else result.at[done]
                    out_copies.append(
                        pltpu.make_async_copy(source, out_ref, out_sem.at[len(out_copies)])
                    )
                    out_copies[-1].start()
                done += max(size, 1)
        for copy in out_copies:
            copy.wait()

    vmem = pl.BlockSpec(memory_space=pltpu.VMEM)
    shapes = [(size, rows, width) if size else (rows, width) for size in sizes]
    return pl.pallas_call(
        kernel,
        in_specs=[pl.BlockSpec(memory_space=pltpu.SMEM)] * 2
        + [vmem, vmem, pl.BlockSpec(memory_space=pl.ANY)],
        out_specs=(pl.BlockSpec(memory_space=pl.ANY),) * len(shapes),
        scratch_shapes=[
            pltpu.VMEM((rows, width), BF),
            pltpu.VMEM((MODALITIES, WINDOW, width), BF),
            pltpu.VMEM((blocks // 2, MODALITIES, width, 2 * width), BF),
            pltpu.VMEM((rows, 2 * width), F32),
            pltpu.VMEM((blocks, rows, width), BF),
            pltpu.SemaphoreType.DMA((blocks,)),
            pltpu.SemaphoreType.DMA((len(shapes),)),
        ],
        out_shape=tuple(jax.ShapeDtypeStruct(shape, BF) for shape in shapes),
        compiler_params=pltpu.CompilerParams(vmem_limit_bytes=VMEM_BYTES),
        cost_estimate=pl.CostEstimate(flops=0, bytes_accessed=rows, transcendentals=0),
    )(table, seg, own, other, weights)


def add(*arrays):
    return sum(array.astype(F32) for array in arrays).astype(BF)


def local(tokens, modality, w_query, w_key, w_value, w_out):
    seg = segment_scalars(modality)
    core = seg[2 * MODALITIES :]
    weights = (w_key, w_value, w_query)

    before, after = move(tokens, True, 1), move(tokens, True, -1)
    opposite = move(tokens, True, 2)
    plus_first = jnp.stack([tokens, before])
    minus_first = jnp.stack([tokens, after])
    before_first = move(plus_first, False, 1)
    after_first = move(minus_first, False, -1)
    before, after, opposite, _ = lax.optimization_barrier((before, after, opposite, plus_first))
    plus_second = jnp.stack([after, opposite])
    minus_second = jnp.stack([before, opposite])
    before_second = move(plus_second, False, 1)
    after_second = move(minus_second, False, -1)
    names = dict(self=0, before=3, after=1, opposite=2)

    def shards(second, *firsts):
        return [(names[first], second) for first in firsts]

    lists = [
        shards(0, "self", "before", "after", "opposite"),
        shards(3, "self", "before") + shards(1, "self", "after"),
        shards(3, "after", "opposite") + shards(1, "before", "opposite") + shards(2, "after"),
        shards(2, "self", "before", "opposite"),
    ]
    tables = [shard_table(*zip(*chosen)) for chosen in lists]
    partial = project([plus_first, plus_second], weights, tables[0], seg)
    before_first, after_first, partial = lax.optimization_barrier(
        (before_first, after_first, partial)
    )
    far_first = move(before_first, False, 1)
    far_after = move(after_first[1:], False, -1)
    partial = project([before_first, after_first], weights, tables[1], seg, before=partial)
    after_second, partial = lax.optimization_barrier((after_second, partial))
    far_opposite = move(after_second[1:], False, -1)
    partial = project(
        [before_second, after_second, far_after], weights, tables[2], seg, before=partial
    )
    query, kv, query_send, kv_send = project(
        [far_first, far_opposite], weights, tables[3], seg, before=partial, last=True
    )

    kv_other = swap_core(kv_send)
    query_other = swap_core(query_send)
    kv_before = move_x(kv, 1)
    kv_other_after = move_x(kv_other, -1)
    kv_other_before = move_x(kv_other, 1)
    kv_after = move_x(kv, -1)
    chip = lax.axis_index("ctx") // 2
    near_use = jnp.stack([chip >= 1, chip == 3]).astype(jnp.int32)
    far_use = jnp.stack([chip >= 2, chip >= 2]).astype(jnp.int32)
    queries = (query, query_other)
    state = attend_own(*queries, kv, kv_other, core)
    order = [
        [(2, 0), (2, 2), (2, 1), (2, 3)],
        [(1, 1), (1, 3), (3, 0), (3, 2)],
        [(1, 2), (1, 0), (3, 1), (3, 3)],
        [(0, 0), (0, 2), (0, 1), (0, 3)],
    ]
    t_two, t_first, t_later, t_here = (shard_table(*zip(*blocks)) for blocks in order)
    picked = pick_weights(w_out, [t_two, t_first, t_later])
    kv_before, kv_other_after, state, *picked = lax.optimization_barrier(
        (kv_before, kv_other_after, state, *picked)
    )
    w_two, w_first, w_later = picked
    kv_far = move_x(kv_before, 1)
    kv_other_far = move_x(kv_other_after, -1)
    state = attend_other(*queries, state, [kv_before, kv_other_after], near_use)
    state = attend_other(*queries, state, [kv_other_before, kv_after], near_use)
    own, own_send = attend_other(*queries, state, [kv_far, kv_other_far], far_use, last=True)
    other = swap_core(own_send)

    part = functools.partial(output_part, own, other)
    two_low, two_high = part(w_two, t_two, seg, (2, 2))
    two_low = move(two_low, True, 1)
    two_high = move(two_high, True, -1)
    plus_high, minus_low = part(w_first, t_first, seg, (2, 2))
    plus_high = move(plus_high, True, 1)
    minus_low = move(minus_low, True, -1)
    plus_2, plus_0, minus_high = part(w_later, t_later, seg, (0, 0, 2))
    plus_2 = add(plus_2, two_low[1])
    plus_0 = add(plus_0, two_low[0])
    minus_high = add(minus_high, two_high)
    plus_2, plus_0, minus_high, own, other = lax.optimization_barrier(
        (plus_2, plus_0, minus_high, own, other)
    )
    here = output_part(own, other, w_out, t_here, seg, (0, 0, 0, 0))
    plus_2 = move(plus_2, True, 1)
    minus_high = move(minus_high, True, -1)
    plus_0 = move(plus_0, True, 1)
    plus_2, plus_high, minus_low = lax.optimization_barrier((plus_2, plus_high, minus_low))
    sums = [
        add(here[1], plus_2, minus_low[1]),
        add(here[2], plus_high[0], minus_high[0]),
        add(here[3], plus_high[1], minus_high[1]),
    ]
    opposite, after, before = (move(part, False, step) for part, step in zip(sums, (2, 1, -1)))
    plus_0, *_ = lax.optimization_barrier((plus_0, *sums))
    mine = lax.optimization_barrier(add(here[0], plus_0, minus_low[0]))
    return add(tokens, mine, after, opposite, before)


def solution(mesh):
    in_specs = (
        P("ctx", "tp"),
        P("ctx"),
        P(None, None, "tp"),
        P(None, None, "tp"),
        P(None, None, "tp"),
        P(None, "tp", None),
    )
    return jax.shard_map(
        local, mesh=mesh, in_specs=in_specs, out_specs=P("ctx", "tp"), check_vma=False
    )
```
